128 devices in a mesh: dp: 8 (over y, core), ctx: 16 (over z, x).
Axes of the slice: x: 4, y: 4, z: 4, core: 2. Of those that a mesh axis runs over, the one named last changes fastest.
Arguments:
- block_in: bfloat16 [16, 2048, 1024], P('dp', 'ctx'), may hold values from -6 to 6
- segment_ids: int32 [16, 2048], P('dp'), may hold values from -1 to 34, as said below
- attn_gain: float32 [1024], replicated, may hold values from 0.1 to 1.9
- w_query: bfloat16 [1024, 1024], P(('dp', 'ctx')), may hold values from -0.1875 to 0.1875
- w_key: bfloat16 [1024, 512], P(('dp', 'ctx')), may hold values from -0.1875 to 0.1875
- w_value: bfloat16 [1024, 512], P(('dp', 'ctx')), may hold values from -0.1875 to 0.1875
- query_gain: float32 [64], replicated, may hold values from 0.1 to 1.9
- key_gain: float32 [64], replicated, may hold values from 0.1 to 1.9
- w_out: bfloat16 [1024, 1024], P(('dp', 'ctx')), may hold values from -2 to 2
- ffn_gain: float32 [1024], replicated, may hold values from 0.1 to 1.9
- w_gate: bfloat16 [1024, 4608], P(('dp', 'ctx')), may hold values from -0.1875 to 0.1875
- w_up: bfloat16 [1024, 4608], P(('dp', 'ctx')), may hold values from -0.1875 to 0.1875
- w_down: bfloat16 [4608, 1024], P(('dp', 'ctx')), may hold values from -0.09375 to 0.09375
- out_grad: bfloat16 [16, 2048, 1024], P('dp', 'ctx'), may hold values from -6 to 6
Outputs:
- block_out: bfloat16 [16, 2048, 1024], P('dp', 'ctx')
- block_in_grad: bfloat16 [16, 2048, 1024], P('dp', 'ctx')
- grad_query: float32 [1024, 1024], P(('dp', 'ctx'))
- grad_key: float32 [1024, 512], P(('dp', 'ctx'))
- grad_value: float32 [1024, 512], P(('dp', 'ctx'))
- grad_out: float32 [1024, 1024], P(('dp', 'ctx'))
- grad_gate: float32 [1024, 4608], P(('dp', 'ctx'))
- grad_up: float32 [1024, 4608], P(('dp', 'ctx'))
- grad_down: float32 [4608, 1024], P(('dp', 'ctx'))
- grad_attn_gain: float32 [1024], replicated
- grad_query_gain: float32 [64], replicated
- grad_key_gain: float32 [64], replicated
- grad_ffn_gain: float32 [1024], replicated
The draws below stay inside these ranges and needn't reach their ends.
Inputs may be any that keep to these rules, and one draw needn't show every extreme that they name: `segment_ids`: each sequence ends in 1 to 64 padding tokens of id -1. In each group of 2 sequences of one index of dp, one sequence holds a first document numbered 0 of fewer than 128 tokens and a second one numbered 2048 // 60 up to the padding; the others hold documents of 60 to 800 tokens numbered 0, 1, 2 and so on, the last one cut short by the padding.
All inputs are finite; a program needn't handle non-finite values.
Results may differ from the reference program's by a relative error of at most 0.018.
Values may be sent and summed in bfloat16 or wider, within the bound.
A program may use at most 256 MiB of HBM per device.

```python
import jax
import jax.numpy as jnp
from jax import lax

D = 1024
H = 16
KVH = 8
HDIM = 64
FF = 4608
SEQ_LEN = 2048
DOC_LO = 60
DOC_HI = 800
PAD_MOST = 64
SEQ_DEV = 2
HD = 1024
KVD = 512
SEQS = 16
SPAN = 128


def draw_segment_ids(key, part):
    key = jax.random.fold_in(key, 11)
    key_len, key_pad, key_split, key_pick = jax.random.split(key, 4)
    doc_slots = SEQ_LEN // DOC_LO + 1
    lengths = jax.random.randint(key_len, (SEQS, doc_slots), DOC_LO, DOC_HI + 1)
    doc_ends = jnp.cumsum(lengths, axis=1)
    places = jnp.arange(SEQ_LEN, dtype=jnp.int32)
    packed = jnp.sum((doc_ends[:, None, :] <= places[None, :, None]).astype(jnp.int32), axis=2)
    split_at = jax.random.randint(key_split, (SEQS, 1), 1, SPAN)
    single = jnp.where(places[None, :] >= split_at, SEQ_LEN // DOC_LO, 0).astype(jnp.int32)
    picked = jax.random.randint(key_pick, (SEQS // SEQ_DEV, 1), 0, SEQ_DEV)
    chosen = (jnp.arange(SEQS, dtype=jnp.int32) % SEQ_DEV)[:, None] == jnp.repeat(picked, SEQ_DEV, axis=0)
    combined = jnp.where(chosen, single, packed)
    pad_count = jax.random.randint(key_pad, (SEQS, 1), 1, PAD_MOST + 1)
    return jnp.where(places[None, :] >= SEQ_LEN - pad_count, -1, combined).astype(jnp.int32)


def shard_levels(key, shape, pieces, least, top_value):
    factor_of, own = 1.0, jax.random.fold_in(key, 6)
    for dim, blocks in pieces:
        steps = jnp.exp(jax.random.uniform(jax.random.fold_in(own, dim), (blocks,), jnp.float32, least / len(pieces), top_value / len(pieces)))
        factor_of = factor_of * jnp.repeat(steps, shape[dim] // blocks).reshape([-1 if axis == dim else 1 for axis in range(len(shape))])
    return factor_of


def bell_draw(stream_key, shape, scale, reach, pieces=(), kind=jnp.bfloat16):
    drawn = jax.random.normal(stream_key, shape, jnp.float32) * scale
    if len(pieces) > 0:
        drawn = shard_levels(stream_key, shape, pieces, -0.22, 0.18) * drawn
    return jnp.clip(drawn, min=-reach, max=reach).astype(kind)


def setup_inputs(seed: int = 0) -> dict:
    seeds = jax.random.split(jax.random.key(seed), 15)
    block_in = bell_draw(seeds[0], (SEQS, SEQ_LEN, D), 1.0, 6.0, ((0, 8), (1, 16)))
    segment_ids = draw_segment_ids(jax.random.fold_in(seeds[14], 71), 0)
    attn_gain = jnp.clip(1.0 + 0.18 * jax.random.normal(seeds[2], (D,), jnp.float32), 0.1, 1.9)
    w_query = bell_draw(seeds[3], (D, HD), D ** -0.5, 0.1875, ((0, 128),))
    w_key = bell_draw(seeds[4], (D, KVD), D ** -0.5, 0.1875, ((0, 128),))
    w_value = bell_draw(seeds[5], (D, KVD), D ** -0.5, 0.1875, ((0, 128),))
    query_gain = jnp.clip(1.0 + 0.18 * jax.random.normal(seeds[6], (HDIM,), jnp.float32), 0.1, 1.9)
    key_gain = jnp.clip(1.0 + 0.18 * jax.random.normal(seeds[7], (HDIM,), jnp.float32), 0.1, 1.9)
    w_out = bell_draw(seeds[8], (HD, D), (HD // 128) ** -0.5, 2.0, ((0, 128),))
    ffn_gain = jnp.clip(1.0 + 0.18 * jax.random.normal(seeds[9], (D,), jnp.float32), 0.1, 1.9)
    w_gate = bell_draw(seeds[10], (D, FF), D ** -0.5, 0.1875, ((0, 128),))
    w_up = bell_draw(seeds[11], (D, FF), D ** -0.5, 0.1875, ((0, 128),))
    w_down = bell_draw(seeds[12], (FF, D), FF ** -0.5, 0.09375, ((0, 128),))
    out_grad = bell_draw(seeds[13], (SEQS, SEQ_LEN, D), 1.0, 6.0, ((0, 8), (1, 16)))
    return {"block_in": block_in, "segment_ids": segment_ids, "attn_gain": attn_gain, "w_query": w_query, "w_key": w_key, "w_value": w_value, "query_gain": query_gain, "key_gain": key_gain, "w_out": w_out, "ffn_gain": ffn_gain, "w_gate": w_gate, "w_up": w_up, "w_down": w_down, "out_grad": out_grad}


EPSILON = 1e-05
THETA_BASE = 1000000.0

@jax.custom_vjp
def low(v):
    return lax.optimization_barrier(v.astype(jnp.bfloat16)).astype(jnp.float32)

@jax.custom_vjp
def low_back(v):
    return v

def low_keep(v):
    return (low(v), None)

def low_pass(kept, grad):
    return (grad,)

def back_keep(v):
    return (v, None)

def back_low(kept, grad):
    return (low(grad),)
low.defvjp(low_keep, low_pass)
low_back.defvjp(back_keep, back_low)

def product(left, right):
    return jnp.dot(left, right, precision=lax.Precision.HIGHEST, preferred_element_type=jnp.float32)

def rms_scale(inputs, gain_vec):
    factor = lax.rsqrt(lax.optimization_barrier(jnp.mean(inputs * inputs, axis=-1, keepdims=True)) + EPSILON)
    return inputs * factor * gain_vec

def rope_tables(places):
    frequency = THETA_BASE ** (-jnp.arange(0, HDIM, 2, dtype=jnp.float32) / HDIM)
    angles = places.astype(jnp.float32)[:, None] * frequency[None, :]
    cosine = jnp.concatenate([jnp.cos(angles), jnp.cos(angles)], axis=-1)
    sine_rows = jnp.concatenate([jnp.sin(angles), jnp.sin(angles)], axis=-1)
    return (cosine, sine_rows)

def rotate(inputs, cosine, sine_rows):
    half_dim = inputs.shape[-1] // 2
    turned = jnp.concatenate([-inputs[..., half_dim:], inputs[..., :half_dim]], axis=-1)
    return inputs * cosine + turned * sine_rows

def sequence_forward(tokens, seg_row, attn_gain, w_query, w_key, w_value, query_gain, key_gain, w_out, ffn_gain, w_gate, w_up, w_down):
    length = tokens.shape[0]
    group_size = H // KVH
    places = jnp.arange(length, dtype=jnp.int32)
    cosine, sine_rows = rope_tables(places)
    cosine = cosine[:, None, :]
    sine_rows = sine_rows[:, None, :]
    normed_in = low(rms_scale(tokens, attn_gain))
    query_raw = low_back(product(normed_in, w_query)).reshape(length, H, HDIM)
    key_raw = low_back(product(normed_in, w_key)).reshape(length, KVH, HDIM)
    value_heads = low_back(low(product(normed_in, w_value))).reshape(length, KVH, HDIM)
    query_rot = low_back(low(rotate(rms_scale(query_raw, query_gain), cosine, sine_rows)))
    key_rot = low_back(low(rotate(rms_scale(key_raw, key_gain), cosine, sine_rows)))
    query_grouped = query_rot.reshape(length, KVH, group_size, HDIM)
    scores = low_back(jnp.einsum('qkgd,tkd->kgqt', query_grouped, key_rot, precision=lax.Precision.HIGHEST) * HDIM ** (-0.5))
    allowed = (seg_row[:, None] == seg_row[None, :]) & (places[:, None] >= places[None, :])
    weights = jax.nn.softmax(jnp.where(allowed, scores, -1e+30), axis=-1)
    mixed_out = jnp.einsum('kgqt,tkd->qkgd', low(weights), value_heads, precision=lax.Precision.HIGHEST)
    attended = low_back(low(mixed_out.reshape(length, H * HDIM)))
    residual = tokens + low_back(product(attended, w_out))
    normed_mid = low(rms_scale(residual, ffn_gain))
    gate_val = low_back(product(normed_mid, w_gate))
    up_val = low_back(product(normed_mid, w_up))
    hidden = low(jax.nn.silu(gate_val) * up_val)
    return residual + low_back(product(hidden, w_down))

def reference(block_in, segment_ids, attn_gain, w_query, w_key, w_value, query_gain, key_gain, w_out, ffn_gain, w_gate, w_up, w_down, out_grad):
    parameters = tuple((element.astype(jnp.float32) for element in (attn_gain, w_query, w_key, w_value, query_gain, key_gain, w_out, ffn_gain, w_gate, w_up, w_down)))

    def one_sequence(totals, sequence_set):
        tokens, seg_row, cotangent = sequence_set

        def forward(inputs, *weight_set):
            return sequence_forward(inputs, seg_row, *weight_set)
        output, pull_back = jax.vjp(forward, tokens.astype(jnp.float32), *parameters)
        gradients = pull_back(cotangent.astype(jnp.float32))
        updated = tuple((summed + latest for summed, latest in zip(totals, gradients[1:])))
        return (updated, (output.astype(jnp.bfloat16), gradients[0].astype(jnp.bfloat16)))
    zero_sums = tuple((jnp.zeros_like(element) for element in parameters))
    totals, (outputs, input_grads) = lax.scan(one_sequence, zero_sums, (block_in, segment_ids, out_grad))
    grad_attn, grad_query, grad_key, grad_value, grad_qgain, grad_kgain, grad_out, grad_ffn, grad_gate, grad_up, grad_down = totals
    return (outputs, input_grads, grad_query, grad_key, grad_value, grad_out, grad_gate, grad_up, grad_down, grad_attn, grad_qgain, grad_kgain, grad_ffn)
```

```python
import functools

import jax
import jax.numpy as jnp
from jax import lax
from jax.experimental import pallas as pl
from jax.experimental.pallas import tpu as pltpu
from jax.sharding import PartitionSpec as P

MESH = pl.DeviceIdType.MESH
BF = jnp.bfloat16
F32 = jnp.float32

D = 1024
HDIM = 64
HEADS = 8
ROWS = 256
SEQ = 2048
PADDED = 40
HALF = 64 * PADDED
EPSILON = 1e-05
THETA_BASE = 1000000.0
LOG2E = 1.4426950408889634
VMEM_MOST = 60 * 1024 * 1024


def params(**more):
    return pltpu.CompilerParams(vmem_limit_bytes=VMEM_MOST, **more)


def vmem():
    return pl.BlockSpec(memory_space=pltpu.VMEM)


def hbm():
    return pl.BlockSpec(memory_space=pl.ANY)


def dot(left, right):
    return lax.dot_general(left, right, (((1,), (0,)), ((), ())), preferred_element_type=F32)


def dot_rows(left, right):
    return lax.dot_general(left, right, (((0,), (0,)), ((), ())), preferred_element_type=F32)


def dot_cols(left, right):
    return lax.dot_general(left, right, (((1,), (1,)), ((), ())), preferred_element_type=F32)


def place():
    dp, ctx = lax.axis_index("dp"), lax.axis_index("ctx")
    return {"y": dp // 2, "c": dp % 2, "z": ctx // 4, "x": ctx % 4}


def device(at, **moved):
    spot = dict(at)
    spot.update(moved)
    return (spot["y"] * 2 + spot["c"], spot["z"] * 4 + spot["x"])


def beside(at, dim, by):
    return device(at, **{dim: (at[dim] + by) % 4})


def greet(at, dims="xyz", core=True):
    barrier = pltpu.get_barrier_semaphore()
    count = 0
    for dim in dims:
        for by in (1, 3):
            pl.semaphore_signal(barrier, inc=1, device_id=beside(at, dim, by), device_id_type=MESH)
            count += 1
    if core:
        pl.semaphore_signal(barrier, inc=1, device_id=device(at, c=1 - at["c"]), device_id_type=MESH)
        count += 1
    pl.semaphore_wait(barrier, count)


ORDERS = (("x", "z", "y"), ("y", "x", "z"), ("z", "y", "x"))


class Layout:
    def __init__(self, kind, order, columns):
        self.kind, self.order, self.columns = kind, order, columns

    def index(self, at, full, fixed=None, half=None):
        spot = dict(at)
        if fixed:
            spot.update(fixed)
        ids = {d: (slice(None) if d in full else spot[d]) for d in "xyz"}
        c = {"own": at["c"], "both": slice(None), "none": None}[self.kind]
        out = [ids["y"]] + ([] if c is None else [c]) + [ids["z"], ids["x"], slice(None)]
        if half is None:
            out.append(slice(None))
        else:
            out.append(pl.ds(half * (self.columns // 2), self.columns // 2))
        return tuple(out)


def gather_kernel(q_in, kv_in, o_in, g_in, u_in, d_in, q_out, kv_out, o_out, g_out, u_out, d_out, local_sem, core_send, core_recv, send, recv):
    at = place()
    c = at["c"]
    partner = device(at, c=1 - c)
    greet(at)
    layouts = [
        Layout("own", ORDERS[0], 1024), Layout("own", ORDERS[1], 1024), Layout("own", ORDERS[2], 1024),
        Layout("both", ORDERS[0], HALF), Layout("both", ORDERS[1], HALF), Layout("none", ORDERS[2], 1024),
    ]
    outs = [q_out, kv_out, o_out, g_out, u_out, d_out]
    here = (at["y"], c, at["z"], at["x"])
    down_here = (at["y"], at["z"], at["x"])

    core = []
    for i, (src, dst) in enumerate(((g_in, g_out), (u_in, u_out))):
        core.append(pltpu.make_async_remote_copy(
            src_ref=src.at[1 - c], dst_ref=dst.at[here], send_sem=core_send.at[i], recv_sem=core_recv.at[i],
            device_id=partner, device_id_type=MESH))
    for copy in core:
        copy.start()
    locals_ = [
        pltpu.make_async_copy(q_in, q_out.at[here], local_sem.at[0]),
        pltpu.make_async_copy(kv_in, kv_out.at[here], local_sem.at[1]),
        pltpu.make_async_copy(o_in, o_out.at[here], local_sem.at[2]),
        pltpu.make_async_copy(g_in.at[c], g_out.at[here], local_sem.at[3]),
        pltpu.make_async_copy(u_in.at[c], u_out.at[here], local_sem.at[4]),
        pltpu.make_async_copy(d_in, d_out.at[down_here], local_sem.at[5]),
    ]
    for copy in locals_:
        copy.start()
    for copy in locals_:
        copy.wait()

    sends = []

    def remote(i, stage, slot, index, to):
        copy = pltpu.make_async_remote_copy(
            src_ref=outs[i].at[index], dst_ref=outs[i].at[index], send_sem=send.at[i, stage, slot],
            recv_sem=recv.at[i, stage, slot], device_id=to, device_id_type=MESH)
        copy.start()
        sends.append(copy)

    def first(i, stage):
        lay = layouts[i]
        dim, full = lay.order[stage], lay.order[:stage]
        index = lay.index(at, full)
        remote(i, stage, 0, index, beside(at, dim, 1))
        remote(i, stage, 1, index, beside(at, dim, 3))

    def arrived(i, stage, slot, by, half):
        lay = layouts[i]
        dim, full = lay.order[stage], lay.order[:stage]
        index = lay.index(at, full, {dim: (at[dim] + by) % 4}, half)
        pltpu.make_async_remote_copy(
            src_ref=outs[i].at[index], dst_ref=outs[i].at[index], send_sem=send.at[i, stage, slot],
            recv_sem=recv.at[i, stage, slot], device_id=partner, device_id_type=MESH).wait_recv()

    def second(i, stage):
        lay = layouts[i]
        dim, full = lay.order[stage], lay.order[:stage]
        arrived(i, stage, 0, 3, None)
        remote(i, stage, 2, lay.index(at, full, {dim: (at[dim] + 3) % 4}, 0), beside(at, dim, 1))
        arrived(i, stage, 1, 1, None)
        remote(i, stage, 3, lay.index(at, full, {dim: (at[dim] + 1) % 4}, 1), beside(at, dim, 3))

    def last(i, stage):
        arrived(i, stage, 2, 2, 0)
        arrived(i, stage, 3, 2, 1)

    for i in range(3):
        first(i, 0)
    for copy in core:
        copy.wait_recv()
    for i in range(3, 6):
        first(i, 0)
    swaps = []
    for stage in range(3):
        for i in range(6):
            second(i, stage)
        for i in range(6):
            last(i, stage)
            if stage < 2:
                first(i, stage + 1)
            elif i < 3:
                index = (slice(None), c)
                copy = pltpu.make_async_remote_copy(
                    src_ref=outs[i].at[index], dst_ref=outs[i].at[index], send_sem=core_send.at[2 + i],
                    recv_sem=core_recv.at[2 + i], device_id=partner, device_id_type=MESH)
                copy.start()
                swaps.append(copy)
    for copy in core:
        copy.wait_send()
    for i in range(3):
        index = (slice(None), 1 - c)
        pltpu.make_async_remote_copy(
            src_ref=outs[i].at[index], dst_ref=outs[i].at[index], send_sem=core_send.at[2 + i],
            recv_sem=core_recv.at[2 + i], device_id=partner, device_id_type=MESH).wait_recv()
    for copy in swaps:
        copy.wait_send()
    for copy in sends:
        copy.wait_send()


def gather(*shards):
    attn = jax.ShapeDtypeStruct((4, 2, 4, 4, 8, D), BF)
    wide = jax.ShapeDtypeStruct((4, 2, 4, 4, 8, HALF), BF)
    down = jax.ShapeDtypeStruct((4, 4, 4, PADDED, D), BF)
    dma = pltpu.SemaphoreType.DMA
    return pl.pallas_call(
        gather_kernel,
        out_shape=(attn, attn, attn, wide, wide, down),
        in_specs=[hbm()] * 6,
        out_specs=[hbm()] * 6,
        scratch_shapes=[dma((6,)), dma((5,)), dma((5,)), dma((6, 3, 4)), dma((6, 3, 4))],
        compiler_params=params(collective_id=0, has_side_effects=True),
    )(*shards)


def scatter_kernel(*refs):
    grads, gains_in = refs[:6], refs[6]
    q_fin, kv_fin, o_fin, g_fin, u_fin, d_fin, gains_out = refs[7:14]
    fins = [q_fin, kv_fin, o_fin, g_fin, u_fin, d_fin]
    core_bufs = refs[14:17]
    recvs = [refs[17 + 6 * i : 23 + 6 * i] for i in range(6)]
    gain_bufs = refs[53]
    wide_fin = refs[54:56]
    core_send, core_recv, send, recv, fin_send, fin_recv, gain_send, gain_recv = refs[56:64]
    at = place()
    c = at["c"]
    partner = device(at, c=1 - c)
    greet(at)
    layouts = [
        Layout("own", ORDERS[0], 1024), Layout("own", ORDERS[1], 1024), Layout("own", ORDERS[2], 1024),
        Layout("both", ORDERS[0], HALF), Layout("both", ORDERS[1], HALF), Layout("none", ORDERS[2], 1024),
    ]
    waits = []

    for i in range(3):
        copy = pltpu.make_async_remote_copy(
            src_ref=grads[i].at[:, 1 - c], dst_ref=core_bufs[i], send_sem=core_send.at[i], recv_sem=core_recv.at[i],
            device_id=partner, device_id_type=MESH)
        copy.start()
        waits.append(copy)

    def remote(src, dst, i, stage, slot, to):
        copy = pltpu.make_async_remote_copy(
            src_ref=src, dst_ref=dst, send_sem=send.at[i, stage, slot], recv_sem=recv.at[i, stage, slot],
            device_id=to, device_id_type=MESH)
        copy.start()
        waits.append(copy)

    def arrived(dst, i, stage, slot):
        pltpu.make_async_remote_copy(
            src_ref=dst, dst_ref=dst, send_sem=send.at[i, stage, slot], recv_sem=recv.at[i, stage, slot],
            device_id=partner, device_id_type=MESH).wait_recv()

    def bufs(i, stage):
        lay = layouts[i]
        half = lay.columns // 2
        both = recvs[i][2 * stage]
        near = recvs[i][2 * stage + 1]
        return both.at[0], both.at[1], near.at[0], near.at[1], half

    def chunk(i, stage, by, half=None):
        lay = layouts[i]
        dim, full = lay.order[stage], lay.order[stage + 1 :]
        return lay.index(at, full, {dim: (at[dim] + by) % 4}, half)

    def first(i, stage):
        dim = layouts[i].order[stage]
        h0, h1, _, _, _ = bufs(i, stage)
        remote(grads[i].at[chunk(i, stage, 2, 0)], h0, i, stage, 0, beside(at, dim, 1))
        remote(grads[i].at[chunk(i, stage, 2, 1)], h1, i, stage, 1, beside(at, dim, 3))

    def add(target, others, lead):
        def body(ids):
            spot = tuple(ids)
            total = target[spot].astype(F32)
            for other in others:
                total = total + other[spot].astype(F32)
            target[spot] = total.astype(target.dtype)
        loop(lead, body)

    def loop(lead, body):
        count = 1
        for n in lead:
            count *= n
        if count == 1:
            body([0] * len(lead))
            return

        @pl.loop(0, count)
        def _(flat):
            ids = []
            for n in reversed(lead):
                ids.insert(0, flat % n)
                flat = flat // n
            body(ids)

    def leads(ref):
        return ref.shape[:-2]

    def second(i, stage):
        dim = layouts[i].order[stage]
        h0, h1, left, right, half = bufs(i, stage)
        arrived(h0, i, stage, 0)
        target = grads[i].at[chunk(i, stage, 1, 0)]
        add(target, [h0], leads(h0))
        remote(grads[i].at[chunk(i, stage, 1)], left, i, stage, 2, beside(at, dim, 1))
        arrived(h1, i, stage, 1)
        target = grads[i].at[chunk(i, stage, 3, 1)]
        add(target, [h1], leads(h1))
        remote(grads[i].at[chunk(i, stage, 3)], right, i, stage, 3, beside(at, dim, 3))

    def last(i, stage):
        _, _, left, right, _ = bufs(i, stage)
        arrived(left, i, stage, 2)
        arrived(right, i, stage, 3)
        target = grads[i].at[chunk(i, stage, 0)]
        if stage < 2:
            add(target, [left, right], leads(left))
            return
        fin = fins[i] if i not in (3, 4) else wide_fin[i - 3]

        def body(ids):
            spot = tuple(ids)
            fin[spot] = target[spot].astype(F32) + left[spot].astype(F32) + right[spot].astype(F32)
        loop(leads(left), body)

    order = (3, 4, 5, 0, 1, 2)
    for i in (3, 4, 5):
        first(i, 0)
    for i in range(3):
        waits[i].wait_recv()
        add(grads[i].at[:, c], [core_bufs[i]], leads(core_bufs[i]))
        first(i, 0)

    def gain_stage(stage, dim):
        slots = gain_bufs.at[stage]
        p = at[dim]

        def move(slot, by, index):
            copy = pltpu.make_async_remote_copy(
                src_ref=slots.at[index], dst_ref=slots.at[index], send_sem=gain_send.at[stage, slot],
                recv_sem=gain_recv.at[stage, slot], device_id=beside(at, dim, by), device_id_type=MESH)
            copy.start()
            waits.append(copy)

        def here(slot, index):
            pltpu.make_async_remote_copy(
                src_ref=slots.at[index], dst_ref=slots.at[index], send_sem=gain_send.at[stage, slot],
                recv_sem=gain_recv.at[stage, slot], device_id=partner, device_id_type=MESH).wait_recv()

        move(0, 1, p)
        move(1, 3, p)
        here(0, (p + 3) % 4)
        move(2, 1, (p + 3) % 4)
        here(1, (p + 1) % 4)
        here(2, (p + 2) % 4)
        return slots[0] + slots[1] + slots[2] + slots[3]

    gain_bufs[0, at["x"]] = gains_in[...]
    total = None
    for stage in range(3):
        if stage > 0:
            gain_bufs[stage, at["xyz"[stage]]] = total
        total = gain_stage(stage, "xyz"[stage])
        for i in order:
            second(i, stage)
        for i in order:
            last(i, stage)
            if stage < 2:
                first(i, stage + 1)
    gain_bufs[3, c] = total
    spot = gain_bufs.at[3, c]
    copy = pltpu.make_async_remote_copy(
        src_ref=spot, dst_ref=spot, send_sem=gain_send.at[3, 0], recv_sem=gain_recv.at[3, 0], device_id=partner,
        device_id_type=MESH)
    copy.start()
    swaps = []
    for k in range(2):
        swap = pltpu.make_async_remote_copy(
            src_ref=wide_fin[k].at[1 - c], dst_ref=fins[3 + k].at[c], send_sem=fin_send.at[k], recv_sem=fin_recv.at[k],
            device_id=partner, device_id_type=MESH)
        swap.start()
        swaps.append(swap)
        fins[3 + k][c] = wide_fin[k][c]
    copy.wait()
    gains_out[...] = gain_bufs[3, 0] + gain_bufs[3, 1]
    for k in range(2):
        swaps[k].wait_send()
        pltpu.make_async_remote_copy(
            src_ref=fins[3 + k].at[1 - c], dst_ref=fins[3 + k].at[1 - c], send_sem=fin_send.at[k], recv_sem=fin_recv.at[k],
            device_id=partner, device_id_type=MESH).wait_recv()
    for copy in waits:
        copy.wait_send()


def chunk_shapes(kind, order, rows, columns):
    shapes = []
    for stage in range(3):
        left = order[stage + 1 :]
        lead = ([4] if "y" in left else []) + ([2] if kind == "both" else [])
        lead += [4] if "z" in left else []
        lead += [4] if "x" in left else []
        shapes.append(tuple(lead))
    out = []
    for lead in shapes:
        out.append(pltpu.VMEM((2, *lead, rows, columns // 2), BF))
        out.append(pltpu.VMEM((2, *lead, rows, columns), BF))
    return out


def scatter(q, kv, o, g, u, d, gains):
    small = jax.ShapeDtypeStruct((8, D), F32)
    wide = jax.ShapeDtypeStruct((2, 8, HALF), F32)
    down = jax.ShapeDtypeStruct((PADDED, D), F32)
    dma = pltpu.SemaphoreType.DMA
    scratch = [pltpu.VMEM((4, 4, 4, 8, D), BF)] * 3
    for order in ORDERS:
        scratch += chunk_shapes("own", order, 8, D)
    scratch += chunk_shapes("both", ORDERS[0], 8, HALF)
    scratch += chunk_shapes("both", ORDERS[1], 8, HALF)
    scratch += chunk_shapes("none", ORDERS[2], PADDED, D)
    scratch += [pltpu.VMEM((4, 4, *gains.shape), F32)]
    scratch += [pltpu.VMEM((2, 8, HALF), F32)] * 2
    scratch += [dma((3,)), dma((3,)), dma((6, 3, 4)), dma((6, 3, 4)), dma((2,)), dma((2,)), dma((4, 3)), dma((4, 3))]
    return pl.pallas_call(
        scatter_kernel,
        out_shape=(small, small, small, wide, wide, down, jax.ShapeDtypeStruct(gains.shape, F32)),
        in_specs=[vmem()] * 7,
        out_specs=[vmem()] * 7,
        scratch_shapes=scratch,
        compiler_params=params(collective_id=1, has_side_effects=True),
    )(q, kv, o, g, u, d, gains)


def swap_kernel(count, *refs):
    ins, outs = refs[:count], refs[count : 2 * count]
    send, recv, local = refs[2 * count :]
    dp, ctx = lax.axis_index("dp"), lax.axis_index("ctx")
    barrier = pltpu.get_barrier_semaphore()
    for step in range(1, 16):
        pl.semaphore_signal(barrier, inc=1, device_id=(dp, (ctx + step) % 16), device_id_type=MESH)
    copies = []
    for k in range(count):
        copy = pltpu.make_async_copy(ins[k].at[ctx], outs[k].at[ctx], local.at[k])
        copy.start()
        copies.append(copy)
    pl.semaphore_wait(barrier, 15)
    for step in range(1, 16):
        to = (ctx + step) % 16
        for k in range(count):
            copy = pltpu.make_async_remote_copy(
                src_ref=ins[k].at[to], dst_ref=outs[k].at[ctx], send_sem=send.at[k, step], recv_sem=recv.at[k, step],
                device_id=(dp, to), device_id_type=MESH)
            copy.start()
            copies.append(copy)
    for copy in copies:
        copy.wait()


def swap(name, *arrays):
    count = len(arrays)
    dma = pltpu.SemaphoreType.DMA
    shape = jax.ShapeDtypeStruct((16, 128, 128), BF)
    return pl.pallas_call(
        functools.partial(swap_kernel, count),
        out_shape=(shape,) * count,
        in_specs=[hbm()] * count,
        out_specs=[hbm()] * count,
        scratch_shapes=[dma((count, 16)), dma((count, 16)), dma((count,))],
        compiler_params=params(collective_id=name, has_side_effects=True),
    )(*arrays)


def lanes(shape):
    return lax.broadcasted_iota(jnp.int32, shape, len(shape) - 1)


def norm(values, gain):
    factor = lax.rsqrt(jnp.mean(values * values, axis=-1, keepdims=True) + EPSILON)
    unit = values * factor
    return unit * gain, unit, factor


def split_dot(values, matrix):
    high = values.astype(BF)
    low = (values - high.astype(F32)).astype(BF)
    return dot(high, matrix) + dot(low, matrix)


def head_sum_matrix():
    rows = lax.broadcasted_iota(jnp.int32, (128, 128), 0) // HDIM
    return (rows == lanes((128, 128)) // HDIM).astype(BF)


def turn(values):
    low = lanes(values.shape) % HDIM < HDIM // 2
    ahead = pltpu.roll(values, 128 - HDIM // 2, 1)
    behind = pltpu.roll(values, HDIM // 2, 1)
    return jnp.where(low, -ahead, behind)


def project_kernel(x_ref, gain_ref, qgain_ref, kgain_ref, cos_ref, sin_ref, wq_ref, wkv_ref, h_ref, qraw_ref, kraw_ref, q_ref, kv_ref, low_ref):
    step = pl.program_id(0)

    @pl.when(step == 0)
    def _():
        normed, _, _ = norm(x_ref[...].astype(F32), gain_ref[...])
        low_ref[...] = normed.astype(BF)
        h_ref[...] = normed.astype(BF)

    low = low_ref[...]
    sums = head_sum_matrix()
    query = dot(low, wq_ref[...])
    key_value = dot(low, wkv_ref[...])
    qraw_ref[...] = query
    kraw_ref[...] = key_value
    cosine, sine = cos_ref[...], sin_ref[...]
    for h in range(2):
        def rotated(raw, gain):
            factor = lax.rsqrt(split_dot(raw * raw, sums) * (1.0 / HDIM) + EPSILON)
            normed = raw * factor * gain
            return normed * cosine + turn(normed) * sine
        raw = query[:, h * 128 : (h + 1) * 128]
        out = rotated(raw, qgain_ref[...]).astype(BF)
        raw = key_value[:, h * 128 : (h + 1) * 128]
        pair = jnp.where(lanes(raw.shape) < HDIM, rotated(raw, kgain_ref[...]), raw).astype(BF)
        for s in range(2):
            q_ref[s, h] = out[s * 128 : (s + 1) * 128]
            kv_ref[s, h] = pair[s * 128 : (s + 1) * 128]


def project(x, gain, qgain, kgain, cosine, sine, wq, wkv):
    full = lambda shape: pl.BlockSpec(shape, lambda i: (0,) * len(shape))
    wide = pl.BlockSpec((D, 256), lambda i: (0, i))
    raw = pl.BlockSpec((ROWS, 256), lambda i: (0, i))
    heads = pl.BlockSpec((2, 2, 128, 128), lambda i: (0, i, 0, 0))
    return pl.pallas_call(
        project_kernel,
        grid=(4,),
        out_shape=(
            jax.ShapeDtypeStruct((ROWS, D), BF), jax.ShapeDtypeStruct((ROWS, D), F32), jax.ShapeDtypeStruct((ROWS, D), F32),
            jax.ShapeDtypeStruct((2, 8, 128, 128), BF), jax.ShapeDtypeStruct((2, 8, 128, 128), BF),
        ),
        in_specs=[full((ROWS, D)), full((1, D)), full((1, 128)), full((1, 128)), full((ROWS, 128)), full((ROWS, 128)), wide, wide],
        out_specs=[full((ROWS, D)), raw, raw, heads, heads],
        scratch_shapes=[pltpu.VMEM((ROWS, D), BF)],
        compiler_params=params(),
    )(x, gain, qgain, kgain, cosine, sine, wq, wkv)


BLOCK = 256
SCALE2 = LOG2E * HDIM**-0.5


def attend_kernel(q_ref, kv_ref, segcol_ref, segrow_ref, o_ref, inv_ref):
    block = pl.program_id(0)
    low_lane = lanes((BLOCK, 128)) < HDIM
    q = q_ref[...]
    zero = jnp.zeros_like(q)
    stacked = jnp.concatenate([jnp.where(low_lane, q, zero), jnp.where(low_lane, pltpu.roll(q.astype(F32), HDIM, 1).astype(BF), zero)], axis=0)
    seg_q = segcol_ref[...]
    seg_q = jnp.concatenate([seg_q, seg_q], axis=0)

    def part(j, total, diagonal):
        rows = pl.ds(pl.multiple_of(j * BLOCK, BLOCK), BLOCK)
        kv = kv_ref[rows, :]
        scores = dot_cols(stacked, kv)
        allowed = seg_q == segrow_ref[:, rows]
        if diagonal:
            query = lax.broadcasted_iota(jnp.int32, (2 * BLOCK, BLOCK), 0) % BLOCK
            allowed = allowed & (query >= lanes((2 * BLOCK, BLOCK)))
        weights = jnp.where(allowed, jnp.exp2(scores * SCALE2), 0.0).astype(BF)
        values = jnp.where(low_lane, jnp.ones_like(kv), kv)
        return total + dot(weights, values)

    total = lax.fori_loop(0, block, lambda j, t: part(j, t, False), jnp.zeros((2 * BLOCK, 128), F32))
    total = part(block, total, True)
    sums = pltpu.roll(total, HDIM, 1)
    mixed = total / sums
    first = pltpu.roll(mixed[:BLOCK], HDIM, 1)
    o_ref[...] = jnp.where(low_lane, first, mixed[BLOCK:]).astype(BF)
    inv_ref[0:1, :] = 1.0 / jnp.transpose(total[:BLOCK])[0:1, :]
    inv_ref[1:2, :] = 1.0 / jnp.transpose(total[BLOCK:])[0:1, :]


def attend(q, kv, segcol, segrow):
    return pl.pallas_call(
        attend_kernel,
        grid=(SEQ // BLOCK,),
        out_shape=(jax.ShapeDtypeStruct((SEQ, 128), BF), jax.ShapeDtypeStruct((2, SEQ), F32)),
        in_specs=[
            pl.BlockSpec((BLOCK, 128), lambda i: (i, 0)), pl.BlockSpec((SEQ, 128), lambda i: (0, 0)),
            pl.BlockSpec((BLOCK, 1), lambda i: (i, 0)), pl.BlockSpec((1, SEQ), lambda i: (0, 0)),
        ],
        out_specs=[pl.BlockSpec((BLOCK, 128), lambda i: (i, 0)), pl.BlockSpec((2, BLOCK), lambda i: (0, i))],
        compiler_params=params(),
    )(q, kv, segcol, segrow)


def attend_back_kernel(q_ref, kv_ref, do_ref, o_ref, inv_ref, segcol_ref, segrow_ref, dq_ref, dkv_ref, qs, dos, drow, acc):
    block = pl.program_id(0)

    @pl.when(block == 0)
    def _():
        acc[...] = jnp.zeros_like(acc)
        low_lane = lanes((BLOCK, 128)) < HDIM
        pick = (lax.broadcasted_iota(jnp.int32, (8, 128), 0) == lanes((8, 128)) // HDIM).astype(BF)
        for i in range(SEQ // BLOCK):
            rows = slice(i * BLOCK, (i + 1) * BLOCK)
            q = q_ref[rows, :].astype(F32)
            do = do_ref[rows, :].astype(F32)
            qs[i, :BLOCK] = jnp.where(low_lane, q, 0.0).astype(BF)
            qs[i, BLOCK:] = jnp.where(low_lane, pltpu.roll(q, HDIM, 1), 0.0).astype(BF)
            dos[i, :BLOCK] = jnp.where(low_lane, 0.0, pltpu.roll(do, HDIM, 1)).astype(BF)
            dos[i, BLOCK:] = jnp.where(low_lane, 0.0, do).astype(BF)
            product = do * o_ref[rows, :].astype(F32)
            high = product.astype(BF)
            rest = (product - high.astype(F32)).astype(BF)
            sums = dot_cols(pick, high) + dot_cols(pick, rest)
            drow[i, 0:1, :BLOCK] = sums[0:1]
            drow[i, 0:1, BLOCK:] = sums[1:2]
            drow[i, 1:2, :BLOCK] = inv_ref[0:1, rows]
            drow[i, 1:2, BLOCK:] = inv_ref[1:2, rows]

    kv = kv_ref[...]
    seg_k = segcol_ref[...]

    def part(i, total, diagonal):
        queries, upstream = qs[i], dos[i]
        scores = dot_cols(kv, queries)
        slopes = dot_cols(kv, upstream)
        seg_q = segrow_ref[:, pl.ds(pl.multiple_of(i * BLOCK, BLOCK), BLOCK)]
        seg_q = jnp.concatenate([seg_q, seg_q], axis=1)
        allowed = seg_k == seg_q
        if diagonal:
            key = lax.broadcasted_iota(jnp.int32, (BLOCK, 2 * BLOCK), 0)
            allowed = allowed & (lanes((BLOCK, 2 * BLOCK)) % BLOCK >= key)
        weights = jnp.where(allowed, jnp.exp2(scores * SCALE2), 0.0) * drow[i, 1:2, :]
        change = (weights * (slopes - drow[i, 0:1, :])).astype(BF)
        total = total + dot(change, queries) * HDIM**-0.5 + dot(weights.astype(BF), upstream)
        acc[i] = acc[i] + dot_rows(change, kv)
        return total

    total = part(block, jnp.zeros((BLOCK, 128), F32), True)
    total = lax.fori_loop(block + 1, SEQ // BLOCK, lambda i, t: part(i, t, False), total)
    dkv_ref[...] = total.astype(BF)

    @pl.when(block == SEQ // BLOCK - 1)
    def _():
        low_lane = lanes((BLOCK, 128)) < HDIM
        for i in range(SEQ // BLOCK):
            rows = slice(i * BLOCK, (i + 1) * BLOCK)
            both = jnp.where(low_lane, acc[i, :BLOCK], pltpu.roll(acc[i, BLOCK:], HDIM, 1))
            dq_ref[rows, :] = (both * HDIM**-0.5).astype(BF)


def attend_back(q, kv, do, o, inv, segcol, segrow):
    full = lambda shape: pl.BlockSpec(shape, lambda i: (0,) * len(shape))
    blocks = SEQ // BLOCK
    return pl.pallas_call(
        attend_back_kernel,
        grid=(blocks,),
        out_shape=(jax.ShapeDtypeStruct((SEQ, 128), BF), jax.ShapeDtypeStruct((SEQ, 128), BF)),
        in_specs=[
            full((SEQ, 128)), pl.BlockSpec((BLOCK, 128), lambda i: (i, 0)), full((SEQ, 128)), full((SEQ, 128)), full((2, SEQ)),
            pl.BlockSpec((BLOCK, 1), lambda i: (i, 0)), full((1, SEQ)),
        ],
        out_specs=[full((SEQ, 128)), pl.BlockSpec((BLOCK, 128), lambda i: (i, 0))],
        scratch_shapes=[
            pltpu.VMEM((blocks, 2 * BLOCK, 128), BF), pltpu.VMEM((blocks, 2 * BLOCK, 128), BF),
            pltpu.VMEM((blocks, 2, 2 * BLOCK), F32), pltpu.VMEM((blocks, 2 * BLOCK, 128), F32),
        ],
        compiler_params=params(),
    )(q, kv, do, o, inv, segcol, segrow)


def heads_to_rows(ref):
    parts = [jnp.concatenate([ref[s * 8 + h] for h in range(8)], axis=1) for s in range(2)]
    return jnp.concatenate(parts, axis=0)


def middle_kernel(x_ref, o_ref, wo_ref, gain_ref, full_ref, x1_ref, h2_ref):
    attended = heads_to_rows(o_ref)
    full_ref[...] = attended
    residual = x_ref[...].astype(F32) + dot(attended, wo_ref[...])
    x1_ref[...] = residual
    normed, _, _ = norm(residual, gain_ref[...])
    h2_ref[...] = normed.astype(BF)


def middle(x, o, wo, gain):
    return pl.pallas_call(
        middle_kernel,
        out_shape=(
            jax.ShapeDtypeStruct((ROWS, D), BF), jax.ShapeDtypeStruct((ROWS, D), F32), jax.ShapeDtypeStruct((ROWS, D), BF),
        ),
        in_specs=[vmem()] * 4,
        out_specs=[vmem()] * 3,
        compiler_params=params(),
    )(x, o, wo, gain)


FF_BLOCK = 512


def feed_kernel(h_ref, m_ref, wg_ref, wu_ref, wd_ref, out_ref, back_ref, gg_ref, gu_ref, gd_ref, turned):
    step = pl.program_id(0)

    @pl.when(step == 0)
    def _():
        out_ref[...] = jnp.zeros_like(out_ref)
        back_ref[...] = jnp.zeros_like(back_ref)
        turned[...] = jnp.transpose(h_ref[...])

    low, upstream = h_ref[...], m_ref[...]
    gate = dot(low, wg_ref[...])
    up = dot(low, wu_ref[...])
    sig = jax.nn.sigmoid(gate)
    silu = gate * sig
    hidden = (silu * up).astype(BF)
    out_ref[...] += dot(hidden, wd_ref[...])
    slope = dot_cols(upstream, wd_ref[...])
    gate_grad = (slope * up * sig * (1.0 + gate * (1.0 - sig))).astype(BF)
    up_grad = (slope * silu).astype(BF)
    back_ref[...] += dot_cols(gate_grad, wg_ref[...]) + dot_cols(up_grad, wu_ref[...])
    gd_ref[...] = dot_rows(hidden, upstream).astype(BF)
    gg_ref[...] = dot(turned[...], gate_grad).astype(BF)
    gu_ref[...] = dot(turned[...], up_grad).astype(BF)


def feed(h, m, wg, wu, wd):
    full = lambda shape: pl.BlockSpec(shape, lambda i: (0,) * len(shape))
    wide = pl.BlockSpec((D, FF_BLOCK), lambda i: (0, i))
    tall = pl.BlockSpec((FF_BLOCK, D), lambda i: (i, 0))
    both = 2 * ROWS
    return pl.pallas_call(
        feed_kernel,
        grid=(HALF // FF_BLOCK,),
        out_shape=(
            jax.ShapeDtypeStruct((both, D), F32), jax.ShapeDtypeStruct((both, D), F32),
            jax.ShapeDtypeStruct((D, HALF), BF), jax.ShapeDtypeStruct((D, HALF), BF), jax.ShapeDtypeStruct((HALF, D), BF),
        ),
        in_specs=[full((both, D)), full((both, D)), wide, wide, tall],
        out_specs=[full((both, D)), full((both, D)), wide, wide, tall],
        scratch_shapes=[pltpu.VMEM((D, both), BF)],
        compiler_params=params(),
    )(h, m, wg, wu, wd)


def norm_back(upstream, gain, unit, factor):
    scaled = upstream * gain
    return factor * (scaled - unit * jnp.mean(scaled * unit, axis=-1, keepdims=True))


def after_kernel(x1_ref, out_ref, out_other, back_ref, back_other, m_ref, gain_ref, wo_ref, full_ref, y_ref, dx1_ref, do_ref, gout_ref, gain_out):
    residual = x1_ref[...]
    y_ref[...] = (residual + out_ref[...] + out_other[...]).astype(BF)
    gain = gain_ref[...]
    _, unit, factor = norm(residual, gain)
    upstream = back_ref[...] + back_other[...]
    gain_out[...] = jnp.sum(upstream * unit, axis=0, keepdims=True)
    dx1 = m_ref[...].astype(F32) + norm_back(upstream, gain, unit, factor)
    dx1_ref[...] = dx1
    da = dx1.astype(BF)
    gout_ref[...] = dot_rows(full_ref[...], da).astype(BF)
    do = dot_cols(da, wo_ref[...]).astype(BF)
    for s in range(2):
        for h in range(8):
            do_ref[s * 8 + h] = do[s * 128 : (s + 1) * 128, h * 128 : (h + 1) * 128]


def after(*arrays):
    return pl.pallas_call(
        after_kernel,
        out_shape=(
            jax.ShapeDtypeStruct((ROWS, D), BF), jax.ShapeDtypeStruct((ROWS, D), F32), jax.ShapeDtypeStruct((16, 128, 128), BF),
            jax.ShapeDtypeStruct((D, D), BF), jax.ShapeDtypeStruct((1, D), F32),
        ),
        in_specs=[vmem()] * 9,
        out_specs=[vmem()] * 5,
        compiler_params=params(),
    )(*arrays)


def final_kernel(x_ref, gain_ref, qgain_ref, kgain_ref, cos_ref, sin_ref, h_ref, qraw_ref, kraw_ref, dq_ref, dkv_ref, wq_ref, wkv_ref, dx1_ref,
                 y_ref, gq_ref, gkv_ref, gain_out, qgain_out, kgain_out, dq_full, dkv_full):
    cosine, sine = cos_ref[...], sin_ref[...]
    sums = head_sum_matrix()
    low_lane = lanes((ROWS, 128)) < HDIM
    qg = jnp.zeros((1, 128), F32)
    kg = jnp.zeros((1, 128), F32)

    def back(raw, upstream, gain):
        factor = lax.rsqrt(split_dot(raw * raw, sums) * (1.0 / HDIM) + EPSILON)
        unit = raw * factor
        turned = upstream * cosine - turn(upstream) * sine
        scaled = turned * gain
        mean = split_dot(scaled * unit, sums) * (1.0 / HDIM)
        return factor * (scaled - unit * mean), jnp.sum(turned * unit, axis=0, keepdims=True)

    for h in range(8):
        cols = slice(h * 128, (h + 1) * 128)
        upstream = jnp.concatenate([dq_ref[h], dq_ref[8 + h]], axis=0).astype(F32)
        pre, terms = back(qraw_ref[:, cols], upstream, qgain_ref[...])
        qg = qg + terms
        dq_full[:, cols] = pre.astype(BF)
        upstream = jnp.concatenate([dkv_ref[h], dkv_ref[8 + h]], axis=0).astype(F32)
        pre, terms = back(kraw_ref[:, cols], upstream, kgain_ref[...])
        kg = kg + terms
        dkv_full[:, cols] = jnp.where(low_lane, pre, upstream).astype(BF)
    qgain_out[...] = qg
    kgain_out[...] = kg
    dq, dkv, low = dq_full[...], dkv_full[...], h_ref[...]
    gq_ref[...] = dot_rows(low, dq).astype(BF)
    gkv_ref[...] = dot_rows(low, dkv).astype(BF)
    dh = dot_cols(dq, wq_ref[...]) + dot_cols(dkv, wkv_ref[...])
    _, unit, factor = norm(x_ref[...].astype(F32), gain_ref[...])
    gain_out[...] = jnp.sum(dh * unit, axis=0, keepdims=True)
    y_ref[...] = (dx1_ref[...] + norm_back(dh, gain_ref[...], unit, factor)).astype(BF)


def final(*arrays):
    row = lambda n: jax.ShapeDtypeStruct((1, n), F32)
    return pl.pallas_call(
        final_kernel,
        out_shape=(
            jax.ShapeDtypeStruct((ROWS, D), BF), jax.ShapeDtypeStruct((D, D), BF), jax.ShapeDtypeStruct((D, D), BF),
            row(D), row(128), row(128),
        ),
        in_specs=[vmem()] * 14,
        out_specs=[vmem()] * 6,
        scratch_shapes=[pltpu.VMEM((ROWS, D), BF), pltpu.VMEM((ROWS, D), BF)],
        compiler_params=params(),
    )(*arrays)


def tables(first_row):
    places = first_row + jnp.arange(128, dtype=jnp.int32)
    frequency = THETA_BASE ** (-jnp.arange(0, HDIM, 2, dtype=F32) / HDIM)
    angles = places.astype(F32)[:, None] * frequency[None, :]
    cosine, sine = jnp.tile(jnp.cos(angles), (2, 4)), jnp.tile(jnp.sin(angles), (2, 4))
    return cosine, sine


def pair_heads(wk, wv):
    rows = wk.shape[0]
    return jnp.concatenate([wk.reshape(rows, 8, 1, HDIM), wv.reshape(rows, 8, 1, HDIM)], axis=2).reshape(rows, D)


def by_core(w):
    w = w.reshape(8, 4, 2, 16, 36)
    w = jnp.pad(w, ((0, 0), (0, 0), (0, 0), (0, 0), (0, PADDED - 36)))
    return w.transpose(2, 0, 1, 3, 4).reshape(2, 8, HALF)


def from_core(w):
    w = w.reshape(2, 8, 4, 16, PADDED)[..., :36]
    return w.transpose(1, 2, 0, 3, 4).reshape(8, 4608)


def exchange(*arrays):
    pairs = [(i, i ^ 1) for i in range(8)]
    return [lax.ppermute(a, "dp", pairs) for a in arrays]


def local(block_in, segment_ids, attn_gain, w_query, w_key, w_value, query_gain, key_gain, w_out, ffn_gain, w_gate, w_up, w_down, out_grad):
    ctx = lax.axis_index("ctx")
    x = block_in.reshape(ROWS, D)
    m = out_grad.reshape(ROWS, D)
    cosine, sine = tables(ctx * 128)
    row = lambda v: v.reshape(1, -1)
    qgain, kgain = row(jnp.tile(query_gain, 2)), row(jnp.tile(key_gain, 2))
    seg = lax.dynamic_index_in_dim(segment_ids, ctx // 8, 0, keepdims=False)
    segcol, segrow = seg.reshape(SEQ, 1), seg.reshape(1, SEQ)

    wq, wkv, wo, wg, wu, wd = gather(
        w_query, pair_heads(w_key, w_value), w_out, by_core(w_gate), by_core(w_up), jnp.pad(w_down, ((0, PADDED - 36), (0, 0))))
    wq, wkv, wo = wq.reshape(D, D), wkv.reshape(D, D), wo.reshape(D, D)
    wg, wu, wd = wg.reshape(D, HALF), wu.reshape(D, HALF), wd.reshape(HALF, D)

    h1, qraw, kraw, q, kv = project(x, row(attn_gain), qgain, kgain, cosine, sine, wq, wkv)
    q, kv = swap(2, q.reshape(16, 128, 128), kv.reshape(16, 128, 128))
    q, kv = q.reshape(SEQ, 128), kv.reshape(SEQ, 128)
    o, inv = attend(q, kv, segcol, segrow)
    (o_rows,) = swap(3, o.reshape(16, 128, 128))
    attended, x1, h2 = middle(x, o_rows, wo, row(ffn_gain))
    h2_other, m_other = exchange(h2, m)
    out, back, gg, gu, gd = feed(
        jnp.concatenate([h2, h2_other]), jnp.concatenate([m, m_other]), wg, wu, wd)
    out_other, back_other = exchange(out[ROWS:], back[ROWS:])
    y, dx1, do, gout, ffn_terms = after(
        x1, out[:ROWS], out_other, back[:ROWS], back_other, m, row(ffn_gain), wo, attended)
    (do_seq,) = swap(4, do)
    dq, dkv = attend_back(q, kv, do_seq.reshape(SEQ, 128), o, inv, segcol, segrow)
    dq, dkv = swap(5, dq.reshape(16, 128, 128), dkv.reshape(16, 128, 128))
    y_in, gq, gkv, attn_terms, qterms, kterms = final(
        x, row(attn_gain), qgain, kgain, cosine, sine, h1, qraw, kraw, dq, dkv, wq, wkv, dx1)
    terms = jnp.concatenate([attn_terms, ffn_terms, qterms, kterms, jnp.zeros((1, 768), F32)], axis=1).reshape(24, 128)
    small = lambda a: a.reshape(4, 2, 4, 4, 8, D)
    gq, gkv, gout, gg, gu, gd, terms = scatter(
        small(gq), small(gkv), small(gout), gg.reshape(4, 2, 4, 4, 8, HALF), gu.reshape(4, 2, 4, 4, 8, HALF),
        gd.reshape(4, 4, 4, PADDED, D), terms)
    terms = terms.reshape(-1)
    gkv = gkv.reshape(8, 8, 2, HDIM)
    return (
        y.reshape(2, 128, D), y_in.reshape(2, 128, D), gq, gkv[:, :, 0].reshape(8, 512), gkv[:, :, 1].reshape(8, 512), gout,
        from_core(gg), from_core(gu), gd[:36], terms[:D], terms[2 * D : 2 * D + 64] + terms[2 * D + 64 : 2 * D + 128],
        terms[2 * D + 128 : 2 * D + 192], terms[D : 2 * D],
    )


def solution(mesh):
    both = P(("dp", "ctx"), None)
    acts = P("dp", "ctx", None)
    return jax.shard_map(
        local,
        mesh=mesh,
        in_specs=(acts, P("dp", None), P(), both, both, both, P(), P(), both, P(), both, both, both, acts),
        out_specs=(acts, acts, both, both, both, both, both, both, both, P(), P(), P(), P()),
        check_vma=False,
    )
```

```python
import functools

import jax
import jax.numpy as jnp
from jax import lax
from jax.experimental import pallas as pl
from jax.experimental.pallas import tpu as pltpu
from jax.sharding import PartitionSpec as P

MESH = pl.DeviceIdType.MESH
BF = jnp.bfloat16
F32 = jnp.float32

D = 1024
HDIM = 64
HEADS = 8
ROWS = 256
SEQ = 2048
PADDED = 40
HALF = 64 * PADDED
EPSILON = 1e-05
THETA_BASE = 1000000.0
LOG2E = 1.4426950408889634
VMEM_MOST = 60 * 1024 * 1024


def params(**more):
    return pltpu.CompilerParams(vmem_limit_bytes=VMEM_MOST, **more)


def vmem():
    return pl.BlockSpec(memory_space=pltpu.VMEM)


def hbm():
    return pl.BlockSpec(memory_space=pl.ANY)


def dot(left, right):
    return lax.dot_general(left, right, (((1,), (0,)), ((), ())), preferred_element_type=F32)


def dot_rows(left, right):
    return lax.dot_general(left, right, (((0,), (0,)), ((), ())), preferred_element_type=F32)


def dot_cols(left, right):
    return lax.dot_general(left, right, (((1,), (1,)), ((), ())), preferred_element_type=F32)


def place():
    dp, ctx = lax.axis_index("dp"), lax.axis_index("ctx")
    return {"y": dp // 2, "c": dp % 2, "z": ctx // 4, "x": ctx % 4}


def device(at, **moved):
    spot = dict(at)
    spot.update(moved)
    return (spot["y"] * 2 + spot["c"], spot["z"] * 4 + spot["x"])


def beside(at, dim, by):
    return device(at, **{dim: (at[dim] + by) % 4})


ORDERS = (("x", "z", "y"), ("y", "x", "z"), ("z", "y", "x"))


class Layout:
    def __init__(self, kind, order, columns):
        self.kind, self.order, self.columns = kind, order, columns

    def index(self, at, full, fixed=None, half=None):
        spot = dict(at)
        if fixed:
            spot.update(fixed)
        ids = {d: (slice(None) if d in full else spot[d]) for d in "xyz"}
        c = {"own": at["c"], "both": slice(None), "none": None}[self.kind]
        out = [ids["y"]] + ([] if c is None else [c]) + [ids["z"], ids["x"], slice(None)]
        if half is None:
            out.append(slice(None))
        else:
            out.append(pl.ds(half * (self.columns // 2), self.columns // 2))
        return tuple(out)


class Gather:
    def __init__(self, at, arrays, layouts, send, recv):
        self.at, self.arrays, self.layouts, self.send, self.recv = at, arrays, layouts, send, recv
        self.started = []

    def copy(self, i, stage, slot, index, to):
        ref = self.arrays[i].at[index]
        return pltpu.make_async_remote_copy(
            src_ref=ref, dst_ref=ref, send_sem=self.send.at[i, stage, slot], recv_sem=self.recv.at[i, stage, slot],
            device_id=to, device_id_type=MESH)

    def start(self, i, stage, slot, index, to):
        copy = self.copy(i, stage, slot, index, to)
        copy.start()
        self.started.append(copy)

    def slab(self, i, stage, by, half=None):
        lay = self.layouts[i]
        dim, full = lay.order[stage], lay.order[:stage]
        return lay.index(self.at, full, {dim: (self.at[dim] + by) % 4}, half)

    def first(self, i, stage):
        dim = self.layouts[i].order[stage]
        self.start(i, stage, 0, self.slab(i, stage, 0), beside(self.at, dim, 1))
        self.start(i, stage, 1, self.slab(i, stage, 0), beside(self.at, dim, 3))

    def arrived(self, i, stage, slot, by, half):
        self.copy(i, stage, slot, self.slab(i, stage, by, half), beside(self.at, "x", 1)).wait_recv()

    def second(self, i, stage):
        dim = self.layouts[i].order[stage]
        self.arrived(i, stage, 0, 3, None)
        self.start(i, stage, 2, self.slab(i, stage, 3, 0), beside(self.at, dim, 1))
        self.arrived(i, stage, 1, 1, None)
        self.start(i, stage, 3, self.slab(i, stage, 1, 1), beside(self.at, dim, 3))

    def last(self, i, stage):
        self.arrived(i, stage, 2, 2, 0)
        self.arrived(i, stage, 3, 2, 1)


def layouts():
    return [
        Layout("own", ORDERS[0], D), Layout("own", ORDERS[1], D), Layout("own", ORDERS[2], D),
        Layout("both", ORDERS[0], HALF), Layout("both", ORDERS[1], HALF), Layout("none", ORDERS[2], D),
    ]


def lanes(shape):
    return lax.broadcasted_iota(jnp.int32, shape, len(shape) - 1)


def norm(values, gain):
    factor = lax.rsqrt(jnp.mean(values * values, axis=-1, keepdims=True) + EPSILON)
    unit = values * factor
    return unit * gain, unit, factor


def split_dot(values, matrix):
    high = values.astype(BF)
    low = (values - high.astype(F32)).astype(BF)
    return dot(high, matrix) + dot(low, matrix)


def head_sum_matrix():
    rows = lax.broadcasted_iota(jnp.int32, (128, 128), 0) // HDIM
    return (rows == lanes((128, 128)) // HDIM).astype(BF)


def turn(values):
    low = lanes(values.shape) % HDIM < HDIM // 2
    ahead = pltpu.roll(values, 128 - HDIM // 2, 1)
    behind = pltpu.roll(values, HDIM // 2, 1)
    return jnp.where(low, -ahead, behind)


BLOCK = 256
SCALE2 = LOG2E * HDIM**-0.5


def heads_to_rows(ref):
    parts = [jnp.concatenate([ref[s * 8 + h] for h in range(8)], axis=1) for s in range(2)]
    return jnp.concatenate(parts, axis=0)


def forward_kernel(x_ref, m_ref, gain_ref, qgain_ref, kgain_ref, fgain_ref, cos_ref, sin_ref, segcol_ref, segrow_ref,
                   q_in, kv_in, o_in, g_in, u_in, d_in,
                   wq_ref, wkv_ref, wo_ref, g_out, u_out, d_out, h_ref, qraw_ref, kraw_ref, qseq, kvseq, oseq, inv_ref, full_ref, x1_ref,
                   h2_ref, m2_ref,
                   wq8, wkv8, wo8, qown, kvown, orows,
                   local_sem, core_send, core_recv, send, recv, swap_send, swap_recv, swap_local):
    at = place()
    c = at["c"]
    dp, ctx = lax.axis_index("dp"), lax.axis_index("ctx")
    partner = device(at, c=1 - c)
    barrier = pltpu.get_barrier_semaphore()
    for to in (partner, beside(at, "y", 1), beside(at, "y", 3)):
        pl.semaphore_signal(barrier, inc=1, device_id=to, device_id_type=MESH)

    @pl.loop(1, 16)
    def _(step):
        pl.semaphore_signal(barrier, inc=1, device_id=(dp, (ctx + step) % 16), device_id_type=MESH)

    here = (at["y"], c, at["z"], at["x"])
    stays = [
        pltpu.make_async_copy(q_in, wq8.at[here], local_sem.at[0]),
        pltpu.make_async_copy(kv_in, wkv8.at[here], local_sem.at[1]),
        pltpu.make_async_copy(o_in, wo8.at[here], local_sem.at[2]),
        pltpu.make_async_copy(g_in.at[c], g_out.at[here], local_sem.at[3]),
        pltpu.make_async_copy(u_in.at[c], u_out.at[here], local_sem.at[4]),
        pltpu.make_async_copy(d_in, d_out.at[at["y"], at["z"], at["x"]], local_sem.at[5]),
    ]
    for copy in stays:
        copy.start()
    for copy in stays:
        copy.wait()
    pl.semaphore_wait(barrier, 18)

    ring = Gather(at, [wq8, wkv8, wo8, g_out, u_out, d_out], layouts(), send, recv)
    attn, feed_mats = (0, 1, 2), (3, 4, 5)

    def core_copy(slot, src, dst):
        return pltpu.make_async_remote_copy(
            src_ref=src, dst_ref=dst, send_sem=core_send.at[slot], recv_sem=core_recv.at[slot], device_id=partner,
            device_id_type=MESH)

    for i in attn:
        ring.first(i, 0)
    wide = [core_copy(0, g_in.at[1 - c], g_out.at[here]), core_copy(1, u_in.at[1 - c], u_out.at[here])]
    upstream_copy = core_copy(2, m_ref, m2_ref.at[1])
    for copy in wide:
        copy.start()
    upstream_copy.start()
    normed, _, _ = norm(x_ref[...].astype(F32), gain_ref[...])
    h_ref[...] = normed.astype(BF)
    m2_ref[0] = m_ref[...]
    for copy in wide:
        copy.wait_recv()
    for i in feed_mats:
        ring.first(i, 0)
    for i in attn:
        ring.second(i, 0)
    for i in attn:
        ring.last(i, 0)
        ring.first(i, 1)
    for i in feed_mats:
        ring.second(i, 0)
    for i in attn:
        ring.second(i, 1)
    for i in feed_mats:
        ring.last(i, 0)
        ring.first(i, 1)
    for i in attn:
        ring.last(i, 1)
        ring.first(i, 2)
    for i in feed_mats:
        ring.second(i, 1)
    for i in attn:
        ring.second(i, 2)
    for i in feed_mats:
        ring.last(i, 1)
        ring.first(i, 2)
    swaps = []
    eights = (wq8, wkv8, wo8)
    for i in attn:
        ring.last(i, 2)
        copy = core_copy(3 + i, eights[i].at[:, c], eights[i].at[:, c])
        copy.start()
        swaps.append(copy)

    def flatten(eight, flat, core):
        @pl.loop(0, 4)
        def _(y):
            rows = pl.ds(pl.multiple_of(y * 256 + core * 128, 128), 128)
            flat[rows, :] = eight[y, core].astype(F32).reshape(128, D).astype(BF)

    def other_rows(i):
        core_copy(3 + i, eights[i].at[:, 1 - c], eights[i].at[:, 1 - c]).wait_recv()

    flatten(wq8, wq_ref, c)
    flatten(wkv8, wkv_ref, c)
    other_rows(0)
    flatten(wq8, wq_ref, 1 - c)
    low = h_ref[...]
    query = dot(low, wq_ref[...])
    for h in range(8):
        qraw_ref[h] = query[:, h * 128 : (h + 1) * 128]
    other_rows(1)
    flatten(wkv8, wkv_ref, 1 - c)
    key_value = dot(low, wkv_ref[...])
    for h in range(8):
        kraw_ref[h] = key_value[:, h * 128 : (h + 1) * 128]

    sums = head_sum_matrix()
    cosine, sine = cos_ref[...], sin_ref[...]

    def rotated(raw, gain):
        factor = lax.rsqrt(split_dot(raw * raw, sums) * (1.0 / HDIM) + EPSILON)
        unit = raw * factor * gain
        return unit * cosine + turn(unit) * sine

    def swap_copy(k, src, dst, to, slot):
        return pltpu.make_async_remote_copy(
            src_ref=src, dst_ref=dst, send_sem=swap_send.at[k, to], recv_sem=swap_recv.at[k, slot], device_id=(dp, to),
            device_id_type=MESH)

    @pl.loop(0, 8)
    def _(step):
        h = (ctx + step) % 8
        raw = qraw_ref[h]
        qown[h] = rotated(raw, qgain_ref[...]).astype(BF)
        raw = kraw_ref[h]
        kvown[h] = jnp.where(lanes(raw.shape) < HDIM, rotated(raw, kgain_ref[...]), raw).astype(BF)
        for s in range(2):
            to = s * 8 + h
            rows = pl.ds(s * 128, 128)

            @pl.when(to != ctx)
            def _():
                swap_copy(0, kvown.at[h, rows], kvseq.at[ctx], to, ctx).start()
                swap_copy(1, qown.at[h, rows], qseq.at[ctx], to, ctx).start()

            @pl.when(to == ctx)
            def _():
                pltpu.make_async_copy(kvown.at[h, rows], kvseq.at[ctx], swap_local.at[0]).start()
                pltpu.make_async_copy(qown.at[h, rows], qseq.at[ctx], swap_local.at[1]).start()

    other_rows(2)
    flatten(wo8, wo_ref, c)
    flatten(wo8, wo_ref, 1 - c)

    low_lane = lanes((BLOCK, 128)) < HDIM

    def arrive(source):
        @pl.when(source != ctx)
        def _():
            swap_copy(0, kvseq.at[source], kvseq.at[source], source, source).wait_recv()
            swap_copy(1, qseq.at[source], qseq.at[source], source, source).wait_recv()

        @pl.when(source == ctx)
        def _():
            pltpu.make_async_copy(kvown.at[0, pl.ds(0, 128)], kvseq.at[ctx], swap_local.at[0]).wait()
            pltpu.make_async_copy(qown.at[0, pl.ds(0, 128)], qseq.at[ctx], swap_local.at[1]).wait()

    def queries(block):
        arrive(2 * block)
        arrive(2 * block + 1)
        q = qseq[pl.ds(2 * block, 2)].reshape(BLOCK, 128)
        zero = jnp.zeros_like(q)
        second = pltpu.roll(q.astype(F32), HDIM, 1).astype(BF)
        stacked = jnp.concatenate([jnp.where(low_lane, q, zero), jnp.where(low_lane, second, zero)], axis=0)
        rows = pl.ds(pl.multiple_of(block * BLOCK, BLOCK), BLOCK)
        seg_q = segcol_ref[rows, :]
        seg_q = jnp.concatenate([seg_q, seg_q], axis=0)

        def part(j, total, diagonal):
            kv = kvseq[pl.ds(2 * j, 2)].reshape(BLOCK, 128)
            scores = dot_cols(stacked, kv)
            allowed = seg_q == segrow_ref[:, pl.ds(pl.multiple_of(j * BLOCK, BLOCK), BLOCK)]
            if diagonal:
                query = lax.broadcasted_iota(jnp.int32, (2 * BLOCK, BLOCK), 0) % BLOCK
                allowed = allowed & (query >= lanes((2 * BLOCK, BLOCK)))
            weights = jnp.where(allowed, jnp.exp2(scores * SCALE2), 0.0).astype(BF)
            values = jnp.where(low_lane, jnp.ones_like(kv), kv)
            return total + dot(weights, values)

        total = lax.fori_loop(0, block, lambda j, t: part(j, t, False), jnp.zeros((2 * BLOCK, 128), F32))
        total = part(block, total, True)
        mixed = total / pltpu.roll(total, HDIM, 1)
        first = pltpu.roll(mixed[:BLOCK], HDIM, 1)
        oseq[pl.ds(2 * block, 2)] = jnp.where(low_lane, first, mixed[BLOCK:]).astype(BF).reshape(2, 128, 128)
        inv_ref[0:1, rows] = 1.0 / jnp.transpose(total[:BLOCK])[0:1, :]
        inv_ref[1:2, rows] = 1.0 / jnp.transpose(total[BLOCK:])[0:1, :]
        for k in range(2):
            to = 2 * block + k

            @pl.when(to != ctx)
            def _():
                swap_copy(2, oseq.at[to], orows.at[ctx], to, ctx).start()

            @pl.when(to == ctx)
            def _():
                pltpu.make_async_copy(oseq.at[to], orows.at[ctx], swap_local.at[2]).start()

    @pl.loop(0, 6)
    def _(block):
        queries(block)

    for i in feed_mats:
        ring.second(i, 2)

    @pl.loop(6, 8)
    def _(block):
        queries(block)

    @pl.loop(0, 16)
    def _(source):
        @pl.when(source != ctx)
        def _():
            swap_copy(2, orows.at[source], orows.at[source], source, source).wait_recv()

        @pl.when(source == ctx)
        def _():
            pltpu.make_async_copy(oseq.at[ctx], orows.at[ctx], swap_local.at[2]).wait()

    attended = heads_to_rows(orows)
    full_ref[...] = attended
    residual = x_ref[...].astype(F32) + dot(attended, wo_ref[...])
    x1_ref[...] = residual
    normed, _, _ = norm(residual, fgain_ref[...])
    h2_ref[0] = normed.astype(BF)
    mid_copy = core_copy(6, h2_ref.at[0], h2_ref.at[1])
    mid_copy.start()
    for i in feed_mats:
        ring.last(i, 2)

    @pl.loop(0, 16)
    def _(to):
        @pl.when(to != ctx)
        def _():
            swap_copy(0, kvown.at[0, pl.ds(0, 128)], kvseq.at[to], to, to).wait_send()
            swap_copy(1, qown.at[0, pl.ds(0, 128)], qseq.at[to], to, to).wait_send()
            swap_copy(2, oseq.at[to], orows.at[to], to, to).wait_send()

    for copy in wide + swaps:
        copy.wait_send()
    upstream_copy.wait()
    mid_copy.wait()
    for copy in ring.started:
        copy.wait_send()


def forward(*arrays):
    shape = jax.ShapeDtypeStruct
    dma = pltpu.SemaphoreType.DMA
    wide = shape((4, 2, 4, 4, 8, HALF), BF)
    return pl.pallas_call(
        forward_kernel,
        out_shape=(
            shape((D, D), BF), shape((D, D), BF), shape((D, D), BF), wide, wide, shape((4, 4, 4, PADDED, D), BF),
            shape((ROWS, D), BF), shape((8, ROWS, 128), F32), shape((8, ROWS, 128), F32), shape((16, 128, 128), BF),
            shape((16, 128, 128), BF), shape((16, 128, 128), BF), shape((2, SEQ), F32), shape((ROWS, D), BF), shape((ROWS, D), F32),
            shape((2, ROWS, D), BF), shape((2, ROWS, D), BF),
        ),
        in_specs=[vmem()] * 13 + [hbm()] * 3,
        out_specs=[vmem()] * 3 + [hbm()] * 3 + [vmem()] * 11,
        scratch_shapes=[pltpu.VMEM((4, 2, 4, 4, 8, D), BF)] * 3 + [pltpu.VMEM((8, ROWS, 128), BF)] * 2 + [pltpu.VMEM((16, 128, 128), BF)]
        + [dma((6,)), dma((7,)), dma((7,)), dma((6, 3, 4)), dma((6, 3, 4)), dma((3, 16)), dma((3, 16)), dma((3,))],
        compiler_params=params(collective_id=0, has_side_effects=True),
    )(*arrays)


FF_BLOCK = 512


def feed_kernel(h_ref, m_ref, wg_ref, wu_ref, wd_ref, out_ref, back_ref, gg_ref, gu_ref, gd_ref, turned):
    step = pl.program_id(0)

    @pl.when(step == 0)
    def _():
        out_ref[...] = jnp.zeros_like(out_ref)
        back_ref[...] = jnp.zeros_like(back_ref)
        turned[...] = jnp.transpose(h_ref[...])

    low, upstream = h_ref[...], m_ref[...]
    gate = dot(low, wg_ref[...])
    up = dot(low, wu_ref[...])
    sig = jax.nn.sigmoid(gate)
    silu = gate * sig
    hidden = (silu * up).astype(BF)
    out_ref[...] += dot(hidden, wd_ref[...])
    slope = dot_cols(upstream, wd_ref[...])
    gate_grad = (slope * up * sig * (1.0 + gate * (1.0 - sig))).astype(BF)
    up_grad = (slope * silu).astype(BF)
    back_ref[...] += dot_cols(gate_grad, wg_ref[...]) + dot_cols(up_grad, wu_ref[...])
    gd_ref[...] = dot_rows(hidden, upstream).astype(BF)
    gg_ref[...] = dot(turned[...], gate_grad).astype(BF)
    gu_ref[...] = dot(turned[...], up_grad).astype(BF)


def feed(h, m, wg, wu, wd):
    full = lambda shape: pl.BlockSpec(shape, lambda i: (0,) * len(shape))
    wide = pl.BlockSpec((D, FF_BLOCK), lambda i: (0, i))
    tall = pl.BlockSpec((FF_BLOCK, D), lambda i: (i, 0))
    both = 2 * ROWS
    return pl.pallas_call(
        feed_kernel,
        grid=(HALF // FF_BLOCK,),
        out_shape=(
            jax.ShapeDtypeStruct((both, D), F32), jax.ShapeDtypeStruct((both, D), F32),
            jax.ShapeDtypeStruct((D, HALF), BF), jax.ShapeDtypeStruct((D, HALF), BF), jax.ShapeDtypeStruct((HALF, D), BF),
        ),
        in_specs=[full((both, D)), full((both, D)), wide, wide, tall],
        out_specs=[full((both, D)), full((both, D)), wide, wide, tall],
        scratch_shapes=[pltpu.VMEM((D, both), BF)],
        compiler_params=params(),
    )(h, m, wg, wu, wd)


def norm_back(upstream, gain, unit, factor):
    scaled = upstream * gain
    return factor * (scaled - unit * jnp.mean(scaled * unit, axis=-1, keepdims=True))


class Scatter:
    def __init__(self, at, grads, layouts, bufs, own, fins, send, recv, load):
        self.at, self.grads, self.layouts, self.bufs, self.own, self.fins = at, grads, layouts, bufs, own, fins
        self.send, self.recv, self.load = send, recv, load
        self.started = []

    def copy(self, i, stage, slot, src, dst, to):
        return pltpu.make_async_remote_copy(
            src_ref=src, dst_ref=dst, send_sem=self.send.at[i, stage, slot], recv_sem=self.recv.at[i, stage, slot],
            device_id=to, device_id_type=MESH)

    def start(self, *args):
        copy = self.copy(*args)
        copy.start()
        self.started.append(copy)

    def arrived(self, i, stage, slot, dst):
        self.copy(i, stage, slot, dst, dst, beside(self.at, "x", 1)).wait_recv()

    def lanes(self, i, half):
        width = self.layouts[i].columns // 2
        return pl.ds(half * width, width)

    def source(self, i, stage, by, half):
        lay = self.layouts[i]
        dim, full = lay.order[stage], lay.order[stage + 1 :]
        if stage == 0:
            return self.grads[i].at[lay.index(self.at, full, {dim: (self.at[dim] + by) % 4}, half)]
        kept = [d for d in "yzx" if d in lay.order[stage:]]
        index = [slice(None) if d != dim else (self.at[dim] + by) % 4 for d in kept]
        if lay.kind == "both":
            index.insert(1 if "y" in kept else 0, slice(None))
        return self.bufs[i][2 * stage - 1].at[(0, *index, slice(None), self.lanes(i, half))]

    def parts(self, i, stage):
        halves, near = self.bufs[i][2 * stage], self.bufs[i][2 * stage + 1]
        row = (slice(None),) * (len(near.shape) - 2)
        return halves, near, lambda side, half: near.at[(side, *row, self.lanes(i, half))]

    def in_vmem(self, i, stage):
        return stage > 0 or self.own[i] is None

    def loads(self, i, stage, second):
        steps = ((0, 0, 0), (1, 0, 1)) if second else ((0, 1, 0), (1, 3, 1))
        return [
            pltpu.make_async_copy(self.source(i, stage, by, half), self.own[i].at[k], self.load.at[i, k]) for k, by, half in steps
        ]

    def first(self, i, stage):
        dim = self.layouts[i].order[stage]
        halves, near, part = self.parts(i, stage)
        ahead, behind = beside(self.at, dim, 1), beside(self.at, dim, 3)
        self.start(i, stage, 0, self.source(i, stage, 2, 0), halves.at[0], ahead)
        self.start(i, stage, 1, self.source(i, stage, 2, 1), halves.at[1], behind)
        self.start(i, stage, 2, self.source(i, stage, 1, 1), part(0, 1), ahead)
        self.start(i, stage, 3, self.source(i, stage, 3, 0), part(1, 0), behind)
        if not self.in_vmem(i, stage):
            for copy in self.loads(i, stage, False):
                copy.start()

    def second(self, i, stage):
        dim = self.layouts[i].order[stage]
        halves, near, part = self.parts(i, stage)
        for side, by in ((0, 1), (1, 3)):
            self.arrived(i, stage, side, halves.at[side])
            if self.in_vmem(i, stage):
                mine = self.source(i, stage, by, side)
            else:
                self.loads(i, stage, False)[side].wait()
                mine = self.own[i].at[side]
            add_into(halves.at[side], halves.at[side], mine)
            self.start(i, stage, 4 + side, halves.at[side], part(side, side), beside(self.at, dim, by))
        if not self.in_vmem(i, stage):
            for copy in self.loads(i, stage, True):
                copy.start()

    def last(self, i, stage):
        halves, near, part = self.parts(i, stage)
        self.arrived(i, stage, 2, part(0, 1))
        self.arrived(i, stage, 3, part(1, 0))
        self.arrived(i, stage, 4, part(0, 0))
        self.arrived(i, stage, 5, part(1, 1))
        for half in range(2):
            if self.in_vmem(i, stage):
                mine = self.source(i, stage, 0, half)
            else:
                self.loads(i, stage, True)[half].wait()
                mine = self.own[i].at[half]
            target = part(0, half)
            if stage == 2:
                target = self.fins[i].at[(slice(None),) * (len(self.fins[i].shape) - 1) + (self.lanes(i, half),)]
            add_into(target, part(0, half), part(1, half), mine)


def add_into(target, *terms):
    def body(spot):
        total = terms[0][spot].astype(F32)
        for term in terms[1:]:
            total = total + term[spot].astype(F32)
        target[spot] = total.astype(target.dtype)

    lead = target.shape[:-2]
    count = 1
    for n in lead:
        count *= n
    if count == 1:
        body((0,) * len(lead))
        return

    @pl.loop(0, count)
    def _(flat):
        spot = []
        for n in reversed(lead):
            spot.insert(0, flat % n)
            flat = flat // n
        body(tuple(spot))


def stage_shapes(lay, rows):
    shapes = []
    for stage in range(3):
        left = lay.order[stage + 1 :]
        lead = ([4] if "y" in left else []) + ([2] if lay.kind == "both" else [])
        lead += [4] * (("z" in left) + ("x" in left))
        shapes.append((2, *lead, rows, lay.columns // 2))
        shapes.append((2, *lead, rows, lay.columns))
    return shapes


def norm_back(upstream, gain, unit, factor):
    scaled = upstream * gain
    return factor * (scaled - unit * jnp.mean(scaled * unit, axis=-1, keepdims=True))


GAIN_ROWS = 24


def backward_kernel(*refs):
    (x_ref, m_ref, gain_ref, qgain_ref, kgain_ref, fgain_ref, cos_ref, sin_ref, segcol_ref, segrow_ref, x1_ref, out_hbm, back_hbm,
     full_ref, qseq, kvseq, oseq, inv_ref, h_ref, qraw_ref, kraw_ref, wo_hbm, wq_hbm, wkv_hbm, g_hbm, u_hbm, d_hbm) = refs[:27]
    (y_ref, yin_ref, q_fin, kv_fin, o_fin, g_fin, u_fin, d_fin, gains_out) = refs[27:36]
    (gq, gkv, go, out_own, back_own, out_other, back_other, do_own, do_seq, dq_own, dkv_own, dq_in, dkv_in, acc, dq_full, dkv_full,
     gains, gain_slots, wide_g, wide_u, first_mat, second_mat) = refs[36:58]
    cores = refs[58:61]
    own = [None, None, None, *refs[61:64]]
    bufs = [refs[64 + 6 * i : 70 + 6 * i] for i in range(6)]
    (core_send, core_recv, local_sem, send, recv, load_sem, swap_send, swap_recv, swap_local, gain_send, gain_recv) = refs[100:111]
    at = place()
    c = at["c"]
    dp, ctx = lax.axis_index("dp"), lax.axis_index("ctx")
    partner = device(at, c=1 - c)
    barrier = pltpu.get_barrier_semaphore()
    for to in (partner, beside(at, "y", 1), beside(at, "y", 3)):
        pl.semaphore_signal(barrier, inc=1, device_id=to, device_id_type=MESH)

    @pl.loop(1, 16)
    def _(step):
        pl.semaphore_signal(barrier, inc=1, device_id=(dp, (ctx + step) % 16), device_id_type=MESH)

    def core_copy(slot, src, dst):
        return pltpu.make_async_remote_copy(
            src_ref=src, dst_ref=dst, send_sem=core_send.at[slot], recv_sem=core_recv.at[slot], device_id=partner,
            device_id_type=MESH)

    rows_own, rows_other = pl.ds(0, ROWS), pl.ds(ROWS, ROWS)
    stays = [
        pltpu.make_async_copy(back_hbm.at[rows_own], back_own, local_sem.at[0]),
        pltpu.make_async_copy(out_hbm.at[rows_own], out_own, local_sem.at[1]),
        pltpu.make_async_copy(wo_hbm, first_mat, local_sem.at[2]),
        pltpu.make_async_copy(wkv_hbm, second_mat, local_sem.at[3]),
    ]
    for copy in stays:
        copy.start()
    pl.semaphore_wait(barrier, 18)
    swaps = [core_copy(0, back_hbm.at[rows_other], back_other), core_copy(1, out_hbm.at[rows_other], out_other)]
    for copy in swaps:
        copy.start()
    fins = [q_fin, kv_fin, o_fin, wide_g, wide_u, d_fin]
    ring = Scatter(at, [gq, gkv, go, g_hbm, u_hbm, d_hbm], layouts(), bufs, own, fins, send, recv, load_sem)
    attn, feed_mats = (0, 1, 2), (3, 4, 5)
    for i in feed_mats:
        ring.first(i, 0)

    for copy in stays:
        copy.wait()
    swaps[0].wait()
    residual = x1_ref[...]
    gain = fgain_ref[...]
    _, unit, factor = norm(residual, gain)
    upstream = back_own[...] + back_other[...]
    for k in range(8):
        gains[8 + k : 9 + k, :] = jnp.sum(upstream[:, k * 128 : (k + 1) * 128] * unit[:, k * 128 : (k + 1) * 128], axis=0, keepdims=True)
    dx1 = m_ref[...].astype(F32) + norm_back(upstream, gain, unit, factor)
    back_own[...] = dx1
    do = dot_cols(dx1.astype(BF), first_mat[...]).astype(BF)
    for s in range(2):
        for h in range(8):
            do_own[s * 8 + h] = do[s * 128 : (s + 1) * 128, h * 128 : (h + 1) * 128]
    query_mat = pltpu.make_async_copy(wq_hbm, first_mat, local_sem.at[4])
    query_mat.start()

    def swap_copy(k, src, dst, to, slot):
        return pltpu.make_async_remote_copy(
            src_ref=src, dst_ref=dst, send_sem=swap_send.at[k, to], recv_sem=swap_recv.at[k, slot], device_id=(dp, to),
            device_id_type=MESH)

    def swap_start(k, src, dst, to):
        @pl.when(to != ctx)
        def _():
            swap_copy(k, src.at[to], dst.at[ctx], to, ctx).start()

        @pl.when(to == ctx)
        def _():
            pltpu.make_async_copy(src.at[to], dst.at[ctx], swap_local.at[k]).start()

    def swap_wait(k, src, dst, source):
        @pl.when(source != ctx)
        def _():
            swap_copy(k, dst.at[source], dst.at[source], source, source).wait_recv()

        @pl.when(source == ctx)
        def _():
            pltpu.make_async_copy(src.at[ctx], dst.at[ctx], swap_local.at[k]).wait()

    @pl.loop(0, 16)
    def _(step):
        swap_start(0, do_own, do_seq, (ctx + step) % 16)

    acc[...] = jnp.zeros_like(acc)
    swaps[1].wait()
    y_ref[...] = (residual + out_own[...] + out_other[...]).astype(BF)

    def rows_gradient(grad, left, right):
        @pl.loop(0, 4)
        def _(y):
            cols = pl.ds(pl.multiple_of(y * 256, 256), 256)
            value = dot_rows(left[:, cols], right[...])
            grad[y] = value.reshape(2, 4, 4, 8, D).astype(BF)

    dq_full[...] = back_own[...].astype(BF)
    rows_gradient(go, full_ref, dq_full)
    swaps.append(core_copy(2, go.at[:, 1 - c], cores[2]))
    swaps[2].start()

    low_lane = lanes((BLOCK, 128)) < HDIM
    pick = (lax.broadcasted_iota(jnp.int32, (8, 128), 0) == lanes((8, 128)) // HDIM).astype(BF)

    def queries(block):
        swap_wait(0, do_own, do_seq, 2 * block)
        swap_wait(0, do_own, do_seq, 2 * block + 1)
        pair = pl.ds(2 * block, 2)
        rows = pl.ds(pl.multiple_of(block * BLOCK, BLOCK), BLOCK)
        q = qseq[pair].reshape(BLOCK, 128).astype(F32)
        do = do_seq[pair].reshape(BLOCK, 128).astype(F32)
        product = do * oseq[pair].reshape(BLOCK, 128).astype(F32)
        stacked = jnp.concatenate([jnp.where(low_lane, q, 0.0), jnp.where(low_lane, pltpu.roll(q, HDIM, 1), 0.0)], axis=0).astype(BF)
        above = jnp.concatenate([jnp.where(low_lane, 0.0, pltpu.roll(do, HDIM, 1)), jnp.where(low_lane, 0.0, do)], axis=0).astype(BF)
        high = product.astype(BF)
        rest = (product - high.astype(F32)).astype(BF)
        sums = dot_cols(pick, high) + dot_cols(pick, rest)
        row_dots = jnp.concatenate([sums[0:1], sums[1:2]], axis=1)
        inv = jnp.concatenate([inv_ref[0:1, rows], inv_ref[1:2, rows]], axis=1)
        seg_q = jnp.concatenate([segrow_ref[:, rows], segrow_ref[:, rows]], axis=1)

        def part(j, total, diagonal):
            kv = kvseq[pl.ds(2 * j, 2)].reshape(BLOCK, 128)
            scores = dot_cols(kv, stacked)
            slopes = dot_cols(kv, above)
            allowed = segcol_ref[pl.ds(pl.multiple_of(j * BLOCK, BLOCK), BLOCK), :] == seg_q
            if diagonal:
                key = lax.broadcasted_iota(jnp.int32, (BLOCK, 2 * BLOCK), 0)
                allowed = allowed & (lanes((BLOCK, 2 * BLOCK)) % BLOCK >= key)
            weights = jnp.where(allowed, jnp.exp2(scores * SCALE2), 0.0) * inv
            change = (weights * (slopes - row_dots)).astype(BF)
            acc[j] = acc[j] + dot(change, stacked) * HDIM**-0.5 + dot(weights.astype(BF), above)
            return total + dot_rows(change, kv)

        total = lax.fori_loop(0, block, lambda j, t: part(j, t, False), jnp.zeros((2 * BLOCK, 128), F32))
        total = part(block, total, True)
        both = jnp.where(low_lane, total[:BLOCK], pltpu.roll(total[BLOCK:], HDIM, 1)) * HDIM**-0.5
        dq_own[pair] = both.astype(BF).reshape(2, 128, 128)
        dkv_own[pair] = acc[block].astype(BF).reshape(2, 128, 128)
        for k in range(2):
            swap_start(1, dkv_own, dkv_in, 2 * block + k)
            swap_start(2, dq_own, dq_in, 2 * block + k)

    @pl.loop(0, 5)
    def _(step):
        queries(7 - step)

    for i in feed_mats:
        ring.second(i, 0)

    @pl.loop(5, 8)
    def _(step):
        queries(7 - step)

    cosine, sine = cos_ref[...], sin_ref[...]
    head_sums = head_sum_matrix()
    wide_lane = lanes((ROWS, 128)) < HDIM

    def head_back(raw, upstream, gain):
        factor = lax.rsqrt(split_dot(raw * raw, head_sums) * (1.0 / HDIM) + EPSILON)
        unit = raw * factor
        turned = upstream * cosine - turn(upstream) * sine
        scaled = turned * gain
        mean = split_dot(scaled * unit, head_sums) * (1.0 / HDIM)
        return factor * (scaled - unit * mean), jnp.sum(turned * unit, axis=0, keepdims=True)

    @pl.loop(0, 16)
    def _(source):
        swap_wait(1, dkv_own, dkv_in, source)
        swap_wait(2, dq_own, dq_in, source)

    qterms = jnp.zeros((1, 128), F32)
    kterms = jnp.zeros((1, 128), F32)
    for h in range(8):
        cols = slice(h * 128, (h + 1) * 128)
        upstream = jnp.concatenate([dq_in[h], dq_in[8 + h]], axis=0).astype(F32)
        pre, terms = head_back(qraw_ref[h], upstream, qgain_ref[...])
        qterms = qterms + terms
        dq_full[:, cols] = pre.astype(BF)
        upstream = jnp.concatenate([dkv_in[h], dkv_in[8 + h]], axis=0).astype(F32)
        pre, terms = head_back(kraw_ref[h], upstream, kgain_ref[...])
        kterms = kterms + terms
        dkv_full[:, cols] = jnp.where(wide_lane, pre, upstream).astype(BF)
    gains[16:17, :] = qterms
    gains[17:18, :] = kterms
    gains[18:24, :] = jnp.zeros((6, 128), F32)
    rows_gradient(gq, h_ref, dq_full)
    swaps.append(core_copy(3, gq.at[:, 1 - c], cores[0]))
    swaps[3].start()
    rows_gradient(gkv, h_ref, dkv_full)
    swaps.append(core_copy(4, gkv.at[:, 1 - c], cores[1]))
    swaps[4].start()
    for i in feed_mats:
        ring.last(i, 0)
        ring.first(i, 1)
    for slot, i in ((2, 2), (3, 0), (4, 1)):
        swaps[slot].wait_recv()
        mine = ring.grads[i].at[:, c]
        add_into(mine, mine, cores[i])
        ring.first(i, 0)

    query_mat.wait()
    dh = dot_cols(dq_full[...], first_mat[...]) + dot_cols(dkv_full[...], second_mat[...])
    gain = gain_ref[...]
    _, unit, factor = norm(x_ref[...].astype(F32), gain)
    for k in range(8):
        gains[k : k + 1, :] = jnp.sum(dh[:, k * 128 : (k + 1) * 128] * unit[:, k * 128 : (k + 1) * 128], axis=0, keepdims=True)
    yin_ref[...] = (back_own[...] + norm_back(dh, gain, unit, factor)).astype(BF)

    started = []

    def gain_copy(stage, slot, index, to):
        ref = gain_slots.at[stage, index]
        return pltpu.make_async_remote_copy(
            src_ref=ref, dst_ref=ref, send_sem=gain_send.at[stage, slot], recv_sem=gain_recv.at[stage, slot], device_id=to,
            device_id_type=MESH)

    def gain_start(stage, slot, index, to):
        copy = gain_copy(stage, slot, index, to)
        copy.start()
        started.append(copy)

    def gain_first(stage, total):
        dim = "xyz"[stage]
        p = at[dim]
        gain_slots[stage, p] = total
        gain_start(stage, 0, p, beside(at, dim, 1))
        gain_start(stage, 1, p, beside(at, dim, 3))

    def gain_second(stage):
        dim = "xyz"[stage]
        before = (at[dim] + 3) % 4
        gain_copy(stage, 0, before, partner).wait_recv()
        gain_start(stage, 2, before, beside(at, dim, 1))

    def gain_last(stage):
        dim = "xyz"[stage]
        gain_copy(stage, 1, (at[dim] + 1) % 4, partner).wait_recv()
        gain_copy(stage, 2, (at[dim] + 2) % 4, partner).wait_recv()
        return gain_slots[stage, 0] + gain_slots[stage, 1] + gain_slots[stage, 2] + gain_slots[stage, 3]

    gain_first(0, gains[...])
    for i in attn:
        ring.second(i, 0)
    gain_second(0)
    for i in feed_mats:
        ring.second(i, 1)
    for i in attn:
        ring.last(i, 0)
        ring.first(i, 1)
    gain_first(1, gain_last(0))
    for i in feed_mats:
        ring.last(i, 1)
        ring.first(i, 2)
    for i in attn:
        ring.second(i, 1)
    gain_second(1)
    for i in feed_mats:
        ring.second(i, 2)
    for i in attn:
        ring.last(i, 1)
        ring.first(i, 2)
    gain_first(2, gain_last(1))
    finals = []
    for i in feed_mats:
        ring.last(i, 2)
        if i < 5:
            wide, fin = ring.fins[i], (g_fin, u_fin)[i - 3]
            finals.append(core_copy(2 + i, wide.at[1 - c], fin.at[c]))
            finals[-1].start()
            fin[c] = wide[c]
    for i in attn:
        ring.second(i, 2)
    gain_second(2)
    for i in attn:
        ring.last(i, 2)
    gain_slots[3, c] = gain_last(2)
    finals.append(core_copy(7, gain_slots.at[3, c], gain_slots.at[3, c]))
    finals[-1].start()
    for slot, fin in ((5, g_fin), (6, u_fin)):
        core_copy(slot, fin.at[1 - c], fin.at[1 - c]).wait_recv()
    core_copy(7, gain_slots.at[3, 1 - c], gain_slots.at[3, 1 - c]).wait_recv()
    gains_out[...] = gain_slots[3, 0] + gain_slots[3, 1]

    @pl.loop(0, 16)
    def _(to):
        @pl.when(to != ctx)
        def _():
            swap_copy(0, do_own.at[to], do_seq.at[to], to, to).wait_send()
            swap_copy(1, dkv_own.at[to], dkv_in.at[to], to, to).wait_send()
            swap_copy(2, dq_own.at[to], dq_in.at[to], to, to).wait_send()

    for copy in swaps[2:] + finals + started + ring.started:
        copy.wait_send()


def backward(*arrays):
    shape = jax.ShapeDtypeStruct
    dma = pltpu.SemaphoreType.DMA
    small = shape((8, D), F32)
    wide = shape((2, 8, HALF), F32)
    block = pltpu.VMEM((16, 128, 128), BF)
    own = pltpu.VMEM((ROWS, D), F32)
    scratch = [pltpu.VMEM((4, 2, 4, 4, 8, D), BF)] * 3 + [own] * 4 + [block] * 6
    scratch += [pltpu.VMEM((SEQ // BLOCK, BLOCK, 128), F32)] + [pltpu.VMEM((ROWS, D), BF)] * 2
    scratch += [pltpu.VMEM((GAIN_ROWS, 128), F32), pltpu.VMEM((4, 4, GAIN_ROWS, 128), F32)] + [pltpu.VMEM((2, 8, HALF), F32)] * 2
    scratch += [pltpu.VMEM((D, D), BF)] * 2 + [pltpu.VMEM((4, 4, 4, 8, D), BF)] * 3
    lays = layouts()
    shapes = [stage_shapes(lay, PADDED if lay.kind == "none" else 8) for lay in lays]
    scratch += [pltpu.VMEM(shapes[i][0], BF) for i in (3, 4, 5)]
    for group in shapes:
        scratch += [pltpu.VMEM(s, BF) for s in group]
    scratch += [
        dma((8,)), dma((8,)), dma((5,)), dma((6, 3, 6)), dma((6, 3, 6)), dma((6, 2)), dma((3, 16)), dma((3, 16)), dma((3,)), dma((3, 3)),
        dma((3, 3)),
    ]
    return pl.pallas_call(
        backward_kernel,
        out_shape=(
            shape((ROWS, D), BF), shape((ROWS, D), BF), small, small, small, wide, wide, shape((PADDED, D), F32),
            shape((GAIN_ROWS, 128), F32),
        ),
        in_specs=[vmem()] * 11 + [hbm()] * 2 + [vmem()] * 8 + [hbm()] * 6,
        out_specs=[vmem()] * 9,
        scratch_shapes=scratch,
        compiler_params=params(collective_id=1, has_side_effects=True),
    )(*arrays)


def tables(first_row):
    places = first_row + jnp.arange(128, dtype=jnp.int32)
    frequency = THETA_BASE ** (-jnp.arange(0, HDIM, 2, dtype=F32) / HDIM)
    angles = places.astype(F32)[:, None] * frequency[None, :]
    cosine, sine = jnp.tile(jnp.cos(angles), (2, 4)), jnp.tile(jnp.sin(angles), (2, 4))
    return cosine, sine


def pair_heads(wk, wv):
    rows = wk.shape[0]
    return jnp.concatenate([wk.reshape(rows, 8, 1, HDIM), wv.reshape(rows, 8, 1, HDIM)], axis=2).reshape(rows, D)


def by_core(w):
    w = w.reshape(8, 4, 2, 16, 36)
    w = jnp.pad(w, ((0, 0), (0, 0), (0, 0), (0, 0), (0, PADDED - 36)))
    return w.transpose(2, 0, 1, 3, 4).reshape(2, 8, HALF)


def from_core(w):
    w = w.reshape(2, 8, 4, 16, PADDED)[..., :36]
    return w.transpose(1, 2, 0, 3, 4).reshape(8, 4608)


def local(block_in, segment_ids, attn_gain, w_query, w_key, w_value, query_gain, key_gain, w_out, ffn_gain, w_gate, w_up, w_down, out_grad):
    ctx = lax.axis_index("ctx")
    x = block_in.reshape(ROWS, D)
    m = out_grad.reshape(ROWS, D)
    cosine, sine = tables(ctx * 128)
    row = lambda v: v.reshape(1, -1)
    qgain, kgain = row(jnp.tile(query_gain, 2)), row(jnp.tile(key_gain, 2))
    seg = lax.dynamic_index_in_dim(segment_ids, ctx // 8, 0, keepdims=False)
    segcol, segrow = seg.reshape(SEQ, 1), seg.reshape(1, SEQ)

    (wq, wkv, wo, wg, wu, wd, h1, qraw, kraw, q, kv, o, inv, attended, x1, h2, m2) = forward(
        x, m, row(attn_gain), qgain, kgain, row(ffn_gain), cosine, sine, segcol, segrow,
        w_query, pair_heads(w_key, w_value), w_out, by_core(w_gate), by_core(w_up), jnp.pad(w_down, ((0, PADDED - 36), (0, 0))))
    wg, wu, wd = wg.reshape(D, HALF), wu.reshape(D, HALF), wd.reshape(HALF, D)
    out, back, gg, gu, gd = feed(h2.reshape(2 * ROWS, D), m2.reshape(2 * ROWS, D), wg, wu, wd)
    y, y_in, gq, gkv, gout, gg, gu, gd, terms = backward(
        x, m, row(attn_gain), qgain, kgain, row(ffn_gain), cosine, sine, segcol, segrow, x1, out, back, attended, q, kv, o, inv, h1,
        qraw, kraw, wo, wq, wkv, gg.reshape(4, 2, 4, 4, 8, HALF), gu.reshape(4, 2, 4, 4, 8, HALF), gd.reshape(4, 4, 4, PADDED, D))
    terms = terms.reshape(-1)
    gkv = gkv.reshape(8, 8, 2, HDIM)
    return (
        y.reshape(2, 128, D), y_in.reshape(2, 128, D), gq, gkv[:, :, 0].reshape(8, 512), gkv[:, :, 1].reshape(8, 512), gout,
        from_core(gg), from_core(gu), gd[:36], terms[:D], terms[2 * D : 2 * D + 64] + terms[2 * D + 64 : 2 * D + 128],
        terms[2 * D + 128 : 2 * D + 192], terms[D : 2 * D],
    )


def solution(mesh):
    both = P(("dp", "ctx"), None)
    acts = P("dp", "ctx", None)
    return jax.shard_map(
        local,
        mesh=mesh,
        in_specs=(acts, P("dp", None), P(), both, both, both, P(), P(), both, P(), both, both, both, acts),
        out_specs=(acts, acts, both, both, both, both, both, both, both, P(), P(), P(), P()),
        check_vma=False,
    )
```

```python
import functools

import jax
import jax.numpy as jnp
from jax import lax
from jax.experimental import pallas as pl
from jax.experimental.pallas import tpu as pltpu
from jax.sharding import PartitionSpec as P

MESH = pl.DeviceIdType.MESH
BF = jnp.bfloat16
F32 = jnp.float32

D = 1024
HDIM = 64
HEADS = 8
ROWS = 256
SEQ = 2048
PARTS = (16, 16, 8)
PADDED = sum(PARTS)
HALF = 64 * PADDED
EPSILON = 1e-05
THETA_BASE = 1000000.0
LOG2E = 1.4426950408889634
VMEM_MOST = 60 * 1024 * 1024


def params(**more):
    return pltpu.CompilerParams(vmem_limit_bytes=VMEM_MOST, **more)


def vmem():
    return pl.BlockSpec(memory_space=pltpu.VMEM)


def hbm():
    return pl.BlockSpec(memory_space=pl.ANY)


def dot(left, right):
    return lax.dot_general(left, right, (((1,), (0,)), ((), ())), preferred_element_type=F32)


def dot_rows(left, right):
    return lax.dot_general(left, right, (((0,), (0,)), ((), ())), preferred_element_type=F32)


def dot_cols(left, right):
    return lax.dot_general(left, right, (((1,), (1,)), ((), ())), preferred_element_type=F32)


def place():
    dp, ctx = lax.axis_index("dp"), lax.axis_index("ctx")
    return {"y": dp // 2, "c": dp % 2, "z": ctx // 4, "x": ctx % 4}


def device(at, **moved):
    spot = dict(at)
    spot.update(moved)
    return (spot["y"] * 2 + spot["c"], spot["z"] * 4 + spot["x"])


def beside(at, dim, by):
    return device(at, **{dim: (at[dim] + by) % 4})


ORDERS = (("x", "z", "y"), ("y", "x", "z"), ("z", "y", "x"))


class Layout:
    def __init__(self, kind, order, columns):
        self.kind, self.order, self.columns = kind, order, columns

    def index(self, at, full, fixed=None, half=None):
        spot = dict(at)
        if fixed:
            spot.update(fixed)
        ids = {d: (slice(None) if d in full else spot[d]) for d in "xyz"}
        c = {"own": at["c"], "both": slice(None), "none": None}[self.kind]
        out = [ids["y"]] + ([] if c is None else [c]) + [ids["z"], ids["x"], slice(None)]
        if half is None:
            out.append(slice(None))
        else:
            out.append(pl.ds(half * (self.columns // 2), self.columns // 2))
        return tuple(out)


class Gather:
    def __init__(self, at, arrays, layouts, send, recv):
        self.at, self.arrays, self.layouts, self.send, self.recv = at, arrays, layouts, send, recv
        self.started = []

    def copy(self, i, stage, slot, index, to):
        ref = self.arrays[i].at[index]
        return pltpu.make_async_remote_copy(
            src_ref=ref, dst_ref=ref, send_sem=self.send.at[i, stage, slot], recv_sem=self.recv.at[i, stage, slot],
            device_id=to, device_id_type=MESH)

    def start(self, i, stage, slot, index, to):
        copy = self.copy(i, stage, slot, index, to)
        copy.start()
        self.started.append(copy)

    def slab(self, i, stage, by, half=None):
        lay = self.layouts[i]
        dim, full = lay.order[stage], lay.order[:stage]
        return lay.index(self.at, full, {dim: (self.at[dim] + by) % 4}, half)

    def first(self, i, stage):
        dim = self.layouts[i].order[stage]
        self.start(i, stage, 0, self.slab(i, stage, 0), beside(self.at, dim, 1))
        self.start(i, stage, 1, self.slab(i, stage, 0), beside(self.at, dim, 3))

    def arrived(self, i, stage, slot, by, half):
        self.copy(i, stage, slot, self.slab(i, stage, by, half), beside(self.at, "x", 1)).wait_recv()

    def second(self, i, stage):
        dim = self.layouts[i].order[stage]
        self.arrived(i, stage, 0, 3, None)
        self.start(i, stage, 2, self.slab(i, stage, 3, 0), beside(self.at, dim, 1))
        self.arrived(i, stage, 1, 1, None)
        self.start(i, stage, 3, self.slab(i, stage, 1, 1), beside(self.at, dim, 3))

    def last(self, i, stage):
        self.arrived(i, stage, 2, 2, 0)
        self.arrived(i, stage, 3, 2, 1)


def attn_layouts():
    return [Layout("own", ORDERS[0], D), Layout("own", ORDERS[1], D), Layout("own", ORDERS[2], D)]


def gather_layouts():
    shapes = attn_layouts()
    for rows in PARTS:
        shapes += [Layout("both", ORDERS[0], 64 * rows), Layout("both", ORDERS[1], 64 * rows), Layout("none", ORDERS[2], D)]
    return shapes


def scatter_layouts():
    wide = [Layout("both", ORDERS[0], HALF), Layout("both", ORDERS[1], HALF)]
    return attn_layouts() + wide + [Layout("none", ORDERS[2], D)] * 3


def lanes(shape):
    return lax.broadcasted_iota(jnp.int32, shape, len(shape) - 1)


def norm(values, gain):
    factor = lax.rsqrt(jnp.mean(values * values, axis=-1, keepdims=True) + EPSILON)
    unit = values * factor
    return unit * gain, unit, factor


def split_dot(values, matrix):
    high = values.astype(BF)
    low = (values - high.astype(F32)).astype(BF)
    return dot(high, matrix) + dot(low, matrix)


def head_sum_matrix():
    rows = lax.broadcasted_iota(jnp.int32, (128, 128), 0) // HDIM
    return (rows == lanes((128, 128)) // HDIM).astype(BF)


def turn(values):
    low = lanes(values.shape) % HDIM < HDIM // 2
    ahead = pltpu.roll(values, 128 - HDIM // 2, 1)
    behind = pltpu.roll(values, HDIM // 2, 1)
    return jnp.where(low, -ahead, behind)


BLOCK = 256
SCALE2 = LOG2E * HDIM**-0.5


def heads_to_rows(ref):
    parts = [jnp.concatenate([ref[s * 8 + h] for h in range(8)], axis=1) for s in range(2)]
    return jnp.concatenate(parts, axis=0)


def unit_sources():
    column = lax.broadcasted_iota(jnp.int32, (1, 2 * 640), 1)
    core, k = column // 640, column % 640
    last = k >= 512
    ctx = jnp.where(last, (k - 512) // 8, (k % 256) // 16)
    row = jnp.where(last, 32 + k % 8, 16 * (k // 256) + k % 16)
    return jnp.where(row < 36, core * 576 + ctx * 36 + row, -1)


def spread_matrix(k, sources):
    rows = lax.broadcasted_iota(jnp.int32, (128, 2 * 640), 0) + 128 * k
    return jnp.where(rows == sources, 1.0, 0.0).astype(BF)


def part_columns(y):
    return [(0, y * 256, 256), (1, 1024 + y * 256, 256), (2, 2048 + y * 128, 128)]


FF_BLOCK = 512


def rope_of(table_ref):
    table = table_ref[...]
    low, turned = lanes(table.shape) < HDIM, pltpu.roll(table, HDIM, 1)
    cosine, sine = jnp.where(low, table, turned), jnp.where(low, turned, table)
    return jnp.concatenate([cosine, cosine], axis=0), jnp.concatenate([sine, sine], axis=0)


def twice(gain_ref):
    return jnp.concatenate([gain_ref[...], gain_ref[...]], axis=1)


def forward_kernel(*refs):
    (x_ref, m_ref, gain_ref, qgain_ref, kgain_ref, fgain_ref, table_ref, segs_ref, q_in, k_in, v_in,
     o_in, gate_in, up_in, down_in) = refs[:15]
    (wq8, wkv8, wo8, g_grad, u_grad, d_grad_a, d_grad_b, d_grad_c, h_ref, qraw_ref, kraw_ref, qseq, kvseq, oseq, inv_ref, full_ref, x1_ref,
     out_ref, back_ref) = refs[15:34]
    mats = refs[34:43]
    (qown, kvown, orows, h2_ref, m2_ref, turned, g_stage, u_stage, d_stage, d_stage_c, kv_in, down_pad, *wide_shards) = refs[43:61]
    (local_sem, core_send, core_recv, send, recv, swap_send, swap_recv, swap_local, store_sem) = refs[61:70]
    d_grads = (d_grad_a, d_grad_b, d_grad_c)
    at = place()
    c = at["c"]
    dp, ctx = lax.axis_index("dp"), lax.axis_index("ctx")
    partner = device(at, c=1 - c)
    barrier = pltpu.get_barrier_semaphore()
    for to in (partner, beside(at, "y", 1), beside(at, "y", 3)):
        pl.semaphore_signal(barrier, inc=1, device_id=to, device_id_type=MESH)

    @pl.loop(1, 16)
    def _(step):
        pl.semaphore_signal(barrier, inc=1, device_id=(dp, (ctx + step) % 16), device_id_type=MESH)

    sequence = pl.ds(ctx // 8, 1)
    here = (at["y"], c, at["z"], at["x"])
    ring = Gather(at, [wq8, wkv8, wo8, *mats], gather_layouts(), send, recv)
    attn, part_a, part_b, part_c = (0, 1, 2), (3, 4, 5), (6, 7, 8), (9, 10, 11)

    def core_copy(slot, src, dst):
        return pltpu.make_async_remote_copy(
            src_ref=src, dst_ref=dst, send_sem=core_send.at[slot], recv_sem=core_recv.at[slot], device_id=partner,
            device_id_type=MESH)

    low_half = lanes((8, 128)) < HDIM
    for k in range(4):
        key, value = (ref[:, k * 128 : (k + 1) * 128].astype(F32) for ref in (k_in, v_in))
        kv_in[:, k * 256 : k * 256 + 128] = jnp.where(low_half, key, pltpu.roll(value, HDIM, 1)).astype(BF)
        kv_in[:, k * 256 + 128 : (k + 1) * 256] = jnp.where(low_half, pltpu.roll(key, HDIM, 1), value).astype(BF)
    stays = [pltpu.make_async_copy(src, dst.at[here], local_sem.at[i]) for i, (src, dst) in enumerate(((q_in, wq8), (kv_in, wkv8), (o_in, wo8)))]
    for copy in stays:
        copy.start()
    for copy in stays:
        copy.wait()
    pl.semaphore_wait(barrier, 18)
    for i in attn:
        ring.first(i, 0)
    upstream_copy = core_copy(6, m_ref, m2_ref.at[1])
    upstream_copy.start()

    sources = unit_sources()
    units = jnp.concatenate(
        [ref[:, y * 1152 : (y + 1) * 1152].astype(F32) for y in range(4) for ref in (gate_in, up_in)], axis=0).astype(BF)
    spread = jnp.zeros((64, 2 * 640), F32)
    for k in range(9):
        spread = spread + dot(units[:, k * 128 : (k + 1) * 128], spread_matrix(k, sources))
    for y in range(4):
        for part, _, width in part_columns(y):
            for core in range(2):
                start = core * 640 + part * 256
                for j in range(2):
                    block = spread[16 * y + 8 * j : 16 * y + 8 * j + 8, start : start + width]
                    wide_shards[2 * part + j][core, :, y * width : (y + 1) * width] = block.astype(BF)
    down_pad[...] = jnp.concatenate([down_in[32:36, :].astype(F32), jnp.zeros((4, D), F32)], axis=0).astype(BF)
    downs = (down_in.at[pl.ds(0, 16)], down_in.at[pl.ds(16, 16)], down_pad)
    stays = []
    wide = []
    for k in range(3):
        for j in range(2):
            stays.append(pltpu.make_async_copy(wide_shards[2 * k + j].at[c], mats[3 * k + j].at[here], local_sem.at[3 + 3 * k + j]))
            wide.append(core_copy(2 * k + j, wide_shards[2 * k + j].at[1 - c], mats[3 * k + j].at[here]))
        stays.append(pltpu.make_async_copy(downs[k], mats[3 * k + 2].at[at["y"], at["z"], at["x"]], local_sem.at[5 + 3 * k]))
    stays.append(pltpu.make_async_copy(m_ref, m2_ref.at[0], local_sem.at[12]))
    for copy in wide + stays:
        copy.start()
    normed, _, _ = norm(x_ref[...].astype(F32), gain_ref[...])
    h_ref[...] = normed.astype(BF)
    for copy in stays:
        copy.wait()
    for copy in wide:
        copy.wait_recv()
    for i in part_a + part_b + part_c:
        ring.first(i, 0)

    def second(group, stage):
        for i in group:
            ring.second(i, stage)

    def following(group, stage):
        for i in group:
            ring.last(i, stage)
            ring.first(i, stage + 1)

    second(attn, 0)
    following(attn, 0)
    second(part_a, 0)
    second(attn, 1)
    following(part_a, 0)
    following(attn, 1)
    second(part_b + part_c, 0)
    second(part_a, 1)
    second(attn, 2)
    following(part_b + part_c, 0)
    swaps = []
    eights = (wq8, wkv8, wo8)
    for i in attn:
        ring.last(i, 2)
        copy = core_copy(7 + i, eights[i].at[:, c], eights[i].at[:, c])
        copy.start()
        swaps.append(copy)

    following(part_a, 1)
    second(part_b + part_c, 1)

    def other_rows(i):
        core_copy(7 + i, eights[i].at[:, 1 - c], eights[i].at[:, 1 - c]).wait_recv()

    def rows_of(core):
        cols = [h_ref[:, pl.ds(pl.multiple_of((2 * y + core) * 128, 128), 128)] for y in range(4)]
        return jnp.concatenate(cols, axis=1)

    def mat_of(eight, core):
        return eight[:, core].reshape(D // 2, D)

    mine, other = rows_of(c), rows_of(1 - c)
    query = dot(mine, mat_of(wq8, c))
    other_rows(0)
    query = query + dot(other, mat_of(wq8, 1 - c))
    for h in range(8):
        qraw_ref[h] = query[:, h * 128 : (h + 1) * 128]
    other_rows(1)
    key_value = dot(mine, mat_of(wkv8, c)) + dot(other, mat_of(wkv8, 1 - c))
    for h in range(8):
        kraw_ref[h] = key_value[:, h * 128 : (h + 1) * 128]

    sums = head_sum_matrix()
    cosine, sine = rope_of(table_ref)
    qgain, kgain = twice(qgain_ref), twice(kgain_ref)

    def rotated(raw, gain):
        factor = lax.rsqrt(split_dot(raw * raw, sums) * (1.0 / HDIM) + EPSILON)
        unit = raw * factor * gain
        return unit * cosine + turn(unit) * sine

    def swap_copy(k, src, dst, to, slot):
        return pltpu.make_async_remote_copy(
            src_ref=src, dst_ref=dst, send_sem=swap_send.at[k, to], recv_sem=swap_recv.at[k, slot], device_id=(dp, to),
            device_id_type=MESH)

    @pl.loop(0, 8)
    def _(step):
        h = (ctx + step) % 8
        raw = qraw_ref[h]
        qown[h] = rotated(raw, qgain).astype(BF)
        raw = kraw_ref[h]
        kvown[h] = jnp.where(lanes(raw.shape) < HDIM, rotated(raw, kgain), raw).astype(BF)
        for s in range(2):
            to = s * 8 + h
            rows = pl.ds(s * 128, 128)

            @pl.when(to != ctx)
            def _():
                swap_copy(0, kvown.at[h, rows], kvseq.at[ctx], to, ctx).start()
                swap_copy(1, qown.at[h, rows], qseq.at[ctx], to, ctx).start()

            @pl.when(to == ctx)
            def _():
                pltpu.make_async_copy(kvown.at[h, rows], kvseq.at[ctx], swap_local.at[0]).start()
                pltpu.make_async_copy(qown.at[h, rows], qseq.at[ctx], swap_local.at[1]).start()

    other_rows(2)
    low_lane = lanes((BLOCK, 128)) < HDIM

    def arrive(source):
        @pl.when(source != ctx)
        def _():
            swap_copy(0, kvseq.at[source], kvseq.at[source], source, source).wait_recv()
            swap_copy(1, qseq.at[source], qseq.at[source], source, source).wait_recv()

        @pl.when(source == ctx)
        def _():
            pltpu.make_async_copy(kvown.at[0, pl.ds(0, 128)], kvseq.at[ctx], swap_local.at[0]).wait()
            pltpu.make_async_copy(qown.at[0, pl.ds(0, 128)], qseq.at[ctx], swap_local.at[1]).wait()

    def queries(block):
        arrive(2 * block)
        arrive(2 * block + 1)
        q = qseq[pl.ds(2 * block, 2)].reshape(BLOCK, 128)
        zero = jnp.zeros_like(q)
        second = pltpu.roll(q.astype(F32), HDIM, 1).astype(BF)
        stacked = jnp.concatenate([jnp.where(low_lane, q, zero), jnp.where(low_lane, second, zero)], axis=0)
        rows = pl.ds(pl.multiple_of(block * BLOCK, BLOCK), BLOCK)
        seg_q = segment_column(segs_ref[sequence, rows])
        seg_q = jnp.concatenate([seg_q, seg_q], axis=0)

        def part(j, total, diagonal):
            kv = kvseq[pl.ds(2 * j, 2)].reshape(BLOCK, 128)
            scores = dot_cols(stacked, kv)
            allowed = seg_q == segs_ref[sequence, pl.ds(pl.multiple_of(j * BLOCK, BLOCK), BLOCK)]
            if diagonal:
                query = lax.broadcasted_iota(jnp.int32, (2 * BLOCK, BLOCK), 0) % BLOCK
                allowed = allowed & (query >= lanes((2 * BLOCK, BLOCK)))
            weights = jnp.where(allowed, jnp.exp2(scores * SCALE2), 0.0).astype(BF)
            values = jnp.where(low_lane, jnp.ones_like(kv), kv)
            return total + dot(weights, values)

        total = lax.fori_loop(0, block, lambda j, t: part(j, t, False), jnp.zeros((2 * BLOCK, 128), F32))
        total = part(block, total, True)
        mixed = total / pltpu.roll(total, HDIM, 1)
        first = pltpu.roll(mixed[:BLOCK], HDIM, 1)
        oseq[pl.ds(2 * block, 2)] = jnp.where(low_lane, first, mixed[BLOCK:]).astype(BF).reshape(2, 128, 128)
        inv_ref[0:1, rows] = 1.0 / jnp.transpose(total[:BLOCK])[0:1, :]
        inv_ref[1:2, rows] = 1.0 / jnp.transpose(total[BLOCK:])[0:1, :]
        for k in range(2):
            to = 2 * block + k

            @pl.when(to != ctx)
            def _():
                swap_copy(2, oseq.at[to], orows.at[ctx], to, ctx).start()

            @pl.when(to == ctx)
            def _():
                pltpu.make_async_copy(oseq.at[to], orows.at[ctx], swap_local.at[2]).start()

    queries(0)
    second(part_a, 2)
    following(part_b + part_c, 1)

    @pl.loop(1, 7)
    def _(block):
        queries(block)

    second(part_b + part_c, 2)

    @pl.loop(7, 8)
    def _(block):
        queries(block)

    @pl.loop(0, 16)
    def _(source):
        @pl.when(source != ctx)
        def _():
            swap_copy(2, orows.at[source], orows.at[source], source, source).wait_recv()

        @pl.when(source == ctx)
        def _():
            pltpu.make_async_copy(oseq.at[ctx], orows.at[ctx], swap_local.at[2]).wait()

    attended = heads_to_rows(orows)
    full_ref[...] = attended
    residual = x_ref[...].astype(F32) + dot(attended, wo8[...].reshape(D, D))
    x1_ref[...] = residual
    normed, _, _ = norm(residual, fgain_ref[...])
    h2_ref[0] = normed.astype(BF)
    mid_copy = core_copy(10, h2_ref.at[0], h2_ref.at[1])
    mid_copy.start()
    out_ref[...] = jnp.zeros_like(out_ref)
    back_ref[...] = jnp.zeros_like(back_ref)
    upstream_copy.wait()
    mid_copy.wait()
    turned[...] = jnp.transpose(h2_ref[...].reshape(2 * ROWS, D))

    def store_copies(part, step, slot):
        cols = pl.ds(pl.multiple_of(step * FF_BLOCK, FF_BLOCK), FF_BLOCK)
        where = (slice(None),) * 5 + (cols,)
        if part < 2:
            down, rows = d_stage, d_grads[part].at[pl.ds(2 * slot, 2)]
        else:
            down, rows = d_stage_c, d_grads[2]
        return [
            pltpu.make_async_copy(g_stage, g_grad.at[where], store_sem.at[0]),
            pltpu.make_async_copy(u_stage, u_grad.at[where], store_sem.at[1]),
            pltpu.make_async_copy(down, rows, store_sem.at[2 + (part == 2)]),
        ]

    def feed(part, slot):
        rows = PARTS[part]
        gate_mat, up_mat, down_mat = (mats[3 * part + j] for j in range(3))
        step = 2 * part + slot
        cols = pl.ds(pl.multiple_of(slot * FF_BLOCK, FF_BLOCK), FF_BLOCK)
        wg = gate_mat.reshape(D, 64 * rows)[:, cols]
        wu = up_mat.reshape(D, 64 * rows)[:, cols]
        wd = down_mat.reshape(64 * rows, D)[cols, :]
        low, upstream = h2_ref[...].reshape(2 * ROWS, D), m2_ref[...].reshape(2 * ROWS, D)
        gate = dot(low, wg)
        up = dot(low, wu)
        sig = jax.nn.sigmoid(gate)
        silu = gate * sig
        hidden = (silu * up).astype(BF)
        slope = dot_cols(upstream, wd)
        gate_grad = (slope * up * sig * (1.0 + gate * (1.0 - sig))).astype(BF)
        up_grad = (slope * silu).astype(BF)

        def freed():
            g_copy, u_copy, d_copy = store_copies(min(part, 1), step, 0)
            g_copy.wait()
            u_copy.wait()
            if part < 2:
                d_copy.wait()

        if part == 0:
            pl.when(slot > 0)(freed)
        else:
            freed()
        for y in range(0, 4, 2):
            left = turned[y * 256 : (y + 2) * 256, :]
            g_stage[y : y + 2] = dot(left, gate_grad).astype(BF).reshape(2, 2, 4, 4, 8, FF_BLOCK)
            u_stage[y : y + 2] = dot(left, up_grad).astype(BF).reshape(2, 2, 4, 4, 8, FF_BLOCK)
        down_grad = dot_rows(hidden, upstream).astype(BF)
        if part < 2:
            d_stage[...] = down_grad.reshape(2, 4, 4, 16, D)
        else:
            d_stage_c[...] = down_grad.reshape(4, 4, 4, 8, D)
        for copy in store_copies(part, step, slot):
            copy.start()
        out_ref[...] += dot(hidden, wd)
        back_ref[...] += dot_cols(gate_grad, wg)
        back_ref[...] += dot_cols(up_grad, wu)

    for part, group in enumerate((part_a, part_b, part_c)):
        for i in group:
            ring.last(i, 2)
        if part < 2:
            @pl.loop(0, 2)
            def _(slot):
                feed(part, slot)
        else:
            feed(part, 0)

    for copy in store_copies(1, 3, 1)[2:] + store_copies(2, 4, 0):
        copy.wait()

    @pl.loop(0, 16)
    def _(to):
        @pl.when(to != ctx)
        def _():
            swap_copy(0, kvown.at[0, pl.ds(0, 128)], kvseq.at[to], to, to).wait_send()
            swap_copy(1, qown.at[0, pl.ds(0, 128)], qseq.at[to], to, to).wait_send()
            swap_copy(2, oseq.at[to], orows.at[to], to, to).wait_send()

    for copy in wide + swaps + ring.started:
        copy.wait_send()


def forward(*arrays):
    shape = jax.ShapeDtypeStruct
    dma = pltpu.SemaphoreType.DMA
    attn = shape((4, 2, 4, 4, 8, D), BF)
    wide = shape((4, 2, 4, 4, 8, HALF), BF)
    rows, heads = shape((ROWS, D), F32), shape((16, 128, 128), BF)
    mats = []
    for part in PARTS:
        mats += [pltpu.VMEM((4, 2, 4, 4, 8, 64 * part), BF)] * 2 + [pltpu.VMEM((4, 4, 4, part, D), BF)]
    raw = shape((8, ROWS, 128), F32)
    both = shape((2 * ROWS, D), F32)
    return pl.pallas_call(
        forward_kernel,
        out_shape=(
            attn, attn, attn, wide, wide, *(shape((4, 4, 4, part, D), BF) for part in PARTS),
            shape((ROWS, D), BF), raw, raw, heads, heads, heads, shape((2, SEQ), F32), shape((ROWS, D), BF), rows, both, both,
        ),
        in_specs=[vmem()] + [hbm()] + [vmem()] * 13,
        out_specs=[vmem()] * 3 + [hbm()] * 5 + [vmem()] * 11,
        scratch_shapes=mats + [pltpu.VMEM((8, ROWS, 128), BF)] * 2 + [pltpu.VMEM((16, 128, 128), BF)] + [pltpu.VMEM((2, ROWS, D), BF)] * 2
        + [pltpu.VMEM((D, 2 * ROWS), BF)] + [pltpu.VMEM((4, 2, 4, 4, 8, FF_BLOCK), BF)] * 2
        + [pltpu.VMEM((2, 4, 4, 16, D), BF), pltpu.VMEM((4, 4, 4, 8, D), BF)]
        + [pltpu.VMEM((8, D), BF)] * 2 + [pltpu.VMEM((2, 8, 64 * part), BF) for part in PARTS for _ in range(2)]
        + [dma((13,)), dma((11,)), dma((11,)), dma((12, 3, 4)), dma((12, 3, 4)), dma((3, 16)), dma((3, 16)), dma((3,)), dma((4,))],
        compiler_params=params(collective_id=0, has_side_effects=True),
    )(*arrays)


class Scatter:
    def __init__(self, at, grads, layouts, bufs, own, fins, send, recv, load):
        self.at, self.grads, self.layouts, self.bufs, self.own, self.fins = at, grads, layouts, bufs, own, fins
        self.send, self.recv, self.load = send, recv, load
        self.started = []

    def copy(self, i, stage, slot, src, dst, to):
        return pltpu.make_async_remote_copy(
            src_ref=src, dst_ref=dst, send_sem=self.send.at[i, stage, slot], recv_sem=self.recv.at[i, stage, slot],
            device_id=to, device_id_type=MESH)

    def start(self, *args):
        copy = self.copy(*args)
        copy.start()
        self.started.append(copy)

    def arrived(self, i, stage, slot, dst):
        self.copy(i, stage, slot, dst, dst, beside(self.at, "x", 1)).wait_recv()

    def lanes(self, i, half):
        width = self.layouts[i].columns // 2
        return pl.ds(half * width, width)

    def source(self, i, stage, by, half):
        lay = self.layouts[i]
        dim, full = lay.order[stage], lay.order[stage + 1 :]
        if stage == 0:
            return self.grads[i].at[lay.index(self.at, full, {dim: (self.at[dim] + by) % 4}, half)]
        kept = [d for d in "yzx" if d in lay.order[stage:]]
        index = [slice(None) if d != dim else (self.at[dim] + by) % 4 for d in kept]
        if lay.kind == "both":
            index.insert(1 if "y" in kept else 0, slice(None))
        return self.bufs[i][2 * stage - 1].at[(0, *index, slice(None), self.lanes(i, half))]

    def parts(self, i, stage):
        halves, near = self.bufs[i][2 * stage], self.bufs[i][2 * stage + 1]
        row = (slice(None),) * (len(near.shape) - 2)
        return halves, near, lambda side, half: near.at[(side, *row, self.lanes(i, half))]

    def in_vmem(self, i, stage):
        return stage > 0 or self.own[i] is None

    def loads(self, i, stage, second):
        steps = ((0, 0, 0), (1, 0, 1)) if second else ((0, 1, 0), (1, 3, 1))
        return [
            pltpu.make_async_copy(self.source(i, stage, by, half), self.own[i].at[k], self.load.at[i, k]) for k, by, half in steps
        ]

    def first(self, i, stage):
        dim = self.layouts[i].order[stage]
        halves, near, part = self.parts(i, stage)
        ahead, behind = beside(self.at, dim, 1), beside(self.at, dim, 3)
        self.start(i, stage, 0, self.source(i, stage, 2, 0), halves.at[0], ahead)
        self.start(i, stage, 1, self.source(i, stage, 2, 1), halves.at[1], behind)
        self.start(i, stage, 2, self.source(i, stage, 1, 1), part(0, 1), ahead)
        self.start(i, stage, 3, self.source(i, stage, 3, 0), part(1, 0), behind)
        if not self.in_vmem(i, stage):
            for copy in self.loads(i, stage, False):
                copy.start()

    def second(self, i, stage):
        dim = self.layouts[i].order[stage]
        halves, near, part = self.parts(i, stage)
        for side, by in ((0, 1), (1, 3)):
            self.arrived(i, stage, side, halves.at[side])
            if self.in_vmem(i, stage):
                mine = self.source(i, stage, by, side)
            else:
                self.loads(i, stage, False)[side].wait()
                mine = self.own[i].at[side]
            add_into(halves.at[side], halves.at[side], mine)
            self.start(i, stage, 4 + side, halves.at[side], part(side, side), beside(self.at, dim, by))
        if not self.in_vmem(i, stage):
            for copy in self.loads(i, stage, True):
                copy.start()

    def last(self, i, stage):
        halves, near, part = self.parts(i, stage)
        self.arrived(i, stage, 2, part(0, 1))
        self.arrived(i, stage, 3, part(1, 0))
        self.arrived(i, stage, 4, part(0, 0))
        self.arrived(i, stage, 5, part(1, 1))
        for half in range(2):
            if self.in_vmem(i, stage):
                mine = self.source(i, stage, 0, half)
            else:
                self.loads(i, stage, True)[half].wait()
                mine = self.own[i].at[half]
            target = part(0, half)
            if stage == 2:
                target = self.fins[i].at[(slice(None),) * (len(self.fins[i].shape) - 1) + (self.lanes(i, half),)]
            add_into(target, part(0, half), part(1, half), mine)


def add_into(target, *terms):
    def body(spot):
        total = terms[0][spot].astype(F32)
        for term in terms[1:]:
            total = total + term[spot].astype(F32)
        target[spot] = total.astype(target.dtype)

    lead = target.shape[:-2]
    count = 1
    for n in lead:
        count *= n
    if count == 1:
        body((0,) * len(lead))
        return

    @pl.loop(0, count)
    def _(flat):
        spot = []
        for n in reversed(lead):
            spot.insert(0, flat % n)
            flat = flat // n
        body(tuple(spot))


def stage_shapes(lay, rows):
    shapes = []
    for stage in range(3):
        left = lay.order[stage + 1 :]
        lead = ([4] if "y" in left else []) + ([2] if lay.kind == "both" else [])
        lead += [4] * (("z" in left) + ("x" in left))
        shapes.append((2, *lead, rows, lay.columns // 2))
        shapes.append((2, *lead, rows, lay.columns))
    return shapes


def norm_back(upstream, gain, unit, factor):
    scaled = upstream * gain
    return factor * (scaled - unit * jnp.mean(scaled * unit, axis=-1, keepdims=True))


GAIN_ROWS = 24


def segment_column(row):
    return jnp.transpose(jnp.broadcast_to(row.astype(F32), (128, row.shape[1])))[:, :1].astype(jnp.int32)


def backward_kernel(*refs):
    (x_ref, m_ref, gain_ref, qgain_ref, kgain_ref, fgain_ref, table_ref, segs_ref, x1_ref, out_hbm, back_hbm,
     full_ref, qseq, kvseq, oseq, inv_ref, h_ref, qraw_ref, kraw_ref, wo_hbm, wq_hbm, wkv_hbm, g_hbm, u_hbm, *d_hbm) = refs[:27]
    (y_ref, yin_ref, q_fin, k_out, v_out, o_fin, g_out, u_out, d_out, attn_gain_out, ffn_gain_out, q_gain_out, k_gain_out) = refs[27:40]
    (gq, gkv, go, out_own, back_own, out_other, back_other, do_own, do_seq, dq_own, dkv_own, dq_in, dkv_in, acc, dq_full, dkv_full,
     gains, gain_slots, wide_g, wide_u, first_mat, second_mat) = refs[40:62]
    cores = refs[62:65]
    own = [None, None, None, *refs[65:70]]
    bufs = [refs[70 + 6 * i : 76 + 6 * i] for i in range(8)]
    (core_send, core_recv, local_sem, send, recv, load_sem, swap_send, swap_recv, swap_local, gain_send, gain_recv) = refs[118:129]
    kv_fin, g_fin, u_fin, *d_fins, segcol_ref = refs[129:136]
    at = place()
    c = at["c"]
    dp, ctx = lax.axis_index("dp"), lax.axis_index("ctx")
    partner = device(at, c=1 - c)
    barrier = pltpu.get_barrier_semaphore()
    for to in (partner, beside(at, "y", 1), beside(at, "y", 3)):
        pl.semaphore_signal(barrier, inc=1, device_id=to, device_id_type=MESH)

    @pl.loop(1, 16)
    def _(step):
        pl.semaphore_signal(barrier, inc=1, device_id=(dp, (ctx + step) % 16), device_id_type=MESH)

    def core_copy(slot, src, dst):
        return pltpu.make_async_remote_copy(
            src_ref=src, dst_ref=dst, send_sem=core_send.at[slot], recv_sem=core_recv.at[slot], device_id=partner,
            device_id_type=MESH)

    rows_own, rows_other = pl.ds(0, ROWS), pl.ds(ROWS, ROWS)
    stays = [
        pltpu.make_async_copy(back_hbm.at[rows_own], back_own, local_sem.at[0]),
        pltpu.make_async_copy(out_hbm.at[rows_own], out_own, local_sem.at[1]),
        pltpu.make_async_copy(wo_hbm, first_mat, local_sem.at[2]),
        pltpu.make_async_copy(wkv_hbm, second_mat, local_sem.at[3]),
    ]
    for copy in stays:
        copy.start()
    pl.semaphore_wait(barrier, 18)
    swaps = [core_copy(0, back_hbm.at[rows_other], back_other), core_copy(1, out_hbm.at[rows_other], out_other)]
    for copy in swaps:
        copy.start()
    fins = [q_fin, kv_fin, o_fin, wide_g, wide_u, *d_fins]
    ring = Scatter(at, [gq, gkv, go, g_hbm, u_hbm, *d_hbm], scatter_layouts(), bufs, own, fins, send, recv, load_sem)
    attn, feed_mats = (0, 1, 2), (3, 4, 5, 6, 7)
    for i in feed_mats:
        ring.first(i, 0)

    for copy in stays:
        copy.wait()
    swaps[0].wait()
    residual = x1_ref[...]
    gain = fgain_ref[...]
    _, unit, factor = norm(residual, gain)
    upstream = back_own[...] + back_other[...]
    for k in range(8):
        gains[8 + k : 9 + k, :] = jnp.sum(upstream[:, k * 128 : (k + 1) * 128] * unit[:, k * 128 : (k + 1) * 128], axis=0, keepdims=True)
    dx1 = m_ref[...].astype(F32) + norm_back(upstream, gain, unit, factor)
    back_own[...] = dx1
    do = dot_cols(dx1.astype(BF), first_mat[...].reshape(D, D)).astype(BF)
    for s in range(2):
        for h in range(8):
            do_own[s * 8 + h] = do[s * 128 : (s + 1) * 128, h * 128 : (h + 1) * 128]
    query_mat = pltpu.make_async_copy(wq_hbm, first_mat, local_sem.at[4])
    query_mat.start()

    def swap_copy(k, src, dst, to, slot):
        return pltpu.make_async_remote_copy(
            src_ref=src, dst_ref=dst, send_sem=swap_send.at[k, to], recv_sem=swap_recv.at[k, slot], device_id=(dp, to),
            device_id_type=MESH)

    def swap_start(k, src, dst, to):
        @pl.when(to != ctx)
        def _():
            swap_copy(k, src.at[to], dst.at[ctx], to, ctx).start()

        @pl.when(to == ctx)
        def _():
            pltpu.make_async_copy(src.at[to], dst.at[ctx], swap_local.at[k]).start()

    def swap_wait(k, src, dst, source):
        @pl.when(source != ctx)
        def _():
            swap_copy(k, dst.at[source], dst.at[source], source, source).wait_recv()

        @pl.when(source == ctx)
        def _():
            pltpu.make_async_copy(src.at[ctx], dst.at[ctx], swap_local.at[k]).wait()

    @pl.loop(0, 16)
    def _(step):
        swap_start(0, do_own, do_seq, (ctx + step) % 16)

    acc[...] = jnp.zeros_like(acc)
    sequence = pl.ds(ctx // 8, 1)
    for k in range(SEQ // BLOCK):
        rows = slice(k * BLOCK, (k + 1) * BLOCK)
        segcol_ref[rows, :] = segment_column(segs_ref[sequence, rows])
    swaps[1].wait()
    y_ref[...] = (residual + out_own[...] + out_other[...]).astype(BF)

    def rows_gradient(grad, left, right):
        @pl.loop(0, 4)
        def _(y):
            cols = pl.ds(pl.multiple_of(y * 256, 256), 256)
            value = dot_rows(left[:, cols], right[...])
            grad[y] = value.reshape(2, 4, 4, 8, D).astype(BF)

    dq_full[...] = back_own[...].astype(BF)
    rows_gradient(go, full_ref, dq_full)
    swaps.append(core_copy(2, go.at[:, 1 - c], cores[2]))
    swaps[2].start()

    low_lane = lanes((BLOCK, 128)) < HDIM
    pick = (lax.broadcasted_iota(jnp.int32, (8, 128), 0) == lanes((8, 128)) // HDIM).astype(BF)

    def queries(block):
        swap_wait(0, do_own, do_seq, 2 * block)
        swap_wait(0, do_own, do_seq, 2 * block + 1)
        pair = pl.ds(2 * block, 2)
        rows = pl.ds(pl.multiple_of(block * BLOCK, BLOCK), BLOCK)
        q = qseq[pair].reshape(BLOCK, 128).astype(F32)
        do = do_seq[pair].reshape(BLOCK, 128).astype(F32)
        product = do * oseq[pair].reshape(BLOCK, 128).astype(F32)
        stacked = jnp.concatenate([jnp.where(low_lane, q, 0.0), jnp.where(low_lane, pltpu.roll(q, HDIM, 1), 0.0)], axis=0).astype(BF)
        above = jnp.concatenate([jnp.where(low_lane, 0.0, pltpu.roll(do, HDIM, 1)), jnp.where(low_lane, 0.0, do)], axis=0).astype(BF)
        high = product.astype(BF)
        rest = (product - high.astype(F32)).astype(BF)
        sums = dot_cols(pick, high) + dot_cols(pick, rest)
        row_dots = jnp.concatenate([sums[0:1], sums[1:2]], axis=1)
        inv = jnp.concatenate([inv_ref[0:1, rows], inv_ref[1:2, rows]], axis=1)
        seg_q = segs_ref[sequence, rows]
        seg_q = jnp.concatenate([seg_q, seg_q], axis=1)

        def part(j, total, diagonal):
            kv = kvseq[pl.ds(2 * j, 2)].reshape(BLOCK, 128)
            scores = dot_cols(kv, stacked)
            slopes = dot_cols(kv, above)
            allowed = segcol_ref[pl.ds(pl.multiple_of(j * BLOCK, BLOCK), BLOCK), :] == seg_q
            if diagonal:
                key = lax.broadcasted_iota(jnp.int32, (BLOCK, 2 * BLOCK), 0)
                allowed = allowed & (lanes((BLOCK, 2 * BLOCK)) % BLOCK >= key)
            weights = jnp.where(allowed, jnp.exp2(scores * SCALE2), 0.0) * inv
            change = (weights * (slopes - row_dots)).astype(BF)
            acc[j] = acc[j] + dot(change, stacked) * HDIM**-0.5 + dot(weights.astype(BF), above)
            return total + dot_rows(change, kv)

        total = lax.fori_loop(0, block, lambda j, t: part(j, t, False), jnp.zeros((2 * BLOCK, 128), F32))
        total = part(block, total, True)
        both = jnp.where(low_lane, total[:BLOCK], pltpu.roll(total[BLOCK:], HDIM, 1)) * HDIM**-0.5
        dq_own[pair] = both.astype(BF).reshape(2, 128, 128)
        dkv_own[pair] = acc[block].astype(BF).reshape(2, 128, 128)
        for k in range(2):
            swap_start(1, dkv_own, dkv_in, 2 * block + k)
            swap_start(2, dq_own, dq_in, 2 * block + k)

    @pl.loop(0, 5)
    def _(step):
        queries(7 - step)

    for i in feed_mats:
        ring.second(i, 0)

    @pl.loop(5, 8)
    def _(step):
        queries(7 - step)

    cosine, sine = rope_of(table_ref)
    qgain, kgain = twice(qgain_ref), twice(kgain_ref)
    head_sums = head_sum_matrix()
    wide_lane = lanes((ROWS, 128)) < HDIM

    def head_back(raw, upstream, gain):
        factor = lax.rsqrt(split_dot(raw * raw, head_sums) * (1.0 / HDIM) + EPSILON)
        unit = raw * factor
        turned = upstream * cosine - turn(upstream) * sine
        scaled = turned * gain
        mean = split_dot(scaled * unit, head_sums) * (1.0 / HDIM)
        return factor * (scaled - unit * mean), jnp.sum(turned * unit, axis=0, keepdims=True)

    @pl.loop(0, 16)
    def _(source):
        swap_wait(1, dkv_own, dkv_in, source)
        swap_wait(2, dq_own, dq_in, source)

    qterms = jnp.zeros((1, 128), F32)
    kterms = jnp.zeros((1, 128), F32)
    for h in range(8):
        cols = slice(h * 128, (h + 1) * 128)
        upstream = jnp.concatenate([dq_in[h], dq_in[8 + h]], axis=0).astype(F32)
        pre, terms = head_back(qraw_ref[h], upstream, qgain)
        qterms = qterms + terms
        dq_full[:, cols] = pre.astype(BF)
        upstream = jnp.concatenate([dkv_in[h], dkv_in[8 + h]], axis=0).astype(F32)
        pre, terms = head_back(kraw_ref[h], upstream, kgain)
        kterms = kterms + terms
        dkv_full[:, cols] = jnp.where(wide_lane, pre, upstream).astype(BF)
    gains[16:17, :] = qterms
    gains[17:18, :] = kterms
    gains[18:24, :] = jnp.zeros((6, 128), F32)
    rows_gradient(gq, h_ref, dq_full)
    swaps.append(core_copy(3, gq.at[:, 1 - c], cores[0]))
    swaps[3].start()
    rows_gradient(gkv, h_ref, dkv_full)
    swaps.append(core_copy(4, gkv.at[:, 1 - c], cores[1]))
    swaps[4].start()
    for i in feed_mats:
        ring.last(i, 0)
        ring.first(i, 1)
    for slot, i in ((2, 2), (3, 0), (4, 1)):
        swaps[slot].wait_recv()
        mine = ring.grads[i].at[:, c]
        add_into(mine, mine, cores[i])
        ring.first(i, 0)

    query_mat.wait()
    dh = dot_cols(dq_full[...], first_mat[...].reshape(D, D)) + dot_cols(dkv_full[...], second_mat[...].reshape(D, D))
    gain = gain_ref[...]
    _, unit, factor = norm(x_ref[...].astype(F32), gain)
    for k in range(8):
        gains[k : k + 1, :] = jnp.sum(dh[:, k * 128 : (k + 1) * 128] * unit[:, k * 128 : (k + 1) * 128], axis=0, keepdims=True)
    yin_ref[...] = (back_own[...] + norm_back(dh, gain, unit, factor)).astype(BF)

    started = []

    def gain_copy(stage, slot, index, to):
        ref = gain_slots.at[stage, index]
        return pltpu.make_async_remote_copy(
            src_ref=ref, dst_ref=ref, send_sem=gain_send.at[stage, slot], recv_sem=gain_recv.at[stage, slot], device_id=to,
            device_id_type=MESH)

    def gain_start(stage, slot, index, to):
        copy = gain_copy(stage, slot, index, to)
        copy.start()
        started.append(copy)

    def gain_first(stage, total):
        dim = "xyz"[stage]
        p = at[dim]
        gain_slots[stage, p] = total
        gain_start(stage, 0, p, beside(at, dim, 1))
        gain_start(stage, 1, p, beside(at, dim, 3))

    def gain_second(stage):
        dim = "xyz"[stage]
        before = (at[dim] + 3) % 4
        gain_copy(stage, 0, before, partner).wait_recv()
        gain_start(stage, 2, before, beside(at, dim, 1))

    def gain_last(stage):
        dim = "xyz"[stage]
        gain_copy(stage, 1, (at[dim] + 1) % 4, partner).wait_recv()
        gain_copy(stage, 2, (at[dim] + 2) % 4, partner).wait_recv()
        return gain_slots[stage, 0] + gain_slots[stage, 1] + gain_slots[stage, 2] + gain_slots[stage, 3]

    gain_first(0, gains[...])
    for i in attn:
        ring.second(i, 0)
    gain_second(0)
    for i in feed_mats:
        ring.second(i, 1)
    for i in attn:
        ring.last(i, 0)
        ring.first(i, 1)
    gain_first(1, gain_last(0))
    for i in feed_mats:
        ring.last(i, 1)
        ring.first(i, 2)
    for i in attn:
        ring.second(i, 1)
    gain_second(1)
    for i in feed_mats:
        ring.second(i, 2)
    for i in attn:
        ring.last(i, 1)
        ring.first(i, 2)
    gain_first(2, gain_last(1))
    finals = []
    for i in feed_mats:
        ring.last(i, 2)
        if i < 5:
            wide, fin = ring.fins[i], (g_fin, u_fin)[i - 3]
            finals.append(core_copy(2 + i, wide.at[1 - c], fin.at[c]))
            finals[-1].start()
            fin[c] = wide[c]
    for i in attn:
        ring.second(i, 2)
    gain_second(2)
    for i in attn:
        ring.last(i, 2)
    gain_slots[3, c] = gain_last(2)
    finals.append(core_copy(7, gain_slots.at[3, c], gain_slots.at[3, c]))
    finals[-1].start()
    for slot, fin in ((5, g_fin), (6, u_fin)):
        core_copy(slot, fin.at[1 - c], fin.at[1 - c]).wait_recv()
    columns = []
    for y in range(4):
        for fin in (g_fin, u_fin):
            columns.append(jnp.concatenate([fin[core, :, start : start + width] for core in range(2) for _, start, width in part_columns(y)], axis=1))
    columns = jnp.concatenate(columns, axis=0)
    high = columns.astype(BF)
    rest = (columns - high.astype(F32)).astype(BF)
    sources = unit_sources()
    for k in range(9):
        matrix = spread_matrix(k, sources)
        units = dot_cols(high, matrix) + dot_cols(rest, matrix)
        for y in range(4):
            where = slice(y * 1152 + k * 128, y * 1152 + (k + 1) * 128)
            g_out[:, where] = units[16 * y : 16 * y + 8]
            u_out[:, where] = units[16 * y + 8 : 16 * y + 16]
    core_copy(7, gain_slots.at[3, 1 - c], gain_slots.at[3, 1 - c]).wait_recv()
    total = gain_slots[3, 0] + gain_slots[3, 1]
    attn_gain_out[...] = total[:8]
    ffn_gain_out[...] = total[8:16]
    q_gain_out[...] = (total[16:17] + pltpu.roll(total, HDIM, 1)[16:17])[:, :HDIM]
    k_gain_out[...] = total[17:18, :HDIM]
    low_half = lanes((8, 128)) < HDIM
    for k in range(4):
        even, odd = kv_fin[:, k * 256 : k * 256 + 128], kv_fin[:, k * 256 + 128 : (k + 1) * 256]
        k_out[:, k * 128 : (k + 1) * 128] = jnp.where(low_half, even, pltpu.roll(odd, HDIM, 1))
        v_out[:, k * 128 : (k + 1) * 128] = jnp.where(low_half, pltpu.roll(even, HDIM, 1), odd)
    d_out[0:16, :] = d_fins[0][...]
    d_out[16:32, :] = d_fins[1][...]
    d_out[32:36, :] = d_fins[2][0:4, :]

    @pl.loop(0, 16)
    def _(to):
        @pl.when(to != ctx)
        def _():
            swap_copy(0, do_own.at[to], do_seq.at[to], to, to).wait_send()
            swap_copy(1, dkv_own.at[to], dkv_in.at[to], to, to).wait_send()
            swap_copy(2, dq_own.at[to], dq_in.at[to], to, to).wait_send()

    for copy in swaps[2:] + finals + started + ring.started:
        copy.wait_send()


def backward(*arrays):
    shape = jax.ShapeDtypeStruct
    dma = pltpu.SemaphoreType.DMA
    small = shape((8, D), F32)
    block = pltpu.VMEM((16, 128, 128), BF)
    own = pltpu.VMEM((ROWS, D), F32)
    scratch = [pltpu.VMEM((4, 2, 4, 4, 8, D), BF)] * 3 + [own] * 4 + [block] * 6
    scratch += [pltpu.VMEM((SEQ // BLOCK, BLOCK, 128), F32)] + [pltpu.VMEM((ROWS, D), BF)] * 2
    scratch += [pltpu.VMEM((GAIN_ROWS, 128), F32), pltpu.VMEM((4, 4, GAIN_ROWS, 128), F32)] + [pltpu.VMEM((2, 8, HALF), F32)] * 2
    scratch += [pltpu.VMEM((4, 2, 4, 4, 8, D), BF)] * 2 + [pltpu.VMEM((4, 4, 4, 8, D), BF)] * 3
    shapes = [stage_shapes(lay, rows) for lay, rows in zip(scatter_layouts(), (8,) * 5 + PARTS)]
    scratch += [pltpu.VMEM(shapes[i][0], BF) for i in range(3, 8)]
    for group in shapes:
        scratch += [pltpu.VMEM(s, BF) for s in group]
    scratch += [
        dma((8,)), dma((8,)), dma((5,)), dma((8, 3, 6)), dma((8, 3, 6)), dma((8, 2)), dma((3, 16)), dma((3, 16)), dma((3,)), dma((3, 3)),
        dma((3, 3)),
    ]
    scratch += [pltpu.VMEM((8, D), F32)] + [pltpu.VMEM((2, 8, HALF), F32)] * 2 + [pltpu.VMEM((part, D), F32) for part in PARTS]
    scratch += [pltpu.VMEM((SEQ, 1), jnp.int32)]
    return pl.pallas_call(
        backward_kernel,
        out_shape=(
            shape((ROWS, D), BF), shape((ROWS, D), BF), small, shape((8, D // 2), F32), shape((8, D // 2), F32), small, shape((8, 4608), F32),
            shape((8, 4608), F32), shape((36, D), F32), shape((8, 128), F32), shape((8, 128), F32), shape((1, HDIM), F32),
            shape((1, HDIM), F32),
        ),
        in_specs=[vmem()] * 9 + [hbm()] * 2 + [vmem()] * 8 + [hbm()] * 8,
        out_specs=[vmem()] * 13,
        scratch_shapes=scratch,
        compiler_params=params(collective_id=1, has_side_effects=True),
    )(*arrays)


def results_kernel(*refs):
    count = len(refs) // 2
    for source, target in zip(refs[:count], refs[count:]):
        target[...] = source[...]


def results(arrays):
    return pl.pallas_call(
        results_kernel,
        out_shape=tuple(jax.ShapeDtypeStruct(a.shape, a.dtype) for a in arrays),
        in_specs=[vmem()] * len(arrays),
        out_specs=[vmem()] * len(arrays),
        compiler_params=params(),
    )(*arrays)


def rope_table(first_row):
    places = first_row + lax.broadcasted_iota(jnp.int32, (128, 128), 0)
    lane = lax.broadcasted_iota(jnp.int32, (128, 128), 1)
    frequency = THETA_BASE ** (-2.0 * (lane % (HDIM // 2)).astype(F32) / HDIM)
    angles = places.astype(F32) * frequency
    return jnp.where(lane < HDIM, jnp.cos(angles), jnp.sin(angles))


def local(block_in, segment_ids, attn_gain, w_query, w_key, w_value, query_gain, key_gain, w_out, ffn_gain, w_gate, w_up, w_down, out_grad):
    x = block_in.reshape(ROWS, D)
    m = out_grad.reshape(ROWS, D)
    row = lambda v: v.reshape(1, -1)
    gains = row(attn_gain), row(query_gain), row(key_gain), row(ffn_gain)
    table = rope_table(lax.axis_index("ctx") * 128)
    (wq, wkv, wo, gg, gu, gda, gdb, gdc, h1, qraw, kraw, q, kv, o, inv, attended, x1, out, back) = forward(
        x, m, *gains, table, segment_ids, w_query, w_key, w_value, w_out, w_gate, w_up, w_down)
    y, y_in, gq, gk, gv, gout, gg, gu, gd, attn_terms, ffn_terms, q_terms, k_terms = results(backward(
        x, m, *gains, table, segment_ids, x1, out, back, attended, q, kv, o, inv, h1, qraw, kraw, wo, wq, wkv, gg, gu, gda, gdb, gdc))
    return (
        y.reshape(2, 128, D), y_in.reshape(2, 128, D), gq, gk, gv, gout, gg, gu, gd, attn_terms.reshape(D), q_terms.reshape(HDIM),
        k_terms.reshape(HDIM), ffn_terms.reshape(D),
    )


def solution(mesh):
    both = P(("dp", "ctx"), None)
    acts = P("dp", "ctx", None)
    return jax.shard_map(
        local,
        mesh=mesh,
        in_specs=(acts, P("dp", None), P(), both, both, both, P(), P(), both, P(), both, both, both, acts),
        out_specs=(acts, acts, both, both, both, both, both, both, both, P(), P(), P(), P()),
        check_vma=False,
    )
```

```python
import functools

import jax
import jax.numpy as jnp
from jax import lax
from jax.experimental import pallas as pl
from jax.experimental.pallas import tpu as pltpu
from jax.sharding import PartitionSpec as P

MESH = pl.DeviceIdType.MESH
BF = jnp.bfloat16
F32 = jnp.float32

D = 1024
HDIM = 64
HEADS = 8
ROWS = 256
SEQ = 2048
UNITS = (16, 16, 4)
DOWN_ROWS = (16, 16, 8)
HALF = 64 * sum(UNITS)
EPSILON = 1e-05
THETA_BASE = 1000000.0
LOG2E = 1.4426950408889634
VMEM_MOST = 60 * 1024 * 1024


def params(**more):
    return pltpu.CompilerParams(vmem_limit_bytes=VMEM_MOST, **more)


def vmem():
    return pl.BlockSpec(memory_space=pltpu.VMEM)


def hbm():
    return pl.BlockSpec(memory_space=pl.ANY)


def dot(left, right):
    return lax.dot_general(left, right, (((1,), (0,)), ((), ())), preferred_element_type=F32)


def dot_rows(left, right):
    return lax.dot_general(left, right, (((0,), (0,)), ((), ())), preferred_element_type=F32)


def dot_cols(left, right):
    return lax.dot_general(left, right, (((1,), (1,)), ((), ())), preferred_element_type=F32)


def place():
    dp, ctx = lax.axis_index("dp"), lax.axis_index("ctx")
    return {"y": dp // 2, "c": dp % 2, "z": ctx // 4, "x": ctx % 4}


def device(at, **moved):
    spot = dict(at)
    spot.update(moved)
    return (spot["y"] * 2 + spot["c"], spot["z"] * 4 + spot["x"])


def beside(at, dim, by):
    return device(at, **{dim: (at[dim] + by) % 4})


ORDERS = (("x", "z", "y"), ("y", "x", "z"), ("z", "y", "x"))


class Layout:
    def __init__(self, kind, order, columns):
        self.kind, self.order, self.columns = kind, order, columns

    def index(self, at, full, fixed=None, half=None):
        spot = dict(at)
        if fixed:
            spot.update(fixed)
        ids = {d: (slice(None) if d in full else spot[d]) for d in "xyz"}
        c = {"own": at["c"], "both": slice(None), "none": None}[self.kind]
        out = [ids["y"]] + ([] if c is None else [c]) + [ids["z"], ids["x"], slice(None)]
        if half is None:
            out.append(slice(None))
        else:
            out.append(pl.ds(half * (self.columns // 2), self.columns // 2))
        return tuple(out)


class Gather:
    def __init__(self, at, arrays, layouts, send, recv):
        self.at, self.arrays, self.layouts, self.send, self.recv = at, arrays, layouts, send, recv
        self.started = []

    def copy(self, i, stage, slot, index, to):
        ref = self.arrays[i].at[index]
        return pltpu.make_async_remote_copy(
            src_ref=ref, dst_ref=ref, send_sem=self.send.at[i, stage, slot], recv_sem=self.recv.at[i, stage, slot],
            device_id=to, device_id_type=MESH)

    def start(self, i, stage, slot, index, to):
        copy = self.copy(i, stage, slot, index, to)
        copy.start()
        self.started.append(copy)

    def slab(self, i, stage, by, half=None):
        lay = self.layouts[i]
        dim, full = lay.order[stage], lay.order[:stage]
        return lay.index(self.at, full, {dim: (self.at[dim] + by) % 4}, half)

    def first(self, i, stage):
        dim = self.layouts[i].order[stage]
        self.start(i, stage, 0, self.slab(i, stage, 0), beside(self.at, dim, 1))
        self.start(i, stage, 1, self.slab(i, stage, 0), beside(self.at, dim, 3))

    def arrived(self, i, stage, slot, by, half):
        self.copy(i, stage, slot, self.slab(i, stage, by, half), beside(self.at, "x", 1)).wait_recv()

    def second(self, i, stage):
        dim = self.layouts[i].order[stage]
        self.arrived(i, stage, 0, 3, None)
        self.start(i, stage, 2, self.slab(i, stage, 3, 0), beside(self.at, dim, 1))
        self.arrived(i, stage, 1, 1, None)
        self.start(i, stage, 3, self.slab(i, stage, 1, 1), beside(self.at, dim, 3))

    def last(self, i, stage):
        self.arrived(i, stage, 2, 2, 0)
        self.arrived(i, stage, 3, 2, 1)


def attn_layouts():
    return [Layout("own", ORDERS[0], D), Layout("own", ORDERS[1], D), Layout("own", ORDERS[2], D)]


def gather_layouts():
    shapes = attn_layouts()
    for units in UNITS:
        shapes += [Layout("both", ORDERS[0], 64 * units), Layout("both", ORDERS[1], 64 * units), Layout("none", ORDERS[2], D)]
    return shapes


def scatter_layouts():
    wide = [Layout("both", ORDERS[0], HALF), Layout("both", ORDERS[1], HALF)]
    return attn_layouts() + wide + [Layout("none", ORDERS[2], D)] * 3


def lanes(shape):
    return lax.broadcasted_iota(jnp.int32, shape, len(shape) - 1)


def norm(values, gain):
    factor = lax.rsqrt(jnp.mean(values * values, axis=-1, keepdims=True) + EPSILON)
    unit = values * factor
    return unit * gain, unit, factor


def split_dot(values, matrix):
    high = values.astype(BF)
    low = (values - high.astype(F32)).astype(BF)
    return dot(high, matrix) + dot(low, matrix)


def head_sum_matrix():
    rows = lax.broadcasted_iota(jnp.int32, (128, 128), 0) // HDIM
    return (rows == lanes((128, 128)) // HDIM).astype(BF)


def turn(values):
    low = lanes(values.shape) % HDIM < HDIM // 2
    ahead = pltpu.roll(values, 128 - HDIM // 2, 1)
    behind = pltpu.roll(values, HDIM // 2, 1)
    return jnp.where(low, -ahead, behind)


BLOCK = 256
SCALE2 = LOG2E * HDIM**-0.5


def heads_to_rows(ref):
    parts = [jnp.concatenate([ref[s * 8 + h] for h in range(8)], axis=1) for s in range(2)]
    return jnp.concatenate(parts, axis=0)


def unit_sources():
    column = lax.broadcasted_iota(jnp.int32, (1, 1152), 1)
    last = column >= 1024
    k = column - 1024
    core = jnp.where(last, k // 64, (column // 256) % 2)
    ctx = jnp.where(last, (k % 64) // 4, (column % 256) // 16)
    unit = jnp.where(last, 32 + column % 4, 16 * (column // 512) + column % 16)
    return core * 576 + ctx * 36 + unit


def spread_matrix(k, sources):
    rows = lax.broadcasted_iota(jnp.int32, (128, 1152), 0) + 128 * k
    return jnp.where(rows == sources, 1.0, 0.0).astype(BF)


def four_of_eight():
    rows = lax.broadcasted_iota(jnp.int32, (256, 512), 0)
    return jnp.where(lanes((256, 512)) == rows // 4 * 8 + rows % 4, 1.0, 0.0).astype(BF)


def low_pair(first, second):
    return jnp.where(lanes(first.shape) < HDIM, first, pltpu.roll(second, HDIM, 1))


def high_pair(first, second):
    return jnp.where(lanes(first.shape) < HDIM, pltpu.roll(first, HDIM, 1), second)


FF_BLOCK = 512


def rope_of(table_ref):
    table = table_ref[...]
    low, turned = lanes(table.shape) < HDIM, pltpu.roll(table, HDIM, 1)
    cosine, sine = jnp.where(low, table, turned), jnp.where(low, turned, table)
    return jnp.concatenate([cosine, cosine], axis=0), jnp.concatenate([sine, sine], axis=0)


def twice(gain_ref):
    return jnp.concatenate([gain_ref[...], gain_ref[...]], axis=1)


def forward_kernel(*refs):
    (x_ref, m_ref, gain_ref, qgain_ref, kgain_ref, fgain_ref, table_ref, segs_ref, q_in, k_in, v_in,
     o_in, gate_in, up_in, down_in) = refs[:15]
    (wq8, wkv8, wo8, g_grad, u_grad, d_grad_a, d_grad_b, d_grad_c, h_ref, qraw_ref, kraw_ref, qseq, kvseq, oseq, inv_ref, full_ref, x1_ref,
     out_ref, back_ref) = refs[15:34]
    mats = refs[34:43]
    (qown, kvown, orows, h2_ref, m2_ref, turned, g_stage, u_stage, d_stage, d_stage_c, kv_in, down_pad, *wide_shards) = refs[43:61]
    (local_sem, core_send, core_recv, send, recv, swap_send, swap_recv, swap_local, store_sem) = refs[61:70]
    d_grads = (d_grad_a, d_grad_b, d_grad_c)
    at = place()
    c = at["c"]
    dp, ctx = lax.axis_index("dp"), lax.axis_index("ctx")
    partner = device(at, c=1 - c)
    barrier = pltpu.get_barrier_semaphore()
    for to in (partner, beside(at, "y", 1), beside(at, "y", 3)):
        pl.semaphore_signal(barrier, inc=1, device_id=to, device_id_type=MESH)

    @pl.loop(1, 16)
    def _(step):
        pl.semaphore_signal(barrier, inc=1, device_id=(dp, (ctx + step) % 16), device_id_type=MESH)

    sequence = pl.ds(ctx // 8, 1)
    here = (at["y"], c, at["z"], at["x"])
    ring = Gather(at, [wq8, wkv8, wo8, *mats], gather_layouts(), send, recv)
    attn, part_a, part_b, part_c = (0, 1, 2), (3, 4, 5), (6, 7, 8), (9, 10, 11)

    def core_copy(slot, src, dst):
        return pltpu.make_async_remote_copy(
            src_ref=src, dst_ref=dst, send_sem=core_send.at[slot], recv_sem=core_recv.at[slot], device_id=partner,
            device_id_type=MESH)

    low_half = lanes((8, 128)) < HDIM
    for k in range(4):
        key, value = (ref[:, k * 128 : (k + 1) * 128].astype(F32) for ref in (k_in, v_in))
        kv_in[:, k * 256 : k * 256 + 128] = jnp.where(low_half, key, pltpu.roll(value, HDIM, 1)).astype(BF)
        kv_in[:, k * 256 + 128 : (k + 1) * 256] = jnp.where(low_half, pltpu.roll(key, HDIM, 1), value).astype(BF)
    stays = [pltpu.make_async_copy(src, dst.at[here], local_sem.at[i]) for i, (src, dst) in enumerate(((q_in, wq8), (kv_in, wkv8), (o_in, wo8)))]
    for copy in stays:
        copy.start()
    for copy in stays:
        copy.wait()
    pl.semaphore_wait(barrier, 18)
    for i in attn:
        ring.first(i, 0)
    upstream_copy = core_copy(6, m_ref, m2_ref.at[1])
    upstream_copy.start()

    sources = unit_sources()
    units = jnp.concatenate(
        [ref[:, y * 1152 : (y + 1) * 1152].astype(F32) for y in range(4) for ref in (gate_in, up_in)], axis=0).astype(BF)
    spread = jnp.zeros((64, 1152), F32)
    for k in range(9):
        spread = spread + dot(units[:, k * 128 : (k + 1) * 128], spread_matrix(k, sources))
    for j in range(2):
        blocks = [spread[16 * y + 8 * j : 16 * y + 8 * j + 8] for y in range(4)]
        for core in range(2):
            for part in range(2):
                start = part * 512 + core * 256
                for y in range(4):
                    wide_shards[2 * part + j][core, :, y * 256 : (y + 1) * 256] = blocks[y][:, start : start + 256].astype(BF)
            for k in range(2):
                pair = (low_pair, high_pair)[core](blocks[2 * k][:, 1024:], blocks[2 * k + 1][:, 1024:])
                wide_shards[4 + j][core, :, k * 128 : (k + 1) * 128] = pair.astype(BF)
    down_pad[...] = jnp.concatenate([down_in[32:36, :].astype(F32), jnp.zeros((4, D), F32)], axis=0).astype(BF)
    downs = (down_in.at[pl.ds(0, 16)], down_in.at[pl.ds(16, 16)], down_pad)
    stays = []
    wide = []
    for k in range(3):
        for j in range(2):
            stays.append(pltpu.make_async_copy(wide_shards[2 * k + j].at[c], mats[3 * k + j].at[here], local_sem.at[3 + 3 * k + j]))
            wide.append(core_copy(2 * k + j, wide_shards[2 * k + j].at[1 - c], mats[3 * k + j].at[here]))
        stays.append(pltpu.make_async_copy(downs[k], mats[3 * k + 2].at[at["y"], at["z"], at["x"]], local_sem.at[5 + 3 * k]))
    stays.append(pltpu.make_async_copy(m_ref, m2_ref.at[0], local_sem.at[12]))
    for copy in wide + stays:
        copy.start()
    normed, _, _ = norm(x_ref[...].astype(F32), gain_ref[...])
    h_ref[...] = normed.astype(BF)
    for copy in stays:
        copy.wait()
    for copy in wide:
        copy.wait_recv()
    for i in part_a + part_b + part_c:
        ring.first(i, 0)

    def second(group, stage):
        for i in group:
            ring.second(i, stage)

    def following(group, stage):
        for i in group:
            ring.last(i, stage)
            ring.first(i, stage + 1)

    second(attn, 0)
    following(attn, 0)
    second(part_a, 0)
    second(attn, 1)
    following(part_a, 0)
    following(attn, 1)
    second(part_b + part_c, 0)
    second(part_a, 1)
    second(attn, 2)
    following(part_b + part_c, 0)
    swaps = []
    eights = (wq8, wkv8, wo8)
    for i in attn:
        ring.last(i, 2)
        copy = core_copy(7 + i, eights[i].at[:, c], eights[i].at[:, c])
        copy.start()
        swaps.append(copy)

    second(part_b + part_c, 1)

    def other_rows(i):
        core_copy(7 + i, eights[i].at[:, 1 - c], eights[i].at[:, 1 - c]).wait_recv()

    def rows_of(core):
        cols = [h_ref[:, pl.ds(pl.multiple_of((2 * y + core) * 128, 128), 128)] for y in range(4)]
        return jnp.concatenate(cols, axis=1)

    def mat_of(eight, core):
        return eight[:, core].reshape(D // 2, D)

    mine, other = rows_of(c), rows_of(1 - c)
    query = dot(mine, mat_of(wq8, c))
    other_rows(0)
    query = query + dot(other, mat_of(wq8, 1 - c))
    for h in range(8):
        qraw_ref[h] = query[:, h * 128 : (h + 1) * 128]
    other_rows(1)
    key_value = dot(mine, mat_of(wkv8, c)) + dot(other, mat_of(wkv8, 1 - c))
    for h in range(8):
        kraw_ref[h] = key_value[:, h * 128 : (h + 1) * 128]

    sums = head_sum_matrix()
    cosine, sine = rope_of(table_ref)
    qgain, kgain = twice(qgain_ref), twice(kgain_ref)

    def rotated(raw, gain):
        factor = lax.rsqrt(split_dot(raw * raw, sums) * (1.0 / HDIM) + EPSILON)
        unit = raw * factor * gain
        return unit * cosine + turn(unit) * sine

    def swap_copy(k, src, dst, to, slot):
        return pltpu.make_async_remote_copy(
            src_ref=src, dst_ref=dst, send_sem=swap_send.at[k, to], recv_sem=swap_recv.at[k, slot], device_id=(dp, to),
            device_id_type=MESH)

    @pl.loop(0, 8)
    def _(step):
        h = (ctx + step) % 8
        raw = qraw_ref[h]
        qown[h] = rotated(raw, qgain).astype(BF)
        raw = kraw_ref[h]
        kvown[h] = jnp.where(lanes(raw.shape) < HDIM, rotated(raw, kgain), raw).astype(BF)
        for s in range(2):
            to = s * 8 + h
            rows = pl.ds(s * 128, 128)

            @pl.when(to != ctx)
            def _():
                swap_copy(0, kvown.at[h, rows], kvseq.at[ctx], to, ctx).start()
                swap_copy(1, qown.at[h, rows], qseq.at[ctx], to, ctx).start()

            @pl.when(to == ctx)
            def _():
                pltpu.make_async_copy(kvown.at[h, rows], kvseq.at[ctx], swap_local.at[0]).start()
                pltpu.make_async_copy(qown.at[h, rows], qseq.at[ctx], swap_local.at[1]).start()

    other_rows(2)
    following(part_a, 1)
    low_lane = lanes((BLOCK, 128)) < HDIM

    def arrive(source):
        @pl.when(source != ctx)
        def _():
            swap_copy(0, kvseq.at[source], kvseq.at[source], source, source).wait_recv()
            swap_copy(1, qseq.at[source], qseq.at[source], source, source).wait_recv()

        @pl.when(source == ctx)
        def _():
            pltpu.make_async_copy(kvown.at[0, pl.ds(0, 128)], kvseq.at[ctx], swap_local.at[0]).wait()
            pltpu.make_async_copy(qown.at[0, pl.ds(0, 128)], qseq.at[ctx], swap_local.at[1]).wait()

    def queries(block):
        arrive(2 * block)
        arrive(2 * block + 1)
        q = qseq[pl.ds(2 * block, 2)].reshape(BLOCK, 128)
        zero = jnp.zeros_like(q)
        second = pltpu.roll(q.astype(F32), HDIM, 1).astype(BF)
        stacked = jnp.concatenate([jnp.where(low_lane, q, zero), jnp.where(low_lane, second, zero)], axis=0)
        rows = pl.ds(pl.multiple_of(block * BLOCK, BLOCK), BLOCK)
        seg_q = segment_column(segs_ref[sequence, rows])
        seg_q = jnp.concatenate([seg_q, seg_q], axis=0)

        def part(j, total, diagonal):
            kv = kvseq[pl.ds(2 * j, 2)].reshape(BLOCK, 128)
            scores = dot_cols(stacked, kv)
            allowed = seg_q == segs_ref[sequence, pl.ds(pl.multiple_of(j * BLOCK, BLOCK), BLOCK)]
            if diagonal:
                query = lax.broadcasted_iota(jnp.int32, (2 * BLOCK, BLOCK), 0) % BLOCK
                allowed = allowed & (query >= lanes((2 * BLOCK, BLOCK)))
            weights = jnp.where(allowed, jnp.exp2(scores * SCALE2), 0.0).astype(BF)
            values = jnp.where(low_lane, jnp.ones_like(kv), kv)
            return total + dot(weights, values)

        total = lax.fori_loop(0, block, lambda j, t: part(j, t, False), jnp.zeros((2 * BLOCK, 128), F32))
        total = part(block, total, True)
        mixed = total / pltpu.roll(total, HDIM, 1)
        first = pltpu.roll(mixed[:BLOCK], HDIM, 1)
        oseq[pl.ds(2 * block, 2)] = jnp.where(low_lane, first, mixed[BLOCK:]).astype(BF).reshape(2, 128, 128)
        inv_ref[0:1, rows] = 1.0 / jnp.transpose(total[:BLOCK])[0:1, :]
        inv_ref[1:2, rows] = 1.0 / jnp.transpose(total[BLOCK:])[0:1, :]
        for k in range(2):
            to = 2 * block + k

            @pl.when(to != ctx)
            def _():
                swap_copy(2, oseq.at[to], orows.at[ctx], to, ctx).start()

            @pl.when(to == ctx)
            def _():
                pltpu.make_async_copy(oseq.at[to], orows.at[ctx], swap_local.at[2]).start()

    queries(0)

    @pl.loop(1, 4)
    def _(block):
        queries(block)

    second(part_a, 2)

    @pl.loop(4, 7)
    def _(block):
        queries(block)

    @pl.loop(7, 8)
    def _(block):
        queries(block)

    following(part_b, 1)

    @pl.loop(0, 16)
    def _(source):
        @pl.when(source != ctx)
        def _():
            swap_copy(2, orows.at[source], orows.at[source], source, source).wait_recv()

        @pl.when(source == ctx)
        def _():
            pltpu.make_async_copy(oseq.at[ctx], orows.at[ctx], swap_local.at[2]).wait()

    attended = heads_to_rows(orows)
    full_ref[...] = attended
    residual = x_ref[...].astype(F32) + dot(attended, wo8[...].reshape(D, D))
    x1_ref[...] = residual
    normed, _, _ = norm(residual, fgain_ref[...])
    h2_ref[0] = normed.astype(BF)
    mid_copy = core_copy(10, h2_ref.at[0], h2_ref.at[1])
    mid_copy.start()
    out_ref[...] = jnp.zeros_like(out_ref)
    back_ref[...] = jnp.zeros_like(back_ref)
    upstream_copy.wait()
    mid_copy.wait()
    turned[...] = jnp.transpose(h2_ref[...].reshape(2 * ROWS, D))

    def store_copies(part, step, slot):
        if part < 2:
            cols = (slice(None),) * 5 + (pl.ds(step * FF_BLOCK, FF_BLOCK),)
            g_part, u_part, down, rows = g_stage, u_stage, d_stage, d_grads[part].at[pl.ds(2 * slot, 2)]
        else:
            cols, less = ((slice(None),) * 5 + (pl.ds(start, 256),) for start in (2048, 0))
            g_part, u_part, down, rows = g_stage.at[less], u_stage.at[less], d_stage_c, d_grads[2]
        return [
            pltpu.make_async_copy(g_part, g_grad.at[cols], store_sem.at[0]),
            pltpu.make_async_copy(u_part, u_grad.at[cols], store_sem.at[1]),
            pltpu.make_async_copy(down, rows, store_sem.at[2 + (part == 2)]),
        ]

    def feed(part, slot):
        gate_mat, up_mat, down_mat = (mats[3 * part + j] for j in range(3))
        step = 2 * part + slot
        width = FF_BLOCK if part < 2 else 256
        cols = pl.ds(slot * width, width)
        wg = gate_mat.reshape(D, 64 * UNITS[part])[:, cols]
        wu = up_mat.reshape(D, 64 * UNITS[part])[:, cols]
        if part < 2:
            wd = down_mat.reshape(64 * UNITS[part], D)[cols, :]
        else:
            wd = dot(four_of_eight(), down_mat[...].reshape(512, D)).astype(BF)
        low, upstream = h2_ref[...].reshape(2 * ROWS, D), m2_ref[...].reshape(2 * ROWS, D)
        gate = dot(low, wg)
        up = dot(low, wu)
        sig = jax.nn.sigmoid(gate)
        silu = gate * sig
        hidden = (silu * up).astype(BF)
        slope = dot_cols(upstream, wd)
        gate_grad = (slope * up * sig * (1.0 + gate * (1.0 - sig))).astype(BF)
        up_grad = (slope * silu).astype(BF)

        def freed():
            g_copy, u_copy, d_copy = store_copies((step - 1) // 2, step - 1, (step - 1) % 2)
            g_copy.wait()
            u_copy.wait()
            if part < 2:
                d_copy.wait()

        if step > 0:
            freed()
        for y in range(0, 4, 2):
            left = turned[y * 256 : (y + 2) * 256, :]
            g_stage[y : y + 2, :, :, :, :, :width] = dot(left, gate_grad).astype(BF).reshape(2, 2, 4, 4, 8, width)
            u_stage[y : y + 2, :, :, :, :, :width] = dot(left, up_grad).astype(BF).reshape(2, 2, 4, 4, 8, width)
        down_grad = dot_rows(hidden, upstream).astype(BF)
        if part < 2:
            d_stage[...] = down_grad.reshape(2, 4, 4, 16, D)
        else:
            d_stage_c[...] = dot_rows(four_of_eight(), down_grad).astype(BF).reshape(4, 4, 4, 8, D)
        for copy in store_copies(part, step, slot):
            copy.start()
        out_ref[...] += dot(hidden, wd)
        back_ref[...] += dot_cols(gate_grad, wg)
        back_ref[...] += dot_cols(up_grad, wu)

    for i in part_a:
        ring.last(i, 2)
    feed(0, 0)
    second(part_b, 2)
    following(part_c, 1)
    feed(0, 1)
    for i in part_b:
        ring.last(i, 2)
    feed(1, 0)
    second(part_c, 2)
    feed(1, 1)
    for i in part_c:
        ring.last(i, 2)
    feed(2, 0)

    for copy in store_copies(1, 3, 1)[2:] + store_copies(2, 4, 0):
        copy.wait()

    @pl.loop(0, 16)
    def _(to):
        @pl.when(to != ctx)
        def _():
            swap_copy(0, kvown.at[0, pl.ds(0, 128)], kvseq.at[to], to, to).wait_send()
            swap_copy(1, qown.at[0, pl.ds(0, 128)], qseq.at[to], to, to).wait_send()
            swap_copy(2, oseq.at[to], orows.at[to], to, to).wait_send()

    for copy in wide + swaps + ring.started:
        copy.wait_send()


def forward(*arrays):
    shape = jax.ShapeDtypeStruct
    dma = pltpu.SemaphoreType.DMA
    attn = shape((4, 2, 4, 4, 8, D), BF)
    wide = shape((4, 2, 4, 4, 8, HALF), BF)
    rows, heads = shape((ROWS, D), F32), shape((16, 128, 128), BF)
    mats = []
    for units, down in zip(UNITS, DOWN_ROWS):
        mats += [pltpu.VMEM((4, 2, 4, 4, 8, 64 * units), BF)] * 2 + [pltpu.VMEM((4, 4, 4, down, D), BF)]
    raw = shape((8, ROWS, 128), F32)
    both = shape((2 * ROWS, D), F32)
    return pl.pallas_call(
        forward_kernel,
        out_shape=(
            attn, attn, attn, wide, wide, *(shape((4, 4, 4, down, D), BF) for down in DOWN_ROWS),
            shape((ROWS, D), BF), raw, raw, heads, heads, heads, shape((2, SEQ), F32), shape((ROWS, D), BF), rows, both, both,
        ),
        in_specs=[vmem()] + [hbm()] + [vmem()] * 13,
        out_specs=[vmem()] * 3 + [hbm()] * 5 + [vmem()] * 11,
        scratch_shapes=mats + [pltpu.VMEM((8, ROWS, 128), BF)] * 2 + [pltpu.VMEM((16, 128, 128), BF)] + [pltpu.VMEM((2, ROWS, D), BF)] * 2
        + [pltpu.VMEM((D, 2 * ROWS), BF)] + [pltpu.VMEM((4, 2, 4, 4, 8, FF_BLOCK), BF)] * 2
        + [pltpu.VMEM((2, 4, 4, 16, D), BF), pltpu.VMEM((4, 4, 4, 8, D), BF)]
        + [pltpu.VMEM((8, D), BF)] * 2 + [pltpu.VMEM((2, 8, 64 * units), BF) for units in UNITS for _ in range(2)]
        + [dma((13,)), dma((11,)), dma((11,)), dma((12, 3, 4)), dma((12, 3, 4)), dma((3, 16)), dma((3, 16)), dma((3,)), dma((4,))],
        compiler_params=params(collective_id=0, has_side_effects=True),
    )(*arrays)


class Scatter:
    def __init__(self, at, grads, layouts, bufs, own, fins, send, recv, load):
        self.at, self.grads, self.layouts, self.bufs, self.own, self.fins = at, grads, layouts, bufs, own, fins
        self.send, self.recv, self.load = send, recv, load
        self.started = []

    def copy(self, i, stage, slot, src, dst, to):
        return pltpu.make_async_remote_copy(
            src_ref=src, dst_ref=dst, send_sem=self.send.at[i, stage, slot], recv_sem=self.recv.at[i, stage, slot],
            device_id=to, device_id_type=MESH)

    def start(self, *args):
        copy = self.copy(*args)
        copy.start()
        self.started.append(copy)

    def arrived(self, i, stage, slot, dst):
        self.copy(i, stage, slot, dst, dst, beside(self.at, "x", 1)).wait_recv()

    def lanes(self, i, half):
        width = self.layouts[i].columns // 2
        return pl.ds(half * width, width)

    def source(self, i, stage, by, half):
        lay = self.layouts[i]
        dim, full = lay.order[stage], lay.order[stage + 1 :]
        if stage == 0:
            return self.grads[i].at[lay.index(self.at, full, {dim: (self.at[dim] + by) % 4}, half)]
        kept = [d for d in "yzx" if d in lay.order[stage:]]
        index = [slice(None) if d != dim else (self.at[dim] + by) % 4 for d in kept]
        if lay.kind == "both":
            index.insert(1 if "y" in kept else 0, slice(None))
        return self.bufs[i][2 * stage - 1].at[(0, *index, slice(None), self.lanes(i, half))]

    def parts(self, i, stage):
        halves, near = self.bufs[i][2 * stage], self.bufs[i][2 * stage + 1]
        row = (slice(None),) * (len(near.shape) - 2)
        return halves, near, lambda side, half: near.at[(side, *row, self.lanes(i, half))]

    def in_vmem(self, i, stage):
        return stage > 0 or self.own[i] is None

    def loads(self, i, stage, second):
        steps = ((0, 0, 0), (1, 0, 1)) if second else ((0, 1, 0), (1, 3, 1))
        return [
            pltpu.make_async_copy(self.source(i, stage, by, half), self.own[i].at[k], self.load.at[i, k]) for k, by, half in steps
        ]

    def first(self, i, stage):
        dim = self.layouts[i].order[stage]
        halves, near, part = self.parts(i, stage)
        ahead, behind = beside(self.at, dim, 1), beside(self.at, dim, 3)
        self.start(i, stage, 0, self.source(i, stage, 2, 0), halves.at[0], ahead)
        self.start(i, stage, 1, self.source(i, stage, 2, 1), halves.at[1], behind)
        self.start(i, stage, 2, self.source(i, stage, 1, 1), part(0, 1), ahead)
        self.start(i, stage, 3, self.source(i, stage, 3, 0), part(1, 0), behind)
        if not self.in_vmem(i, stage):
            for copy in self.loads(i, stage, False):
                copy.start()

    def second(self, i, stage):
        dim = self.layouts[i].order[stage]
        halves, near, part = self.parts(i, stage)
        for side, by in ((0, 1), (1, 3)):
            self.arrived(i, stage, side, halves.at[side])
            if self.in_vmem(i, stage):
                mine = self.source(i, stage, by, side)
            else:
                self.loads(i, stage, False)[side].wait()
                mine = self.own[i].at[side]
            add_into(halves.at[side], halves.at[side], mine)
            self.start(i, stage, 4 + side, halves.at[side], part(side, side), beside(self.at, dim, by))
        if not self.in_vmem(i, stage):
            for copy in self.loads(i, stage, True):
                copy.start()

    def last(self, i, stage):
        halves, near, part = self.parts(i, stage)
        self.arrived(i, stage, 2, part(0, 1))
        self.arrived(i, stage, 3, part(1, 0))
        self.arrived(i, stage, 4, part(0, 0))
        self.arrived(i, stage, 5, part(1, 1))
        for half in range(2):
            if self.in_vmem(i, stage):
                mine = self.source(i, stage, 0, half)
            else:
                self.loads(i, stage, True)[half].wait()
                mine = self.own[i].at[half]
            target = part(0, half)
            if stage == 2:
                target = self.fins[i].at[(slice(None),) * (len(self.fins[i].shape) - 1) + (self.lanes(i, half),)]
            add_into(target, part(0, half), part(1, half), mine)


def add_into(target, *terms):
    def body(spot):
        total = terms[0][spot].astype(F32)
        for term in terms[1:]:
            total = total + term[spot].astype(F32)
        target[spot] = total.astype(target.dtype)

    lead = target.shape[:-2]
    count = 1
    for n in lead:
        count *= n
    if count == 1:
        body((0,) * len(lead))
        return

    @pl.loop(0, count)
    def _(flat):
        spot = []
        for n in reversed(lead):
            spot.insert(0, flat % n)
            flat = flat // n
        body(tuple(spot))


def stage_shapes(lay, rows):
    shapes = []
    for stage in range(3):
        left = lay.order[stage + 1 :]
        lead = ([4] if "y" in left else []) + ([2] if lay.kind == "both" else [])
        lead += [4] * (("z" in left) + ("x" in left))
        shapes.append((2, *lead, rows, lay.columns // 2))
        shapes.append((2, *lead, rows, lay.columns))
    return shapes


def norm_back(upstream, gain, unit, factor):
    scaled = upstream * gain
    return factor * (scaled - unit * jnp.mean(scaled * unit, axis=-1, keepdims=True))


GAIN_ROWS = 24


def segment_column(row):
    return jnp.transpose(jnp.broadcast_to(row.astype(F32), (128, row.shape[1])))[:, :1].astype(jnp.int32)


def backward_kernel(*refs):
    (x_ref, m_ref, gain_ref, qgain_ref, kgain_ref, fgain_ref, table_ref, segs_ref, x1_ref, out_hbm, back_hbm,
     full_ref, qseq, kvseq, oseq, inv_ref, h_ref, qraw_ref, kraw_ref, wo_hbm, wq_hbm, wkv_hbm, g_hbm, u_hbm, *d_hbm) = refs[:27]
    (y_ref, yin_ref, q_fin, k_out, v_out, o_fin, g_out, u_out, d_out, attn_gain_out, ffn_gain_out, q_gain_out, k_gain_out) = refs[27:40]
    (gq, gkv, go, out_own, back_own, out_other, back_other, do_own, do_seq, dq_own, dkv_own, dq_in, dkv_in, acc, dq_full, dkv_full,
     gains, gain_slots, wide_g, wide_u, first_mat, second_mat) = refs[40:62]
    cores = refs[62:65]
    own = [None, None, None, *refs[65:70]]
    bufs = [refs[70 + 6 * i : 76 + 6 * i] for i in range(8)]
    (core_send, core_recv, local_sem, send, recv, load_sem, swap_send, swap_recv, swap_local, gain_send, gain_recv) = refs[118:129]
    kv_fin, g_fin, u_fin, *d_fins, segcol_ref = refs[129:136]
    at = place()
    c = at["c"]
    dp, ctx = lax.axis_index("dp"), lax.axis_index("ctx")
    partner = device(at, c=1 - c)
    barrier = pltpu.get_barrier_semaphore()
    for to in (partner, beside(at, "y", 1), beside(at, "y", 3)):
        pl.semaphore_signal(barrier, inc=1, device_id=to, device_id_type=MESH)

    @pl.loop(1, 16)
    def _(step):
        pl.semaphore_signal(barrier, inc=1, device_id=(dp, (ctx + step) % 16), device_id_type=MESH)

    def core_copy(slot, src, dst):
        return pltpu.make_async_remote_copy(
            src_ref=src, dst_ref=dst, send_sem=core_send.at[slot], recv_sem=core_recv.at[slot], device_id=partner,
            device_id_type=MESH)

    rows_own, rows_other = pl.ds(0, ROWS), pl.ds(ROWS, ROWS)
    stays = [
        pltpu.make_async_copy(back_hbm.at[rows_own], back_own, local_sem.at[0]),
        pltpu.make_async_copy(out_hbm.at[rows_own], out_own, local_sem.at[1]),
        pltpu.make_async_copy(wo_hbm, first_mat, local_sem.at[2]),
        pltpu.make_async_copy(wkv_hbm, second_mat, local_sem.at[3]),
    ]
    for copy in stays:
        copy.start()
    pl.semaphore_wait(barrier, 18)
    swaps = [core_copy(0, back_hbm.at[rows_other], back_other), core_copy(1, out_hbm.at[rows_other], out_other)]
    for copy in swaps:
        copy.start()
    fins = [q_fin, kv_fin, o_fin, wide_g, wide_u, *d_fins]
    ring = Scatter(at, [gq, gkv, go, g_hbm, u_hbm, *d_hbm], scatter_layouts(), bufs, own, fins, send, recv, load_sem)
    attn, feed_mats = (0, 1, 2), (3, 4, 5, 6, 7)
    for i in feed_mats:
        ring.first(i, 0)

    for copy in stays:
        copy.wait()
    swaps[0].wait()
    residual = x1_ref[...]
    gain = fgain_ref[...]
    _, unit, factor = norm(residual, gain)
    upstream = back_own[...] + back_other[...]
    for k in range(8):
        gains[8 + k : 9 + k, :] = jnp.sum(upstream[:, k * 128 : (k + 1) * 128] * unit[:, k * 128 : (k + 1) * 128], axis=0, keepdims=True)
    dx1 = m_ref[...].astype(F32) + norm_back(upstream, gain, unit, factor)
    back_own[...] = dx1
    do = dot_cols(dx1.astype(BF), first_mat[...].reshape(D, D)).astype(BF)
    for s in range(2):
        for h in range(8):
            do_own[s * 8 + h] = do[s * 128 : (s + 1) * 128, h * 128 : (h + 1) * 128]
    query_mat = pltpu.make_async_copy(wq_hbm, first_mat, local_sem.at[4])
    query_mat.start()

    def swap_copy(k, src, dst, to, slot):
        return pltpu.make_async_remote_copy(
            src_ref=src, dst_ref=dst, send_sem=swap_send.at[k, to], recv_sem=swap_recv.at[k, slot], device_id=(dp, to),
            device_id_type=MESH)

    def swap_start(k, src, dst, to):
        @pl.when(to != ctx)
        def _():
            swap_copy(k, src.at[to], dst.at[ctx], to, ctx).start()

        @pl.when(to == ctx)
        def _():
            pltpu.make_async_copy(src.at[to], dst.at[ctx], swap_local.at[k]).start()

    def swap_wait(k, src, dst, source):
        @pl.when(source != ctx)
        def _():
            swap_copy(k, dst.at[source], dst.at[source], source, source).wait_recv()

        @pl.when(source == ctx)
        def _():
            pltpu.make_async_copy(src.at[ctx], dst.at[ctx], swap_local.at[k]).wait()

    @pl.loop(0, 16)
    def _(step):
        swap_start(0, do_own, do_seq, (ctx + step) % 16)

    acc[...] = jnp.zeros_like(acc)
    sequence = pl.ds(ctx // 8, 1)
    for k in range(SEQ // BLOCK):
        rows = slice(k * BLOCK, (k + 1) * BLOCK)
        segcol_ref[rows, :] = segment_column(segs_ref[sequence, rows])
    swaps[1].wait()
    y_ref[...] = (residual + out_own[...] + out_other[...]).astype(BF)

    def rows_gradient(grad, left, right):
        @pl.loop(0, 4)
        def _(y):
            cols = pl.ds(pl.multiple_of(y * 256, 256), 256)
            value = dot_rows(left[:, cols], right[...])
            grad[y] = value.reshape(2, 4, 4, 8, D).astype(BF)

    dq_full[...] = back_own[...].astype(BF)
    rows_gradient(go, full_ref, dq_full)
    swaps.append(core_copy(2, go.at[:, 1 - c], cores[2]))
    swaps[2].start()

    low_lane = lanes((BLOCK, 128)) < HDIM
    pick = (lax.broadcasted_iota(jnp.int32, (8, 128), 0) == lanes((8, 128)) // HDIM).astype(BF)

    def queries(block):
        swap_wait(0, do_own, do_seq, 2 * block)
        swap_wait(0, do_own, do_seq, 2 * block + 1)
        pair = pl.ds(2 * block, 2)
        rows = pl.ds(pl.multiple_of(block * BLOCK, BLOCK), BLOCK)
        q = qseq[pair].reshape(BLOCK, 128).astype(F32)
        do = do_seq[pair].reshape(BLOCK, 128).astype(F32)
        product = do * oseq[pair].reshape(BLOCK, 128).astype(F32)
        stacked = jnp.concatenate([jnp.where(low_lane, q, 0.0), jnp.where(low_lane, pltpu.roll(q, HDIM, 1), 0.0)], axis=0).astype(BF)
        above = jnp.concatenate([jnp.where(low_lane, 0.0, pltpu.roll(do, HDIM, 1)), jnp.where(low_lane, 0.0, do)], axis=0).astype(BF)
        high = product.astype(BF)
        rest = (product - high.astype(F32)).astype(BF)
        sums = dot_cols(pick, high) + dot_cols(pick, rest)
        row_dots = jnp.concatenate([sums[0:1], sums[1:2]], axis=1)
        inv = jnp.concatenate([inv_ref[0:1, rows], inv_ref[1:2, rows]], axis=1)
        seg_q = segs_ref[sequence, rows]
        seg_q = jnp.concatenate([seg_q, seg_q], axis=1)

        def part(j, total, diagonal):
            kv = kvseq[pl.ds(2 * j, 2)].reshape(BLOCK, 128)
            scores = dot_cols(kv, stacked)
            slopes = dot_cols(kv, above)
            allowed = segcol_ref[pl.ds(pl.multiple_of(j * BLOCK, BLOCK), BLOCK), :] == seg_q
            if diagonal:
                key = lax.broadcasted_iota(jnp.int32, (BLOCK, 2 * BLOCK), 0)
                allowed = allowed & (lanes((BLOCK, 2 * BLOCK)) % BLOCK >= key)
            weights = jnp.where(allowed, jnp.exp2(scores * SCALE2), 0.0) * inv
            change = (weights * (slopes - row_dots)).astype(BF)
            acc[j] = acc[j] + dot(change, stacked) * HDIM**-0.5 + dot(weights.astype(BF), above)
            return total + dot_rows(change, kv)

        total = lax.fori_loop(0, block, lambda j, t: part(j, t, False), jnp.zeros((2 * BLOCK, 128), F32))
        total = part(block, total, True)
        both = jnp.where(low_lane, total[:BLOCK], pltpu.roll(total[BLOCK:], HDIM, 1)) * HDIM**-0.5
        dq_own[pair] = both.astype(BF).reshape(2, 128, 128)
        dkv_own[pair] = acc[block].astype(BF).reshape(2, 128, 128)
        for k in range(2):
            swap_start(1, dkv_own, dkv_in, 2 * block + k)
            swap_start(2, dq_own, dq_in, 2 * block + k)

    @pl.loop(0, 2)
    def _(step):
        queries(7 - step)

    for i in feed_mats:
        ring.second(i, 0)

    @pl.loop(2, 8)
    def _(step):
        queries(7 - step)

    for i in feed_mats:
        ring.last(i, 0)
        ring.first(i, 1)

    cosine, sine = rope_of(table_ref)
    qgain, kgain = twice(qgain_ref), twice(kgain_ref)
    head_sums = head_sum_matrix()
    wide_lane = lanes((ROWS, 128)) < HDIM

    def head_back(raw, upstream, gain):
        factor = lax.rsqrt(split_dot(raw * raw, head_sums) * (1.0 / HDIM) + EPSILON)
        unit = raw * factor
        turned = upstream * cosine - turn(upstream) * sine
        scaled = turned * gain
        mean = split_dot(scaled * unit, head_sums) * (1.0 / HDIM)
        return factor * (scaled - unit * mean), jnp.sum(turned * unit, axis=0, keepdims=True)

    @pl.loop(0, 16)
    def _(source):
        swap_wait(1, dkv_own, dkv_in, source)
        swap_wait(2, dq_own, dq_in, source)

    qterms = jnp.zeros((1, 128), F32)
    kterms = jnp.zeros((1, 128), F32)
    for h in range(8):
        cols = slice(h * 128, (h + 1) * 128)
        upstream = jnp.concatenate([dq_in[h], dq_in[8 + h]], axis=0).astype(F32)
        pre, terms = head_back(qraw_ref[h], upstream, qgain)
        qterms = qterms + terms
        dq_full[:, cols] = pre.astype(BF)
        upstream = jnp.concatenate([dkv_in[h], dkv_in[8 + h]], axis=0).astype(F32)
        pre, terms = head_back(kraw_ref[h], upstream, kgain)
        kterms = kterms + terms
        dkv_full[:, cols] = jnp.where(wide_lane, pre, upstream).astype(BF)
    gains[16:17, :] = qterms
    gains[17:18, :] = kterms
    gains[18:24, :] = jnp.zeros((6, 128), F32)
    rows_gradient(gq, h_ref, dq_full)
    swaps.append(core_copy(3, gq.at[:, 1 - c], cores[0]))
    swaps[3].start()
    rows_gradient(gkv, h_ref, dkv_full)
    swaps.append(core_copy(4, gkv.at[:, 1 - c], cores[1]))
    swaps[4].start()
    for slot, i in ((2, 2), (3, 0), (4, 1)):
        swaps[slot].wait_recv()
        mine = ring.grads[i].at[:, c]
        add_into(mine, mine, cores[i])
        ring.first(i, 0)

    query_mat.wait()
    dh = dot_cols(dq_full[...], first_mat[...].reshape(D, D)) + dot_cols(dkv_full[...], second_mat[...].reshape(D, D))
    gain = gain_ref[...]
    _, unit, factor = norm(x_ref[...].astype(F32), gain)
    for k in range(8):
        gains[k : k + 1, :] = jnp.sum(dh[:, k * 128 : (k + 1) * 128] * unit[:, k * 128 : (k + 1) * 128], axis=0, keepdims=True)
    yin_ref[...] = (back_own[...] + norm_back(dh, gain, unit, factor)).astype(BF)

    started = []

    def gain_copy(stage, slot, index, to):
        ref = gain_slots.at[stage, index]
        return pltpu.make_async_remote_copy(
            src_ref=ref, dst_ref=ref, send_sem=gain_send.at[stage, slot], recv_sem=gain_recv.at[stage, slot], device_id=to,
            device_id_type=MESH)

    def gain_start(stage, slot, index, to):
        copy = gain_copy(stage, slot, index, to)
        copy.start()
        started.append(copy)

    def gain_first(stage, total):
        dim = "xyz"[stage]
        p = at[dim]
        gain_slots[stage, p] = total
        gain_start(stage, 0, p, beside(at, dim, 1))
        gain_start(stage, 1, p, beside(at, dim, 3))

    def gain_second(stage):
        dim = "xyz"[stage]
        before = (at[dim] + 3) % 4
        gain_copy(stage, 0, before, partner).wait_recv()
        gain_start(stage, 2, before, beside(at, dim, 1))

    def gain_last(stage):
        dim = "xyz"[stage]
        gain_copy(stage, 1, (at[dim] + 1) % 4, partner).wait_recv()
        gain_copy(stage, 2, (at[dim] + 2) % 4, partner).wait_recv()
        return gain_slots[stage, 0] + gain_slots[stage, 1] + gain_slots[stage, 2] + gain_slots[stage, 3]

    gain_first(0, gains[...])
    for i in attn:
        ring.second(i, 0)
    gain_second(0)
    for i in feed_mats:
        ring.second(i, 1)
    for i in attn:
        ring.last(i, 0)
        ring.first(i, 1)
    gain_first(1, gain_last(0))
    for i in feed_mats:
        ring.last(i, 1)
        ring.first(i, 2)
    for i in attn:
        ring.second(i, 1)
    gain_second(1)
    for i in feed_mats:
        ring.second(i, 2)
    for i in attn:
        ring.last(i, 1)
        ring.first(i, 2)
    gain_first(2, gain_last(1))
    finals = []
    for i in feed_mats:
        ring.last(i, 2)
        if i < 5:
            wide, fin = ring.fins[i], (g_fin, u_fin)[i - 3]
            finals.append(core_copy(2 + i, wide.at[1 - c], fin.at[c]))
            finals[-1].start()
            fin[c] = wide[c]
    for i in attn:
        ring.second(i, 2)
    gain_second(2)
    for i in attn:
        ring.last(i, 2)
    gain_slots[3, c] = gain_last(2)
    finals.append(core_copy(7, gain_slots.at[3, c], gain_slots.at[3, c]))
    finals[-1].start()
    for slot, fin in ((5, g_fin), (6, u_fin)):
        core_copy(slot, fin.at[1 - c], fin.at[1 - c]).wait_recv()
    columns = []
    for y in range(4):
        for fin in (g_fin, u_fin):
            pieces = [fin[core, :, part * 1024 + y * 256 : part * 1024 + (y + 1) * 256] for part in range(2) for core in range(2)]
            where = slice(2048 + y // 2 * 128, 2048 + (y // 2 + 1) * 128)
            pieces.append((low_pair, high_pair)[y % 2](fin[0, :, where], fin[1, :, where]))
            columns.append(jnp.concatenate(pieces, axis=1))
    columns = jnp.concatenate(columns, axis=0)
    high = columns.astype(BF)
    rest = (columns - high.astype(F32)).astype(BF)
    sources = unit_sources()
    for k in range(9):
        matrix = spread_matrix(k, sources)
        units = dot_cols(high, matrix) + dot_cols(rest, matrix)
        for y in range(4):
            where = slice(y * 1152 + k * 128, y * 1152 + (k + 1) * 128)
            g_out[:, where] = units[16 * y : 16 * y + 8]
            u_out[:, where] = units[16 * y + 8 : 16 * y + 16]
    core_copy(7, gain_slots.at[3, 1 - c], gain_slots.at[3, 1 - c]).wait_recv()
    total = gain_slots[3, 0] + gain_slots[3, 1]
    attn_gain_out[...] = total[:8]
    ffn_gain_out[...] = total[8:16]
    q_gain_out[...] = (total[16:17] + pltpu.roll(total, HDIM, 1)[16:17])[:, :HDIM]
    k_gain_out[...] = total[17:18, :HDIM]
    low_half = lanes((8, 128)) < HDIM
    for k in range(4):
        even, odd = kv_fin[:, k * 256 : k * 256 + 128], kv_fin[:, k * 256 + 128 : (k + 1) * 256]
        k_out[:, k * 128 : (k + 1) * 128] = jnp.where(low_half, even, pltpu.roll(odd, HDIM, 1))
        v_out[:, k * 128 : (k + 1) * 128] = jnp.where(low_half, pltpu.roll(even, HDIM, 1), odd)
    d_out[0:16, :] = d_fins[0][...]
    d_out[16:32, :] = d_fins[1][...]
    d_out[32:36, :] = d_fins[2][0:4, :]

    @pl.loop(0, 16)
    def _(to):
        @pl.when(to != ctx)
        def _():
            swap_copy(0, do_own.at[to], do_seq.at[to], to, to).wait_send()
            swap_copy(1, dkv_own.at[to], dkv_in.at[to], to, to).wait_send()
            swap_copy(2, dq_own.at[to], dq_in.at[to], to, to).wait_send()

    for copy in swaps[2:] + finals + started + ring.started:
        copy.wait_send()


def backward(*arrays):
    shape = jax.ShapeDtypeStruct
    dma = pltpu.SemaphoreType.DMA
    small = shape((8, D), F32)
    block = pltpu.VMEM((16, 128, 128), BF)
    own = pltpu.VMEM((ROWS, D), F32)
    scratch = [pltpu.VMEM((4, 2, 4, 4, 8, D), BF)] * 3 + [own] * 4 + [block] * 6
    scratch += [pltpu.VMEM((SEQ // BLOCK, BLOCK, 128), F32)] + [pltpu.VMEM((ROWS, D), BF)] * 2
    scratch += [pltpu.VMEM((GAIN_ROWS, 128), F32), pltpu.VMEM((4, 4, GAIN_ROWS, 128), F32)] + [pltpu.VMEM((2, 8, HALF), F32)] * 2
    scratch += [pltpu.VMEM((4, 2, 4, 4, 8, D), BF)] * 2 + [pltpu.VMEM((4, 4, 4, 8, D), BF)] * 3
    shapes = [stage_shapes(lay, rows) for lay, rows in zip(scatter_layouts(), (8,) * 5 + DOWN_ROWS)]
    scratch += [pltpu.VMEM(shapes[i][0], BF) for i in range(3, 8)]
    for group in shapes:
        scratch += [pltpu.VMEM(s, BF) for s in group]
    scratch += [
        dma((8,)), dma((8,)), dma((5,)), dma((8, 3, 6)), dma((8, 3, 6)), dma((8, 2)), dma((3, 16)), dma((3, 16)), dma((3,)), dma((3, 3)),
        dma((3, 3)),
    ]
    scratch += [pltpu.VMEM((8, D), F32)] + [pltpu.VMEM((2, 8, HALF), F32)] * 2 + [pltpu.VMEM((rows, D), F32) for rows in DOWN_ROWS]
    scratch += [pltpu.VMEM((SEQ, 1), jnp.int32)]
    return pl.pallas_call(
        backward_kernel,
        out_shape=(
            shape((ROWS, D), BF), shape((ROWS, D), BF), small, shape((8, D // 2), F32), shape((8, D // 2), F32), small, shape((8, 4608), F32),
            shape((8, 4608), F32), shape((36, D), F32), shape((8, 128), F32), shape((8, 128), F32), shape((1, HDIM), F32),
            shape((1, HDIM), F32),
        ),
        in_specs=[vmem()] * 9 + [hbm()] * 2 + [vmem()] * 8 + [hbm()] * 8,
        out_specs=[vmem()] * 13,
        scratch_shapes=scratch,
        compiler_params=params(collective_id=1, has_side_effects=True),
    )(*arrays)


def results_kernel(*refs):
    count = len(refs) // 2
    for source, target in zip(refs[:count], refs[count:]):
        target[...] = source[...]


def results(arrays):
    return pl.pallas_call(
        results_kernel,
        out_shape=tuple(jax.ShapeDtypeStruct(a.shape, a.dtype) for a in arrays),
        in_specs=[vmem()] * len(arrays),
        out_specs=[vmem()] * len(arrays),
        compiler_params=params(),
    )(*arrays)


def rope_table(first_row):
    places = first_row + lax.broadcasted_iota(jnp.int32, (128, 128), 0)
    lane = lax.broadcasted_iota(jnp.int32, (128, 128), 1)
    frequency = THETA_BASE ** (-2.0 * (lane % (HDIM // 2)).astype(F32) / HDIM)
    angles = places.astype(F32) * frequency
    return jnp.where(lane < HDIM, jnp.cos(angles), jnp.sin(angles))


def local(block_in, segment_ids, attn_gain, w_query, w_key, w_value, query_gain, key_gain, w_out, ffn_gain, w_gate, w_up, w_down, out_grad):
    x = block_in.reshape(ROWS, D)
    m = out_grad.reshape(ROWS, D)
    row = lambda v: v.reshape(1, -1)
    gains = row(attn_gain), row(query_gain), row(key_gain), row(ffn_gain)
    table = rope_table(lax.axis_index("ctx") * 128)
    (wq, wkv, wo, gg, gu, gda, gdb, gdc, h1, qraw, kraw, q, kv, o, inv, attended, x1, out, back) = forward(
        x, m, *gains, table, segment_ids, w_query, w_key, w_value, w_out, w_gate, w_up, w_down)
    y, y_in, gq, gk, gv, gout, gg, gu, gd, attn_terms, ffn_terms, q_terms, k_terms = results(backward(
        x, m, *gains, table, segment_ids, x1, out, back, attended, q, kv, o, inv, h1, qraw, kraw, wo, wq, wkv, gg, gu, gda, gdb, gdc))
    return (
        y.reshape(2, 128, D), y_in.reshape(2, 128, D), gq, gk, gv, gout, gg, gu, gd, attn_terms.reshape(D), q_terms.reshape(HDIM),
        k_terms.reshape(HDIM), ffn_terms.reshape(D),
    )


def solution(mesh):
    both = P(("dp", "ctx"), None)
    acts = P("dp", "ctx", None)
    return jax.shard_map(
        local,
        mesh=mesh,
        in_specs=(acts, P("dp", None), P(), both, both, both, P(), P(), both, P(), both, both, both, acts),
        out_specs=(acts, acts, both, both, both, both, both, both, both, P(), P(), P(), P()),
        check_vma=False,
    )
```

```python
import functools

import jax
import jax.numpy as jnp
from jax import lax
from jax.experimental import pallas as pl
from jax.experimental.pallas import tpu as pltpu
from jax.sharding import PartitionSpec as P

MESH = pl.DeviceIdType.MESH
BF = jnp.bfloat16
F32 = jnp.float32

D = 1024
HDIM = 64
HEADS = 8
ROWS = 256
SEQ = 2048
UNITS = (16, 16, 4)
DOWN_ROWS = (16, 16, 8)
HALF = 64 * sum(UNITS)
EPSILON = 1e-05
THETA_BASE = 1000000.0
LOG2E = 1.4426950408889634
VMEM_MOST = 60 * 1024 * 1024


def params(**more):
    return pltpu.CompilerParams(vmem_limit_bytes=VMEM_MOST, **more)


def vmem():
    return pl.BlockSpec(memory_space=pltpu.VMEM)


def hbm():
    return pl.BlockSpec(memory_space=pl.ANY)


def dot(left, right):
    return lax.dot_general(left, right, (((1,), (0,)), ((), ())), preferred_element_type=F32)


def dot_rows(left, right):
    return lax.dot_general(left, right, (((0,), (0,)), ((), ())), preferred_element_type=F32)


def dot_cols(left, right):
    return lax.dot_general(left, right, (((1,), (1,)), ((), ())), preferred_element_type=F32)


def place():
    dp, ctx = lax.axis_index("dp"), lax.axis_index("ctx")
    return {"y": dp // 2, "c": dp % 2, "z": ctx // 4, "x": ctx % 4}


def device(at, **moved):
    spot = dict(at)
    spot.update(moved)
    return (spot["y"] * 2 + spot["c"], spot["z"] * 4 + spot["x"])


def beside(at, dim, by):
    return device(at, **{dim: (at[dim] + by) % 4})


ORDERS = (("x", "z", "y"), ("y", "x", "z"), ("z", "y", "x"))


class Layout:
    def __init__(self, kind, order, columns):
        self.kind, self.order, self.columns = kind, order, columns

    def index(self, at, full, fixed=None, half=None):
        spot = dict(at)
        if fixed:
            spot.update(fixed)
        ids = {d: (slice(None) if d in full else spot[d]) for d in "xyz"}
        c = {"own": at["c"], "both": slice(None), "none": None}[self.kind]
        out = [ids["y"]] + ([] if c is None else [c]) + [ids["z"], ids["x"], slice(None)]
        if half is None:
            out.append(slice(None))
        else:
            out.append(pl.ds(half * (self.columns // 2), self.columns // 2))
        return tuple(out)


class Gather:
    def __init__(self, at, arrays, layouts, send, recv):
        self.at, self.arrays, self.layouts, self.send, self.recv = at, arrays, layouts, send, recv
        self.started = []

    def copy(self, i, stage, slot, index, to):
        ref = self.arrays[i].at[index]
        return pltpu.make_async_remote_copy(
            src_ref=ref, dst_ref=ref, send_sem=self.send.at[i, stage, slot], recv_sem=self.recv.at[i, stage, slot],
            device_id=to, device_id_type=MESH)

    def start(self, i, stage, slot, index, to):
        copy = self.copy(i, stage, slot, index, to)
        copy.start()
        self.started.append(copy)

    def slab(self, i, stage, by, half=None):
        lay = self.layouts[i]
        dim, full = lay.order[stage], lay.order[:stage]
        return lay.index(self.at, full, {dim: (self.at[dim] + by) % 4}, half)

    def first(self, i, stage):
        dim = self.layouts[i].order[stage]
        self.start(i, stage, 0, self.slab(i, stage, 0), beside(self.at, dim, 1))
        self.start(i, stage, 1, self.slab(i, stage, 0), beside(self.at, dim, 3))

    def arrived(self, i, stage, slot, by, half):
        self.copy(i, stage, slot, self.slab(i, stage, by, half), beside(self.at, "x", 1)).wait_recv()

    def second(self, i, stage):
        dim = self.layouts[i].order[stage]
        self.arrived(i, stage, 0, 3, None)
        self.start(i, stage, 2, self.slab(i, stage, 3, 0), beside(self.at, dim, 1))
        self.arrived(i, stage, 1, 1, None)
        self.start(i, stage, 3, self.slab(i, stage, 1, 1), beside(self.at, dim, 3))

    def last(self, i, stage):
        self.arrived(i, stage, 2, 2, 0)
        self.arrived(i, stage, 3, 2, 1)


def attn_layouts():
    return [Layout("own", ORDERS[0], D), Layout("own", ORDERS[1], D), Layout("own", ORDERS[2], D)]


def gather_layouts():
    shapes = attn_layouts()
    for units in UNITS:
        shapes += [Layout("both", ORDERS[0], 64 * units), Layout("both", ORDERS[1], 64 * units), Layout("none", ORDERS[2], D)]
    return shapes


def scatter_layouts():
    wide = [Layout("both", ORDERS[0], HALF), Layout("both", ORDERS[1], HALF)]
    return attn_layouts() + wide + [Layout("none", ORDERS[2], D)] * 3


def lanes(shape):
    return lax.broadcasted_iota(jnp.int32, shape, len(shape) - 1)


def norm(values, gain):
    factor = lax.rsqrt(jnp.mean(values * values, axis=-1, keepdims=True) + EPSILON)
    unit = values * factor
    return unit * gain, unit, factor


def split_dot(values, matrix):
    high = values.astype(BF)
    low = (values - high.astype(F32)).astype(BF)
    return dot(high, matrix) + dot(low, matrix)


def head_sum_matrix():
    rows = lax.broadcasted_iota(jnp.int32, (128, 128), 0) // HDIM
    return (rows == lanes((128, 128)) // HDIM).astype(BF)


def turn(values):
    low = lanes(values.shape) % HDIM < HDIM // 2
    ahead = pltpu.roll(values, 128 - HDIM // 2, 1)
    behind = pltpu.roll(values, HDIM // 2, 1)
    return jnp.where(low, -ahead, behind)


BLOCK = 256
SCALE2 = LOG2E * HDIM**-0.5


def heads_to_rows(ref):
    parts = [jnp.concatenate([ref[s * 8 + h] for h in range(8)], axis=1) for s in range(2)]
    return jnp.concatenate(parts, axis=0)


def unit_sources():
    column = lax.broadcasted_iota(jnp.int32, (1, 1152), 1)
    last = column >= 1024
    k = column - 1024
    core = jnp.where(last, k // 64, (column // 256) % 2)
    ctx = jnp.where(last, (k % 64) // 4, (column % 256) // 16)
    unit = jnp.where(last, 32 + column % 4, 16 * (column // 512) + column % 16)
    return core * 576 + ctx * 36 + unit


def spread_matrix(k, sources):
    rows = lax.broadcasted_iota(jnp.int32, (128, 1152), 0) + 128 * k
    return jnp.where(rows == sources, 1.0, 0.0).astype(BF)


def four_of_eight():
    rows = lax.broadcasted_iota(jnp.int32, (256, 512), 0)
    return jnp.where(lanes((256, 512)) == rows // 4 * 8 + rows % 4, 1.0, 0.0).astype(BF)


def low_pair(first, second):
    return jnp.where(lanes(first.shape) < HDIM, first, pltpu.roll(second, HDIM, 1))


def high_pair(first, second):
    return jnp.where(lanes(first.shape) < HDIM, pltpu.roll(first, HDIM, 1), second)


FF_BLOCK = 512


def rope_of(table_ref):
    table = table_ref[...]
    low, turned = lanes(table.shape) < HDIM, pltpu.roll(table, HDIM, 1)
    cosine, sine = jnp.where(low, table, turned), jnp.where(low, turned, table)
    return jnp.concatenate([cosine, cosine], axis=0), jnp.concatenate([sine, sine], axis=0)


def twice(gain_ref):
    return jnp.concatenate([gain_ref[...], gain_ref[...]], axis=1)


def forward_kernel(*refs):
    (x_ref, m_ref, gain_ref, qgain_ref, kgain_ref, fgain_ref, table_ref, segs_ref, q_in, k_in, v_in,
     o_in, gate_in, up_in, down_in) = refs[:15]
    (wq8, wkv8, wo8, g_grad, u_grad, d_grad_a, d_grad_b, d_grad_c, h_ref, qraw_ref, kraw_ref, qseq, kvseq, oseq, inv_ref, full_ref, x1_ref,
     out_ref, back_ref) = refs[15:34]
    mats = refs[34:43]
    (qown, kvown, orows, h2_ref, m2_ref, turned, g_stage, u_stage, d_stage, d_stage_c, kv_in, down_pad, *wide_shards) = refs[43:61]
    (local_sem, core_send, core_recv, send, recv, swap_send, swap_recv, swap_local, store_sem) = refs[61:70]
    d_grads = (d_grad_a, d_grad_b, d_grad_c)
    at = place()
    c = at["c"]
    dp, ctx = lax.axis_index("dp"), lax.axis_index("ctx")
    partner = device(at, c=1 - c)
    barrier = pltpu.get_barrier_semaphore()
    for to in (partner, beside(at, "y", 1), beside(at, "y", 3)):
        pl.semaphore_signal(barrier, inc=1, device_id=to, device_id_type=MESH)

    @pl.loop(1, 16)
    def _(step):
        pl.semaphore_signal(barrier, inc=1, device_id=(dp, (ctx + step) % 16), device_id_type=MESH)

    sequence = pl.ds(ctx // 8, 1)
    here = (at["y"], c, at["z"], at["x"])
    ring = Gather(at, [wq8, wkv8, wo8, *mats], gather_layouts(), send, recv)
    attn, part_a, part_b, part_c = (0, 1, 2), (3, 4, 5), (6, 7, 8), (9, 10, 11)

    def core_copy(slot, src, dst):
        return pltpu.make_async_remote_copy(
            src_ref=src, dst_ref=dst, send_sem=core_send.at[slot], recv_sem=core_recv.at[slot], device_id=partner,
            device_id_type=MESH)

    low_half = lanes((8, 128)) < HDIM
    for k in range(4):
        key, value = (ref[:, k * 128 : (k + 1) * 128].astype(F32) for ref in (k_in, v_in))
        kv_in[:, k * 256 : k * 256 + 128] = jnp.where(low_half, key, pltpu.roll(value, HDIM, 1)).astype(BF)
        kv_in[:, k * 256 + 128 : (k + 1) * 256] = jnp.where(low_half, pltpu.roll(key, HDIM, 1), value).astype(BF)
    stays = [pltpu.make_async_copy(src, dst.at[here], local_sem.at[i]) for i, (src, dst) in enumerate(((q_in, wq8), (kv_in, wkv8), (o_in, wo8)))]
    for copy in stays:
        copy.start()
    for copy in stays:
        copy.wait()
    pl.semaphore_wait(barrier, 18)
    for i in attn:
        ring.first(i, 0)
    upstream_copy = core_copy(6, m_ref, m2_ref.at[1])
    upstream_copy.start()

    sources = unit_sources()
    units = jnp.concatenate(
        [ref[:, y * 1152 : (y + 1) * 1152].astype(F32) for y in range(4) for ref in (gate_in, up_in)], axis=0).astype(BF)
    spread = jnp.zeros((64, 1152), F32)
    for k in range(9):
        spread = spread + dot(units[:, k * 128 : (k + 1) * 128], spread_matrix(k, sources))
    for j in range(2):
        blocks = [spread[16 * y + 8 * j : 16 * y + 8 * j + 8] for y in range(4)]
        for core in range(2):
            for part in range(2):
                start = part * 512 + core * 256
                for y in range(4):
                    wide_shards[2 * part + j][core, :, y * 256 : (y + 1) * 256] = blocks[y][:, start : start + 256].astype(BF)
            for k in range(2):
                pair = (low_pair, high_pair)[core](blocks[2 * k][:, 1024:], blocks[2 * k + 1][:, 1024:])
                wide_shards[4 + j][core, :, k * 128 : (k + 1) * 128] = pair.astype(BF)
    down_pad[...] = jnp.concatenate([down_in[32:36, :].astype(F32), jnp.zeros((4, D), F32)], axis=0).astype(BF)
    downs = (down_in.at[pl.ds(0, 16)], down_in.at[pl.ds(16, 16)], down_pad)
    stays = []
    wide = []
    for k in range(3):
        for j in range(2):
            stays.append(pltpu.make_async_copy(wide_shards[2 * k + j].at[c], mats[3 * k + j].at[here], local_sem.at[3 + 3 * k + j]))
            wide.append(core_copy(2 * k + j, wide_shards[2 * k + j].at[1 - c], mats[3 * k + j].at[here]))
        stays.append(pltpu.make_async_copy(downs[k], mats[3 * k + 2].at[at["y"], at["z"], at["x"]], local_sem.at[5 + 3 * k]))
    stays.append(pltpu.make_async_copy(m_ref, m2_ref.at[0], local_sem.at[12]))
    for copy in wide + stays:
        copy.start()
    normed, _, _ = norm(x_ref[...].astype(F32), gain_ref[...])
    h_ref[...] = normed.astype(BF)
    for copy in stays:
        copy.wait()
    for copy in wide:
        copy.wait_recv()
    for i in part_a + part_b + part_c:
        ring.first(i, 0)

    def second(group, stage):
        for i in group:
            ring.second(i, stage)

    def following(group, stage):
        for i in group:
            ring.last(i, stage)
            ring.first(i, stage + 1)

    second(attn, 0)
    following(attn, 0)
    second(part_a, 0)
    second(attn, 1)
    following(part_a, 0)
    following(attn, 1)
    second(part_a, 1)
    second(attn, 2)
    swaps = []
    eights = (wq8, wkv8, wo8)
    for i in attn:
        ring.last(i, 2)
        copy = core_copy(7 + i, eights[i].at[:, c], eights[i].at[:, c])
        copy.start()
        swaps.append(copy)

    second(part_b + part_c, 0)
    following(part_b + part_c, 0)

    def other_rows(i):
        core_copy(7 + i, eights[i].at[:, 1 - c], eights[i].at[:, 1 - c]).wait_recv()

    def rows_of(core):
        cols = [h_ref[:, pl.ds(pl.multiple_of((2 * y + core) * 128, 128), 128)] for y in range(4)]
        return jnp.concatenate(cols, axis=1)

    def mat_of(eight, core):
        return eight[:, core].reshape(D // 2, D)

    mine, other = rows_of(c), rows_of(1 - c)
    query = dot(mine, mat_of(wq8, c))
    other_rows(0)
    query = query + dot(other, mat_of(wq8, 1 - c))
    for h in range(8):
        qraw_ref[h] = query[:, h * 128 : (h + 1) * 128]
    other_rows(1)
    key_value = dot(mine, mat_of(wkv8, c)) + dot(other, mat_of(wkv8, 1 - c))
    for h in range(8):
        kraw_ref[h] = key_value[:, h * 128 : (h + 1) * 128]

    sums = head_sum_matrix()
    cosine, sine = rope_of(table_ref)
    qgain, kgain = twice(qgain_ref), twice(kgain_ref)

    def rotated(raw, gain):
        factor = lax.rsqrt(split_dot(raw * raw, sums) * (1.0 / HDIM) + EPSILON)
        unit = raw * factor * gain
        return unit * cosine + turn(unit) * sine

    def swap_copy(k, src, dst, to, slot):
        return pltpu.make_async_remote_copy(
            src_ref=src, dst_ref=dst, send_sem=swap_send.at[k, to], recv_sem=swap_recv.at[k, slot], device_id=(dp, to),
            device_id_type=MESH)

    @pl.loop(0, 8)
    def _(step):
        h = (ctx + step) % 8
        raw = qraw_ref[h]
        qown[h] = rotated(raw, qgain).astype(BF)
        raw = kraw_ref[h]
        kvown[h] = jnp.where(lanes(raw.shape) < HDIM, rotated(raw, kgain), raw).astype(BF)
        for s in range(2):
            to = s * 8 + h
            rows = pl.ds(s * 128, 128)

            @pl.when(to != ctx)
            def _():
                swap_copy(0, kvown.at[h, rows], kvseq.at[ctx], to, ctx).start()
                swap_copy(1, qown.at[h, rows], qseq.at[ctx], to, ctx).start()

            @pl.when(to == ctx)
            def _():
                pltpu.make_async_copy(kvown.at[h, rows], kvseq.at[ctx], swap_local.at[0]).start()
                pltpu.make_async_copy(qown.at[h, rows], qseq.at[ctx], swap_local.at[1]).start()

    other_rows(2)
    following(part_a, 1)
    second(part_b + part_c, 1)
    low_lane = lanes((BLOCK, 128)) < HDIM

    def arrive(source):
        @pl.when(source != ctx)
        def _():
            swap_copy(0, kvseq.at[source], kvseq.at[source], source, source).wait_recv()
            swap_copy(1, qseq.at[source], qseq.at[source], source, source).wait_recv()

        @pl.when(source == ctx)
        def _():
            pltpu.make_async_copy(kvown.at[0, pl.ds(0, 128)], kvseq.at[ctx], swap_local.at[0]).wait()
            pltpu.make_async_copy(qown.at[0, pl.ds(0, 128)], qseq.at[ctx], swap_local.at[1]).wait()

    def queries(block):
        arrive(2 * block)
        arrive(2 * block + 1)
        q = qseq[pl.ds(2 * block, 2)].reshape(BLOCK, 128)
        zero = jnp.zeros_like(q)
        second = pltpu.roll(q.astype(F32), HDIM, 1).astype(BF)
        stacked = jnp.concatenate([jnp.where(low_lane, q, zero), jnp.where(low_lane, second, zero)], axis=0)
        rows = pl.ds(pl.multiple_of(block * BLOCK, BLOCK), BLOCK)
        seg_q = segment_column(segs_ref[sequence, rows])
        seg_q = jnp.concatenate([seg_q, seg_q], axis=0)

        def part(j, total, diagonal):
            kv = kvseq[pl.ds(2 * j, 2)].reshape(BLOCK, 128)
            scores = dot_cols(stacked, kv)
            allowed = seg_q == segs_ref[sequence, pl.ds(pl.multiple_of(j * BLOCK, BLOCK), BLOCK)]
            if diagonal:
                query = lax.broadcasted_iota(jnp.int32, (2 * BLOCK, BLOCK), 0) % BLOCK
                allowed = allowed & (query >= lanes((2 * BLOCK, BLOCK)))
            weights = jnp.where(allowed, jnp.exp2(scores * SCALE2), 0.0).astype(BF)
            values = jnp.where(low_lane, jnp.ones_like(kv), kv)
            return total + dot(weights, values)

        total = lax.fori_loop(0, block, lambda j, t: part(j, t, False), jnp.zeros((2 * BLOCK, 128), F32))
        total = part(block, total, True)
        mixed = total / pltpu.roll(total, HDIM, 1)
        first = pltpu.roll(mixed[:BLOCK], HDIM, 1)
        oseq[pl.ds(2 * block, 2)] = jnp.where(low_lane, first, mixed[BLOCK:]).astype(BF).reshape(2, 128, 128)
        inv_ref[0:1, rows] = 1.0 / jnp.transpose(total[:BLOCK])[0:1, :]
        inv_ref[1:2, rows] = 1.0 / jnp.transpose(total[BLOCK:])[0:1, :]
        for k in range(2):
            to = 2 * block + k

            @pl.when(to != ctx)
            def _():
                swap_copy(2, oseq.at[to], orows.at[ctx], to, ctx).start()

            @pl.when(to == ctx)
            def _():
                pltpu.make_async_copy(oseq.at[to], orows.at[ctx], swap_local.at[2]).start()

    queries(0)

    @pl.loop(1, 4)
    def _(block):
        queries(block)

    second(part_a, 2)

    @pl.loop(4, 7)
    def _(block):
        queries(block)

    @pl.loop(7, 8)
    def _(block):
        queries(block)

    following(part_b, 1)

    @pl.loop(0, 16)
    def _(source):
        @pl.when(source != ctx)
        def _():
            swap_copy(2, orows.at[source], orows.at[source], source, source).wait_recv()

        @pl.when(source == ctx)
        def _():
            pltpu.make_async_copy(oseq.at[ctx], orows.at[ctx], swap_local.at[2]).wait()

    attended = heads_to_rows(orows)
    full_ref[...] = attended
    residual = x_ref[...].astype(F32) + dot(attended, wo8[...].reshape(D, D))
    x1_ref[...] = residual
    normed, _, _ = norm(residual, fgain_ref[...])
    h2_ref[0] = normed.astype(BF)
    mid_copy = core_copy(10, h2_ref.at[0], h2_ref.at[1])
    mid_copy.start()
    out_ref[...] = jnp.zeros_like(out_ref)
    back_ref[...] = jnp.zeros_like(back_ref)
    upstream_copy.wait()
    mid_copy.wait()
    turned[...] = jnp.transpose(h2_ref[...].reshape(2 * ROWS, D))

    def store_copies(part, step, slot):
        if part < 2:
            cols = (slice(None),) * 5 + (pl.ds(step * FF_BLOCK, FF_BLOCK),)
            g_part, u_part, down, rows = g_stage, u_stage, d_stage, d_grads[part].at[pl.ds(2 * slot, 2)]
        else:
            cols, less = ((slice(None),) * 5 + (pl.ds(start, 256),) for start in (2048, 0))
            g_part, u_part, down, rows = g_stage.at[less], u_stage.at[less], d_stage_c, d_grads[2]
        return [
            pltpu.make_async_copy(g_part, g_grad.at[cols], store_sem.at[0]),
            pltpu.make_async_copy(u_part, u_grad.at[cols], store_sem.at[1]),
            pltpu.make_async_copy(down, rows, store_sem.at[2 + (part == 2)]),
        ]

    def feed(part, slot):
        gate_mat, up_mat, down_mat = (mats[3 * part + j] for j in range(3))
        step = 2 * part + slot
        width = FF_BLOCK if part < 2 else 256
        cols = pl.ds(slot * width, width)
        wg = gate_mat.reshape(D, 64 * UNITS[part])[:, cols]
        wu = up_mat.reshape(D, 64 * UNITS[part])[:, cols]
        if part < 2:
            wd = down_mat.reshape(64 * UNITS[part], D)[cols, :]
        else:
            wd = dot(four_of_eight(), down_mat[...].reshape(512, D)).astype(BF)
        low, upstream = h2_ref[...].reshape(2 * ROWS, D), m2_ref[...].reshape(2 * ROWS, D)
        gate = dot(low, wg)
        up = dot(low, wu)
        sig = jax.nn.sigmoid(gate)
        silu = gate * sig
        hidden = (silu * up).astype(BF)
        slope = dot_cols(upstream, wd)
        gate_grad = (slope * up * sig * (1.0 + gate * (1.0 - sig))).astype(BF)
        up_grad = (slope * silu).astype(BF)

        def freed():
            g_copy, u_copy, d_copy = store_copies((step - 1) // 2, step - 1, (step - 1) % 2)
            g_copy.wait()
            u_copy.wait()
            if part < 2:
                d_copy.wait()

        if step > 0:
            freed()
        for y in range(0, 4, 2):
            left = turned[y * 256 : (y + 2) * 256, :]
            g_stage[y : y + 2, :, :, :, :, :width] = dot(left, gate_grad).astype(BF).reshape(2, 2, 4, 4, 8, width)
            u_stage[y : y + 2, :, :, :, :, :width] = dot(left, up_grad).astype(BF).reshape(2, 2, 4, 4, 8, width)
        down_grad = dot_rows(hidden, upstream).astype(BF)
        if part < 2:
            d_stage[...] = down_grad.reshape(2, 4, 4, 16, D)
        else:
            d_stage_c[...] = dot_rows(four_of_eight(), down_grad).astype(BF).reshape(4, 4, 4, 8, D)
        for copy in store_copies(part, step, slot):
            copy.start()
        out_ref[...] += dot(hidden, wd)
        back_ref[...] += dot_cols(gate_grad, wg)
        back_ref[...] += dot_cols(up_grad, wu)

    for i in part_a:
        ring.last(i, 2)
    feed(0, 0)
    second(part_b, 2)
    following(part_c, 1)
    feed(0, 1)
    for i in part_b:
        ring.last(i, 2)
    feed(1, 0)
    second(part_c, 2)
    feed(1, 1)
    for i in part_c:
        ring.last(i, 2)
    feed(2, 0)

    for copy in store_copies(1, 3, 1)[2:] + store_copies(2, 4, 0):
        copy.wait()

    @pl.loop(0, 16)
    def _(to):
        @pl.when(to != ctx)
        def _():
            swap_copy(0, kvown.at[0, pl.ds(0, 128)], kvseq.at[to], to, to).wait_send()
            swap_copy(1, qown.at[0, pl.ds(0, 128)], qseq.at[to], to, to).wait_send()
            swap_copy(2, oseq.at[to], orows.at[to], to, to).wait_send()

    for copy in wide + swaps + ring.started:
        copy.wait_send()


def forward(*arrays):
    shape = jax.ShapeDtypeStruct
    dma = pltpu.SemaphoreType.DMA
    attn = shape((4, 2, 4, 4, 8, D), BF)
    wide = shape((4, 2, 4, 4, 8, HALF), BF)
    rows, heads = shape((ROWS, D), F32), shape((16, 128, 128), BF)
    mats = []
    for units, down in zip(UNITS, DOWN_ROWS):
        mats += [pltpu.VMEM((4, 2, 4, 4, 8, 64 * units), BF)] * 2 + [pltpu.VMEM((4, 4, 4, down, D), BF)]
    raw = shape((8, ROWS, 128), F32)
    both = shape((2 * ROWS, D), F32)
    return pl.pallas_call(
        forward_kernel,
        out_shape=(
            attn, attn, attn, wide, wide, *(shape((4, 4, 4, down, D), BF) for down in DOWN_ROWS),
            shape((ROWS, D), BF), raw, raw, heads, heads, heads, shape((2, SEQ), F32), shape((ROWS, D), BF), rows, both, both,
        ),
        in_specs=[vmem()] + [hbm()] + [vmem()] * 13,
        out_specs=[vmem()] * 3 + [hbm()] * 5 + [vmem()] * 11,
        scratch_shapes=mats + [pltpu.VMEM((8, ROWS, 128), BF)] * 2 + [pltpu.VMEM((16, 128, 128), BF)] + [pltpu.VMEM((2, ROWS, D), BF)] * 2
        + [pltpu.VMEM((D, 2 * ROWS), BF)] + [pltpu.VMEM((4, 2, 4, 4, 8, FF_BLOCK), BF)] * 2
        + [pltpu.VMEM((2, 4, 4, 16, D), BF), pltpu.VMEM((4, 4, 4, 8, D), BF)]
        + [pltpu.VMEM((8, D), BF)] * 2 + [pltpu.VMEM((2, 8, 64 * units), BF) for units in UNITS for _ in range(2)]
        + [dma((13,)), dma((11,)), dma((11,)), dma((12, 3, 4)), dma((12, 3, 4)), dma((3, 16)), dma((3, 16)), dma((3,)), dma((4,))],
        compiler_params=params(collective_id=0, has_side_effects=True),
    )(*arrays)


class Scatter:
    def __init__(self, at, grads, layouts, bufs, own, fins, send, recv, load):
        self.at, self.grads, self.layouts, self.bufs, self.own, self.fins = at, grads, layouts, bufs, own, fins
        self.send, self.recv, self.load = send, recv, load
        self.started = []

    def copy(self, i, stage, slot, src, dst, to):
        return pltpu.make_async_remote_copy(
            src_ref=src, dst_ref=dst, send_sem=self.send.at[i, stage, slot], recv_sem=self.recv.at[i, stage, slot],
            device_id=to, device_id_type=MESH)

    def start(self, *args):
        copy = self.copy(*args)
        copy.start()
        self.started.append(copy)

    def arrived(self, i, stage, slot, dst):
        self.copy(i, stage, slot, dst, dst, beside(self.at, "x", 1)).wait_recv()

    def lanes(self, i, half):
        width = self.layouts[i].columns // 2
        return pl.ds(half * width, width)

    def source(self, i, stage, by, half):
        lay = self.layouts[i]
        dim, full = lay.order[stage], lay.order[stage + 1 :]
        if stage == 0:
            return self.grads[i].at[lay.index(self.at, full, {dim: (self.at[dim] + by) % 4}, half)]
        kept = [d for d in "yzx" if d in lay.order[stage:]]
        index = [slice(None) if d != dim else (self.at[dim] + by) % 4 for d in kept]
        if lay.kind == "both":
            index.insert(1 if "y" in kept else 0, slice(None))
        return self.bufs[i][2 * stage - 1].at[(0, *index, slice(None), self.lanes(i, half))]

    def parts(self, i, stage):
        halves, near = self.bufs[i][2 * stage], self.bufs[i][2 * stage + 1]
        row = (slice(None),) * (len(near.shape) - 2)
        return halves, near, lambda side, half: near.at[(side, *row, self.lanes(i, half))]

    def in_vmem(self, i, stage):
        return stage > 0 or self.own[i] is None

    def loads(self, i, stage, second):
        steps = ((0, 0, 0), (1, 0, 1)) if second else ((0, 1, 0), (1, 3, 1))
        return [
            pltpu.make_async_copy(self.source(i, stage, by, half), self.own[i].at[k], self.load.at[i, k]) for k, by, half in steps
        ]

    def first(self, i, stage):
        dim = self.layouts[i].order[stage]
        halves, near, part = self.parts(i, stage)
        ahead, behind = beside(self.at, dim, 1), beside(self.at, dim, 3)
        self.start(i, stage, 0, self.source(i, stage, 2, 0), halves.at[0], ahead)
        self.start(i, stage, 1, self.source(i, stage, 2, 1), halves.at[1], behind)
        self.start(i, stage, 2, self.source(i, stage, 1, 1), part(0, 1), ahead)
        self.start(i, stage, 3, self.source(i, stage, 3, 0), part(1, 0), behind)
        if not self.in_vmem(i, stage):
            for copy in self.loads(i, stage, False):
                copy.start()

    def second(self, i, stage):
        dim = self.layouts[i].order[stage]
        halves, near, part = self.parts(i, stage)
        for side, by in ((0, 1), (1, 3)):
            self.arrived(i, stage, side, halves.at[side])
            if self.in_vmem(i, stage):
                mine = self.source(i, stage, by, side)
            else:
                self.loads(i, stage, False)[side].wait()
                mine = self.own[i].at[side]
            add_into(halves.at[side], halves.at[side], mine)
            self.start(i, stage, 4 + side, halves.at[side], part(side, side), beside(self.at, dim, by))
        if not self.in_vmem(i, stage):
            for copy in self.loads(i, stage, True):
                copy.start()

    def last(self, i, stage):
        halves, near, part = self.parts(i, stage)
        self.arrived(i, stage, 2, part(0, 1))
        self.arrived(i, stage, 3, part(1, 0))
        self.arrived(i, stage, 4, part(0, 0))
        self.arrived(i, stage, 5, part(1, 1))
        for half in range(2):
            if self.in_vmem(i, stage):
                mine = self.source(i, stage, 0, half)
            else:
                self.loads(i, stage, True)[half].wait()
                mine = self.own[i].at[half]
            target = part(0, half)
            if stage == 2:
                target = self.fins[i].at[(slice(None),) * (len(self.fins[i].shape) - 1) + (self.lanes(i, half),)]
            add_into(target, part(0, half), part(1, half), mine)


def add_into(target, *terms):
    def body(spot):
        total = terms[0][spot].astype(F32)
        for term in terms[1:]:
            total = total + term[spot].astype(F32)
        target[spot] = total.astype(target.dtype)

    lead = target.shape[:-2]
    count = 1
    for n in lead:
        count *= n
    if count == 1:
        body((0,) * len(lead))
        return

    @pl.loop(0, count)
    def _(flat):
        spot = []
        for n in reversed(lead):
            spot.insert(0, flat % n)
            flat = flat // n
        body(tuple(spot))


def stage_shapes(lay, rows):
    shapes = []
    for stage in range(3):
        left = lay.order[stage + 1 :]
        lead = ([4] if "y" in left else []) + ([2] if lay.kind == "both" else [])
        lead += [4] * (("z" in left) + ("x" in left))
        shapes.append((2, *lead, rows, lay.columns // 2))
        shapes.append((2, *lead, rows, lay.columns))
    return shapes


def norm_back(upstream, gain, unit, factor):
    scaled = upstream * gain
    return factor * (scaled - unit * jnp.mean(scaled * unit, axis=-1, keepdims=True))


GAIN_ROWS = 24


def segment_column(row):
    return jnp.transpose(jnp.broadcast_to(row.astype(F32), (128, row.shape[1])))[:, :1].astype(jnp.int32)


def backward_kernel(*refs):
    (x_ref, m_ref, gain_ref, qgain_ref, kgain_ref, fgain_ref, table_ref, segs_ref, x1_ref, out_hbm, back_hbm,
     full_ref, qseq, kvseq, oseq, inv_ref, h_ref, qraw_ref, kraw_ref, wo_hbm, wq_hbm, wkv_hbm, g_hbm, u_hbm, *d_hbm) = refs[:27]
    (y_ref, yin_ref, q_fin, k_out, v_out, o_fin, g_out, u_out, d_out, attn_gain_out, ffn_gain_out, q_gain_out, k_gain_out) = refs[27:40]
    (gq, gkv, go, out_own, back_own, out_other, back_other, do_own, do_seq, dq_own, dkv_own, dq_in, dkv_in, acc, dq_full, dkv_full,
     gains, gain_slots, wide_g, wide_u, first_mat, second_mat) = refs[40:62]
    cores = refs[62:65]
    own = [None, None, None, *refs[65:70]]
    bufs = [refs[70 + 6 * i : 76 + 6 * i] for i in range(8)]
    (core_send, core_recv, local_sem, send, recv, load_sem, swap_send, swap_recv, swap_local, gain_send, gain_recv) = refs[118:129]
    kv_fin, g_fin, u_fin, *d_fins, segcol_ref = refs[129:136]
    at = place()
    c = at["c"]
    dp, ctx = lax.axis_index("dp"), lax.axis_index("ctx")
    partner = device(at, c=1 - c)
    barrier = pltpu.get_barrier_semaphore()
    for to in (partner, beside(at, "y", 1), beside(at, "y", 3)):
        pl.semaphore_signal(barrier, inc=1, device_id=to, device_id_type=MESH)

    @pl.loop(1, 16)
    def _(step):
        pl.semaphore_signal(barrier, inc=1, device_id=(dp, (ctx + step) % 16), device_id_type=MESH)

    def core_copy(slot, src, dst):
        return pltpu.make_async_remote_copy(
            src_ref=src, dst_ref=dst, send_sem=core_send.at[slot], recv_sem=core_recv.at[slot], device_id=partner,
            device_id_type=MESH)

    rows_own, rows_other = pl.ds(0, ROWS), pl.ds(ROWS, ROWS)
    stays = [
        pltpu.make_async_copy(back_hbm.at[rows_own], back_own, local_sem.at[0]),
        pltpu.make_async_copy(out_hbm.at[rows_own], out_own, local_sem.at[1]),
        pltpu.make_async_copy(wo_hbm, first_mat, local_sem.at[2]),
        pltpu.make_async_copy(wkv_hbm, second_mat, local_sem.at[3]),
    ]
    for copy in stays:
        copy.start()
    pl.semaphore_wait(barrier, 18)
    swaps = [core_copy(0, back_hbm.at[rows_other], back_other), core_copy(1, out_hbm.at[rows_other], out_other)]
    for copy in swaps:
        copy.start()
    fins = [q_fin, kv_fin, o_fin, wide_g, wide_u, *d_fins]
    ring = Scatter(at, [gq, gkv, go, g_hbm, u_hbm, *d_hbm], scatter_layouts(), bufs, own, fins, send, recv, load_sem)
    attn, feed_mats = (0, 1, 2), (3, 4, 5, 6, 7)
    for i in feed_mats:
        ring.first(i, 0)

    for copy in stays:
        copy.wait()
    swaps[0].wait()
    residual = x1_ref[...]
    gain = fgain_ref[...]
    _, unit, factor = norm(residual, gain)
    upstream = back_own[...] + back_other[...]
    for k in range(8):
        gains[8 + k : 9 + k, :] = jnp.sum(upstream[:, k * 128 : (k + 1) * 128] * unit[:, k * 128 : (k + 1) * 128], axis=0, keepdims=True)
    dx1 = m_ref[...].astype(F32) + norm_back(upstream, gain, unit, factor)
    back_own[...] = dx1
    do = dot_cols(dx1.astype(BF), first_mat[...].reshape(D, D)).astype(BF)
    for s in range(2):
        for h in range(8):
            do_own[s * 8 + h] = do[s * 128 : (s + 1) * 128, h * 128 : (h + 1) * 128]
    query_mat = pltpu.make_async_copy(wq_hbm, first_mat, local_sem.at[4])
    query_mat.start()

    def swap_copy(k, src, dst, to, slot):
        return pltpu.make_async_remote_copy(
            src_ref=src, dst_ref=dst, send_sem=swap_send.at[k, to], recv_sem=swap_recv.at[k, slot], device_id=(dp, to),
            device_id_type=MESH)

    def swap_start(k, src, dst, to):
        @pl.when(to != ctx)
        def _():
            swap_copy(k, src.at[to], dst.at[ctx], to, ctx).start()

        @pl.when(to == ctx)
        def _():
            pltpu.make_async_copy(src.at[to], dst.at[ctx], swap_local.at[k]).start()

    def swap_wait(k, src, dst, source):
        @pl.when(source != ctx)
        def _():
            swap_copy(k, dst.at[source], dst.at[source], source, source).wait_recv()

        @pl.when(source == ctx)
        def _():
            pltpu.make_async_copy(src.at[ctx], dst.at[ctx], swap_local.at[k]).wait()

    @pl.loop(0, 16)
    def _(step):
        swap_start(0, do_own, do_seq, (ctx + step) % 16)

    acc[...] = jnp.zeros_like(acc)
    sequence = pl.ds(ctx // 8, 1)
    for k in range(SEQ // BLOCK):
        rows = slice(k * BLOCK, (k + 1) * BLOCK)
        segcol_ref[rows, :] = segment_column(segs_ref[sequence, rows])
    swaps[1].wait()
    y_ref[...] = (residual + out_own[...] + out_other[...]).astype(BF)

    def rows_gradient(grad, left, right):
        @pl.loop(0, 4)
        def _(y):
            cols = pl.ds(pl.multiple_of(y * 256, 256), 256)
            value = dot_rows(left[:, cols], right[...])
            grad[y] = value.reshape(2, 4, 4, 8, D).astype(BF)

    dq_full[...] = back_own[...].astype(BF)
    rows_gradient(go, full_ref, dq_full)
    swaps.append(core_copy(2, go.at[:, 1 - c], cores[2]))
    swaps[2].start()

    low_lane = lanes((BLOCK, 128)) < HDIM
    pick = (lax.broadcasted_iota(jnp.int32, (8, 128), 0) == lanes((8, 128)) // HDIM).astype(BF)

    def queries(block):
        swap_wait(0, do_own, do_seq, 2 * block)
        swap_wait(0, do_own, do_seq, 2 * block + 1)
        pair = pl.ds(2 * block, 2)
        rows = pl.ds(pl.multiple_of(block * BLOCK, BLOCK), BLOCK)
        q = qseq[pair].reshape(BLOCK, 128).astype(F32)
        do = do_seq[pair].reshape(BLOCK, 128).astype(F32)
        product = do * oseq[pair].reshape(BLOCK, 128).astype(F32)
        stacked = jnp.concatenate([jnp.where(low_lane, q, 0.0), jnp.where(low_lane, pltpu.roll(q, HDIM, 1), 0.0)], axis=0).astype(BF)
        above = jnp.concatenate([jnp.where(low_lane, 0.0, pltpu.roll(do, HDIM, 1)), jnp.where(low_lane, 0.0, do)], axis=0).astype(BF)
        high = product.astype(BF)
        rest = (product - high.astype(F32)).astype(BF)
        sums = dot_cols(pick, high) + dot_cols(pick, rest)
        row_dots = jnp.concatenate([sums[0:1], sums[1:2]], axis=1)
        inv = jnp.concatenate([inv_ref[0:1, rows], inv_ref[1:2, rows]], axis=1)
        seg_q = segs_ref[sequence, rows]
        seg_q = jnp.concatenate([seg_q, seg_q], axis=1)

        def part(j, total, diagonal):
            kv = kvseq[pl.ds(2 * j, 2)].reshape(BLOCK, 128)
            scores = dot_cols(kv, stacked)
            slopes = dot_cols(kv, above)
            allowed = segcol_ref[pl.ds(pl.multiple_of(j * BLOCK, BLOCK), BLOCK), :] == seg_q
            if diagonal:
                key = lax.broadcasted_iota(jnp.int32, (BLOCK, 2 * BLOCK), 0)
                allowed = allowed & (lanes((BLOCK, 2 * BLOCK)) % BLOCK >= key)
            weights = jnp.where(allowed, jnp.exp2(scores * SCALE2), 0.0) * inv
            change = (weights * (slopes - row_dots)).astype(BF)
            acc[j] = acc[j] + dot(change, stacked) * HDIM**-0.5 + dot(weights.astype(BF), above)
            return total + dot_rows(change, kv)

        total = jnp.zeros((2 * BLOCK, 128), F32)
        total = lax.fori_loop(0, block // 2, lambda j, t: part(2 * j + 1, part(2 * j, t, False), False), total)
        total = lax.fori_loop(block // 2 * 2, block, lambda j, t: part(j, t, False), total)
        total = part(block, total, True)
        both = jnp.where(low_lane, total[:BLOCK], pltpu.roll(total[BLOCK:], HDIM, 1)) * HDIM**-0.5
        dq_own[pair] = both.astype(BF).reshape(2, 128, 128)
        dkv_own[pair] = acc[block].astype(BF).reshape(2, 128, 128)
        for k in range(2):
            swap_start(1, dkv_own, dkv_in, 2 * block + k)
            swap_start(2, dq_own, dq_in, 2 * block + k)

    @pl.loop(0, 2)
    def _(step):
        queries(7 - step)

    for i in feed_mats:
        ring.second(i, 0)

    @pl.loop(2, 8)
    def _(step):
        queries(7 - step)

    for i in feed_mats:
        ring.last(i, 0)
        ring.first(i, 1)

    cosine, sine = rope_of(table_ref)
    qgain, kgain = twice(qgain_ref), twice(kgain_ref)
    head_sums = head_sum_matrix()
    wide_lane = lanes((ROWS, 128)) < HDIM

    def head_back(raw, upstream, gain):
        factor = lax.rsqrt(split_dot(raw * raw, head_sums) * (1.0 / HDIM) + EPSILON)
        unit = raw * factor
        turned = upstream * cosine - turn(upstream) * sine
        scaled = turned * gain
        mean = split_dot(scaled * unit, head_sums) * (1.0 / HDIM)
        return factor * (scaled - unit * mean), jnp.sum(turned * unit, axis=0, keepdims=True)

    @pl.loop(0, 16)
    def _(source):
        swap_wait(1, dkv_own, dkv_in, source)
        swap_wait(2, dq_own, dq_in, source)

    qterms = jnp.zeros((1, 128), F32)
    kterms = jnp.zeros((1, 128), F32)
    for h in range(8):
        cols = slice(h * 128, (h + 1) * 128)
        upstream = jnp.concatenate([dq_in[h], dq_in[8 + h]], axis=0).astype(F32)
        pre, terms = head_back(qraw_ref[h], upstream, qgain)
        qterms = qterms + terms
        dq_full[:, cols] = pre.astype(BF)
        upstream = jnp.concatenate([dkv_in[h], dkv_in[8 + h]], axis=0).astype(F32)
        pre, terms = head_back(kraw_ref[h], upstream, kgain)
        kterms = kterms + terms
        dkv_full[:, cols] = jnp.where(wide_lane, pre, upstream).astype(BF)
    gains[16:17, :] = qterms
    gains[17:18, :] = kterms
    gains[18:24, :] = jnp.zeros((6, 128), F32)
    rows_gradient(gq, h_ref, dq_full)
    swaps.append(core_copy(3, gq.at[:, 1 - c], cores[0]))
    swaps[3].start()
    rows_gradient(gkv, h_ref, dkv_full)
    swaps.append(core_copy(4, gkv.at[:, 1 - c], cores[1]))
    swaps[4].start()
    for slot, i in ((2, 2), (3, 0), (4, 1)):
        swaps[slot].wait_recv()
        mine = ring.grads[i].at[:, c]
        add_into(mine, mine, cores[i])
        ring.first(i, 0)

    query_mat.wait()
    dh = dot_cols(dq_full[...], first_mat[...].reshape(D, D)) + dot_cols(dkv_full[...], second_mat[...].reshape(D, D))
    gain = gain_ref[...]
    _, unit, factor = norm(x_ref[...].astype(F32), gain)
    for k in range(8):
        gains[k : k + 1, :] = jnp.sum(dh[:, k * 128 : (k + 1) * 128] * unit[:, k * 128 : (k + 1) * 128], axis=0, keepdims=True)
    yin_ref[...] = (back_own[...] + norm_back(dh, gain, unit, factor)).astype(BF)

    started = []

    def gain_copy(stage, slot, index, to):
        ref = gain_slots.at[stage, index]
        return pltpu.make_async_remote_copy(
            src_ref=ref, dst_ref=ref, send_sem=gain_send.at[stage, slot], recv_sem=gain_recv.at[stage, slot], device_id=to,
            device_id_type=MESH)

    def gain_start(stage, slot, index, to):
        copy = gain_copy(stage, slot, index, to)
        copy.start()
        started.append(copy)

    def gain_first(stage, total):
        dim = "xyz"[stage]
        p = at[dim]
        gain_slots[stage, p] = total
        gain_start(stage, 0, p, beside(at, dim, 1))
        gain_start(stage, 1, p, beside(at, dim, 3))

    def gain_second(stage):
        dim = "xyz"[stage]
        before = (at[dim] + 3) % 4
        gain_copy(stage, 0, before, partner).wait_recv()
        gain_start(stage, 2, before, beside(at, dim, 1))

    def gain_last(stage):
        dim = "xyz"[stage]
        gain_copy(stage, 1, (at[dim] + 1) % 4, partner).wait_recv()
        gain_copy(stage, 2, (at[dim] + 2) % 4, partner).wait_recv()
        return gain_slots[stage, 0] + gain_slots[stage, 1] + gain_slots[stage, 2] + gain_slots[stage, 3]

    gain_first(0, gains[...])
    for i in attn:
        ring.second(i, 0)
    gain_second(0)
    for i in feed_mats:
        ring.second(i, 1)
    for i in attn:
        ring.last(i, 0)
        ring.first(i, 1)
    gain_first(1, gain_last(0))
    for i in feed_mats:
        ring.last(i, 1)
        ring.first(i, 2)
    for i in attn:
        ring.second(i, 1)
    gain_second(1)
    for i in feed_mats:
        ring.second(i, 2)
    for i in attn:
        ring.last(i, 1)
        ring.first(i, 2)
    gain_first(2, gain_last(1))
    finals = []
    for i in feed_mats:
        ring.last(i, 2)
        if i < 5:
            wide, fin = ring.fins[i], (g_fin, u_fin)[i - 3]
            finals.append(core_copy(2 + i, wide.at[1 - c], fin.at[c]))
            finals[-1].start()
            fin[c] = wide[c]
    for i in attn:
        ring.second(i, 2)
    gain_second(2)
    for i in attn:
        ring.last(i, 2)
    gain_slots[3, c] = gain_last(2)
    finals.append(core_copy(7, gain_slots.at[3, c], gain_slots.at[3, c]))
    finals[-1].start()
    for slot, fin in ((5, g_fin), (6, u_fin)):
        core_copy(slot, fin.at[1 - c], fin.at[1 - c]).wait_recv()
    columns = []
    for y in range(4):
        for fin in (g_fin, u_fin):
            pieces = [fin[core, :, part * 1024 + y * 256 : part * 1024 + (y + 1) * 256] for part in range(2) for core in range(2)]
            where = slice(2048 + y // 2 * 128, 2048 + (y // 2 + 1) * 128)
            pieces.append((low_pair, high_pair)[y % 2](fin[0, :, where], fin[1, :, where]))
            columns.append(jnp.concatenate(pieces, axis=1))
    columns = jnp.concatenate(columns, axis=0)
    high = columns.astype(BF)
    rest = (columns - high.astype(F32)).astype(BF)
    sources = unit_sources()
    for k in range(9):
        matrix = spread_matrix(k, sources)
        units = dot_cols(high, matrix) + dot_cols(rest, matrix)
        for y in range(4):
            where = slice(y * 1152 + k * 128, y * 1152 + (k + 1) * 128)
            g_out[:, where] = units[16 * y : 16 * y + 8]
            u_out[:, where] = units[16 * y + 8 : 16 * y + 16]
    core_copy(7, gain_slots.at[3, 1 - c], gain_slots.at[3, 1 - c]).wait_recv()
    total = gain_slots[3, 0] + gain_slots[3, 1]
    attn_gain_out[...] = total[:8]
    ffn_gain_out[...] = total[8:16]
    q_gain_out[...] = (total[16:17] + pltpu.roll(total, HDIM, 1)[16:17])[:, :HDIM]
    k_gain_out[...] = total[17:18, :HDIM]
    low_half = lanes((8, 128)) < HDIM
    for k in range(4):
        even, odd = kv_fin[:, k * 256 : k * 256 + 128], kv_fin[:, k * 256 + 128 : (k + 1) * 256]
        k_out[:, k * 128 : (k + 1) * 128] = jnp.where(low_half, even, pltpu.roll(odd, HDIM, 1))
        v_out[:, k * 128 : (k + 1) * 128] = jnp.where(low_half, pltpu.roll(even, HDIM, 1), odd)
    d_out[0:16, :] = d_fins[0][...]
    d_out[16:32, :] = d_fins[1][...]
    d_out[32:36, :] = d_fins[2][0:4, :]

    @pl.loop(0, 16)
    def _(to):
        @pl.when(to != ctx)
        def _():
            swap_copy(0, do_own.at[to], do_seq.at[to], to, to).wait_send()
            swap_copy(1, dkv_own.at[to], dkv_in.at[to], to, to).wait_send()
            swap_copy(2, dq_own.at[to], dq_in.at[to], to, to).wait_send()

    for copy in swaps[2:] + finals + started + ring.started:
        copy.wait_send()


def backward(*arrays):
    shape = jax.ShapeDtypeStruct
    dma = pltpu.SemaphoreType.DMA
    small = shape((8, D), F32)
    block = pltpu.VMEM((16, 128, 128), BF)
    own = pltpu.VMEM((ROWS, D), F32)
    scratch = [pltpu.VMEM((4, 2, 4, 4, 8, D), BF)] * 3 + [own] * 4 + [block] * 6
    scratch += [pltpu.VMEM((SEQ // BLOCK, BLOCK, 128), F32)] + [pltpu.VMEM((ROWS, D), BF)] * 2
    scratch += [pltpu.VMEM((GAIN_ROWS, 128), F32), pltpu.VMEM((4, 4, GAIN_ROWS, 128), F32)] + [pltpu.VMEM((2, 8, HALF), F32)] * 2
    scratch += [pltpu.VMEM((4, 2, 4, 4, 8, D), BF)] * 2 + [pltpu.VMEM((4, 4, 4, 8, D), BF)] * 3
    shapes = [stage_shapes(lay, rows) for lay, rows in zip(scatter_layouts(), (8,) * 5 + DOWN_ROWS)]
    scratch += [pltpu.VMEM(shapes[i][0], BF) for i in range(3, 8)]
    for group in shapes:
        scratch += [pltpu.VMEM(s, BF) for s in group]
    scratch += [
        dma((8,)), dma((8,)), dma((5,)), dma((8, 3, 6)), dma((8, 3, 6)), dma((8, 2)), dma((3, 16)), dma((3, 16)), dma((3,)), dma((3, 3)),
        dma((3, 3)),
    ]
    scratch += [pltpu.VMEM((8, D), F32)] + [pltpu.VMEM((2, 8, HALF), F32)] * 2 + [pltpu.VMEM((rows, D), F32) for rows in DOWN_ROWS]
    scratch += [pltpu.VMEM((SEQ, 1), jnp.int32)]
    return pl.pallas_call(
        backward_kernel,
        out_shape=(
            shape((ROWS, D), BF), shape((ROWS, D), BF), small, shape((8, D // 2), F32), shape((8, D // 2), F32), small, shape((8, 4608), F32),
            shape((8, 4608), F32), shape((36, D), F32), shape((8, 128), F32), shape((8, 128), F32), shape((1, HDIM), F32),
            shape((1, HDIM), F32),
        ),
        in_specs=[vmem()] * 9 + [hbm()] * 2 + [vmem()] * 8 + [hbm()] * 8,
        out_specs=[vmem()] * 13,
        scratch_shapes=scratch,
        compiler_params=params(collective_id=1, has_side_effects=True),
    )(*arrays)


def results_kernel(*refs):
    count = len(refs) // 2
    for source, target in zip(refs[:count], refs[count:]):
        target[...] = source[...]


def results(arrays):
    return pl.pallas_call(
        results_kernel,
        out_shape=tuple(jax.ShapeDtypeStruct(a.shape, a.dtype) for a in arrays),
        in_specs=[vmem()] * len(arrays),
        out_specs=[vmem()] * len(arrays),
        compiler_params=params(),
    )(*arrays)


def rope_table(first_row):
    places = first_row + lax.broadcasted_iota(jnp.int32, (128, 128), 0)
    lane = lax.broadcasted_iota(jnp.int32, (128, 128), 1)
    frequency = THETA_BASE ** (-2.0 * (lane % (HDIM // 2)).astype(F32) / HDIM)
    angles = places.astype(F32) * frequency
    return jnp.where(lane < HDIM, jnp.cos(angles), jnp.sin(angles))


def local(block_in, segment_ids, attn_gain, w_query, w_key, w_value, query_gain, key_gain, w_out, ffn_gain, w_gate, w_up, w_down, out_grad):
    x = block_in.reshape(ROWS, D)
    m = out_grad.reshape(ROWS, D)
    row = lambda v: v.reshape(1, -1)
    gains = row(attn_gain), row(query_gain), row(key_gain), row(ffn_gain)
    table = rope_table(lax.axis_index("ctx") * 128)
    (wq, wkv, wo, gg, gu, gda, gdb, gdc, h1, qraw, kraw, q, kv, o, inv, attended, x1, out, back) = forward(
        x, m, *gains, table, segment_ids, w_query, w_key, w_value, w_out, w_gate, w_up, w_down)
    y, y_in, gq, gk, gv, gout, gg, gu, gd, attn_terms, ffn_terms, q_terms, k_terms = results(backward(
        x, m, *gains, table, segment_ids, x1, out, back, attended, q, kv, o, inv, h1, qraw, kraw, wo, wq, wkv, gg, gu, gda, gdb, gdc))
    return (
        y.reshape(2, 128, D), y_in.reshape(2, 128, D), gq, gk, gv, gout, gg, gu, gd, attn_terms.reshape(D), q_terms.reshape(HDIM),
        k_terms.reshape(HDIM), ffn_terms.reshape(D),
    )


def solution(mesh):
    both = P(("dp", "ctx"), None)
    acts = P("dp", "ctx", None)
    return jax.shard_map(
        local,
        mesh=mesh,
        in_specs=(acts, P("dp", None), P(), both, both, both, P(), P(), both, P(), both, both, both, acts),
        out_specs=(acts, acts, both, both, both, both, both, both, both, P(), P(), P(), P()),
        check_vma=False,
    )
```
